32 devices in a mesh: net: 8 (over z, x), scen: 4 (over y, core).
Axes of the slice: x: 2, y: 2, z: 4, core: 2. Of those that a mesh axis runs over, the one named last changes fastest.
Arguments:
- arc_flows: float32 [128, 65536], P('scen', 'net'), may hold values from 0 to 1
- node_duals: float32 [128, 16384], P('scen', 'net'), may hold values from -6 to 6
- demand: float32 [128, 16384], P('scen', 'net'), may hold values from -6 to 6
- excess: float32 [128], P('scen'), may hold values from 0 to 0.5
- risk_duals: float32 [128], P('scen'), may hold values from 0.2 to 6
- threshold: float32 [1], replicated, may hold values from -2.5 to -1.5
- arc_costs: float32 [65536], P('net'), may hold values from 0.05 to 0.75
- local_blocks: bfloat16 [512, 4, 128, 128], P('net'), may hold values from -0.125 to 0.125
- head_blocks: bfloat16 [512, 128, 128], P('net'), may hold values from -0.125 to 0.125
- local_index: int32 [512, 4], P('net'), may hold values from 0 to 15
- head_index: int32 [512], P('net'), may hold values from 0 to 127, as said below
Outputs:
- flows_next: float32 [128, 65536], P('scen', 'net')
- duals_next: float32 [128, 16384], P('scen', 'net')
- excess_next: float32 [128], P('scen')
- risk_next: float32 [128], P('scen')
- threshold_next: float32 [1], replicated
The draws below stay inside these ranges and needn't reach their ends.
Inputs may be any that keep to these rules, and one draw needn't show every extreme that they name: Among the arc blocks of one device, at most 16 have their head node block on any one device of net (head_index // 16 names the device), and in every device's arc blocks some device of net is named exactly 16 times.
All inputs are finite; a program needn't handle non-finite values.
Results may differ from the reference program's by a relative error of at most 0.0021.
Values may be sent and summed in bfloat16 or wider, within the bound.
No kernel may reach another device: no remote copies, remote signals or barrier semaphores. Data moves between devices by JAX's collectives and lax.ppermute only.
A program may use at most 128 MiB of HBM per device.

```python
import math
import jax
import jax.numpy as jnp

BLOCK_ROWS = 128
NODE_BLKS = 16
ARC_BLKS = 64
TOUCHES = 4
ROUNDS = 3
SCENARIOS = 128
ARC_BLOCKS = 512
NODE_BLOCKS = 128
ARC_COUNT = 65536
NODE_COUNT = 16384
SLOT_CAP = 16


def draw_head_index(key, part):
    devices = ARC_BLOCKS // ARC_BLKS
    slot_count = devices * SLOT_CAP

    def draw_device(device):
        folded = jax.random.fold_in(key, device)
        subkeys = jax.random.split(folded, 4)
        ordering = jax.random.permutation(subkeys[0], slot_count)
        favored = jax.random.randint(subkeys[1], (), 0, devices)
        places = jnp.arange(slot_count, dtype=jnp.int32)
        scores = jnp.where(ordering // SLOT_CAP == favored, places, places + slot_count)
        ranked = ordering[jnp.argsort(scores)]
        chosen = ranked[:ARC_BLKS]
        chosen = chosen[jax.random.permutation(subkeys[2], ARC_BLKS)]
        inside = jax.random.randint(subkeys[3], (ARC_BLKS,), 0, NODE_BLKS)
        return chosen // SLOT_CAP * NODE_BLKS + inside
    return jax.vmap(draw_device)(jnp.arange(devices)).reshape(-1).astype(jnp.int32)


def draw_arc_costs(key, part):
    rising = 1.0 + 2.0 * jnp.arange(ARC_COUNT).astype(jnp.float32) / ARC_COUNT
    uniform_draw = jax.random.uniform(key, (ARC_COUNT,), jnp.float32)
    levels = 0.05 * jnp.exp(uniform_draw * math.log(5.0))
    return (levels * rising).astype(jnp.float32)


def draw_risk_duals(key, part):
    rising = 1.0 + 2.0 * jnp.arange(SCENARIOS).astype(jnp.float32) / SCENARIOS
    uniform_draw = jax.random.uniform(key, (SCENARIOS,), jnp.float32)
    levels = 0.2 + 1.8 * uniform_draw
    return (levels * rising).astype(jnp.float32)


def place_ends(result, rng, low, high):
    spot = [jax.random.randint(jax.random.fold_in(rng, axis), (), 0, length) for axis, length in enumerate(result.shape)]
    main_axis = result.shape.index(max(result.shape))
    beside = spot[:main_axis] + [(spot[main_axis] + 1) % result.shape[main_axis]] + spot[main_axis + 1:]
    return result.at[tuple(spot)].set(low).at[tuple(beside)].set(high)


def shard_levels(own_key, extent, pieces, low, top_value):
    loudness, own = 1.0, jax.random.fold_in(own_key, 6)
    for position, parts in pieces:
        heights = jnp.exp(jax.random.uniform(jax.random.fold_in(own, position), (parts,), jnp.float32, low / len(pieces), top_value / len(pieces)))
        loudness = loudness * jnp.repeat(heights, extent[position] // parts).reshape([-1 if axis == position else 1 for axis in range(len(extent))])
    return loudness


def centred(own_key, extent, spread, reach, pieces=(), kind=jnp.bfloat16):
    level = shard_levels(own_key, extent, pieces, -0.22, 0.18) if pieces else 1.0
    drawn = jax.random.normal(own_key, extent, jnp.float32) * spread * level
    return jnp.minimum(jnp.maximum(drawn, -reach), reach).astype(kind)


def setup_inputs(seed: int = 0) -> dict:
    streams_of = jax.random.split(jax.random.key(seed), 12)
    arc_flows = jnp.clip(1.0 * jax.random.uniform(streams_of[0], (SCENARIOS, ARC_COUNT), jnp.float32) ** shard_levels(streams_of[0], (SCENARIOS, ARC_COUNT), ((0, 4), (1, 8)), -0.2, 0.2), 0.0, 1.0)
    node_duals = centred(streams_of[1], (SCENARIOS, NODE_COUNT), 1.0, 6.0, ((0, 4), (1, 8)), jnp.float32)
    demand = centred(streams_of[2], (SCENARIOS, NODE_COUNT), 1.0, 6.0, ((0, 4), (1, 8)), jnp.float32)
    excess = jnp.clip(0.5 * jax.random.uniform(streams_of[3], (SCENARIOS,), jnp.float32) ** shard_levels(streams_of[3], (SCENARIOS,), ((0, 4),), -0.2, 0.2), 0.0, 0.5)
    risk_duals = draw_risk_duals(jax.random.fold_in(streams_of[11], 71), 0)
    threshold = jnp.clip(jax.random.uniform(streams_of[5], (1,), jnp.float32, -2.5, -1.5), -2.5, -1.5)
    arc_costs = draw_arc_costs(jax.random.fold_in(streams_of[11], 71), 0)
    local_blocks = centred(streams_of[7], (ARC_BLOCKS, TOUCHES, BLOCK_ROWS, BLOCK_ROWS), (BLOCK_ROWS * 4 * (TOUCHES + 1)) ** -0.5, 0.125, ((0, 8),))
    head_blocks = centred(streams_of[8], (ARC_BLOCKS, BLOCK_ROWS, BLOCK_ROWS), (BLOCK_ROWS * 4 * (TOUCHES + 1)) ** -0.5, 0.125, ((0, 8),))
    local_index = place_ends(jax.random.randint(streams_of[9], (ARC_BLOCKS, TOUCHES), 0, NODE_BLKS), jax.random.fold_in(streams_of[9], 1), 0, NODE_BLKS - 1).astype(jnp.int32)
    head_index = draw_head_index(jax.random.fold_in(streams_of[11], 71), 0)
    return dict(arc_flows=arc_flows, node_duals=node_duals, demand=demand, excess=excess, risk_duals=risk_duals, threshold=threshold, arc_costs=arc_costs, local_blocks=local_blocks, head_blocks=head_blocks, local_index=local_index, head_index=head_index)


primal_step = 0.5
dual_step = 0.5
risk_step = 1.0
tail_weight = 2.0


def apply_forward(flow_panel, local_blocks, head_blocks, node_ids, head_index):
    scen_rows = flow_panel.shape[0]
    arc_panel = flow_panel.astype(jnp.float32).reshape(scen_rows, ARC_BLOCKS, BLOCK_ROWS)
    summed = jnp.zeros((scen_rows, NODE_BLOCKS, BLOCK_ROWS), jnp.float32)
    products = jnp.einsum("sjm,jmn->sjn", arc_panel, head_blocks.astype(jnp.float32))
    summed = summed.at[:, head_index, :].add(products)
    for touched in range(TOUCHES):
        products = jnp.einsum("sjm,jmn->sjn", arc_panel, local_blocks[:, touched].astype(jnp.float32))
        summed = summed.at[:, node_ids[:, touched], :].add(products)
    return summed.reshape(scen_rows, NODE_COUNT)


def apply_adjoint(dual_panel, local_blocks, head_blocks, node_ids, head_index):
    scen_rows = dual_panel.shape[0]
    node_panel = dual_panel.astype(jnp.float32).reshape(scen_rows, NODE_BLOCKS, BLOCK_ROWS)
    head_rows = node_panel[:, head_index, :]
    summed = jnp.einsum("sjn,jmn->sjm", head_rows, head_blocks.astype(jnp.float32))
    for touched in range(TOUCHES):
        local_rows = node_panel[:, node_ids[:, touched], :]
        summed = summed + jnp.einsum("sjn,jmn->sjm", local_rows, local_blocks[:, touched].astype(jnp.float32))
    return summed.reshape(scen_rows, ARC_COUNT)


def reference(arc_flows, node_duals, demand, excess, risk_duals, threshold, arc_costs, local_blocks, head_blocks, local_index, head_index):
    owners = (jnp.arange(ARC_BLOCKS, dtype=jnp.int32) // ARC_BLKS) * NODE_BLKS
    node_ids = (owners[:, None] + local_index).astype(jnp.int32)
    flows = arc_flows
    duals = node_duals
    excess_now = excess
    risk = risk_duals
    level = threshold
    for iteration in range(ROUNDS):
        dual_panel = duals.astype(jnp.bfloat16)
        pulled = apply_adjoint(dual_panel, local_blocks, head_blocks, node_ids, head_index)
        flows_new = jnp.maximum(flows - primal_step * (risk[:, None] * arc_costs[None, :] - pulled), 0.0)
        excess_new = jnp.maximum(excess_now - primal_step * (tail_weight - risk), 0.0)
        level_new = level - primal_step * (1.0 - jnp.mean(risk))
        flows_bar = 2.0 * flows_new - flows
        excess_bar = 2.0 * excess_new - excess_now
        level_bar = 2.0 * level_new - level
        losses = jnp.mean(arc_costs[None, :] * flows_bar, axis=1)
        risk = jnp.maximum(risk + risk_step * (losses - excess_bar - level_bar), 0.0)
        flow_panel = flows_bar.astype(jnp.bfloat16)
        duals = duals + dual_step * (demand - apply_forward(flow_panel, local_blocks, head_blocks, node_ids, head_index))
        flows = flows_new
        excess_now = excess_new
        level = level_new
    return (flows, duals, excess_now, risk, level)
```

```python
import functools

import jax
import jax.numpy as jnp
from jax import lax
from jax.experimental import pallas as pl
from jax.experimental.pallas import tpu as pltpu
from jax.sharding import PartitionSpec as P

ROUNDS = 3

primal_step = 0.5
dual_step = 0.5
risk_step = 1.0
tail_weight = 2.0

VMEM_LIMIT = 50 * 1024 * 1024
GROUP = 8


def contract_last(left, right):
    return lax.dot_general(
        left, right, (((1,), (1,)), ((), ())), preferred_element_type=jnp.float32
    )


def local_adjoint_kernel(touches, group, index_ref, panel_ref, blocks_ref, out_ref):
    rows = blocks_ref.shape[-1]
    first = pl.program_id(0) * group
    for member in range(group):
        total = None
        left = jnp.concatenate(
            [panel_ref[index_ref[(first + member) * touches + k]] for k in range(touches)], axis=1
        )
        right = jnp.concatenate([blocks_ref[member, k] for k in range(touches)], axis=1)
        out_ref[:, member * rows : (member + 1) * rows] = contract_last(left, right)


def head_kernel(
    group,
    steps,
    node_blks,
    has_losses,
    arc_total,
    index_ref,
    panel_ref,
    heads_ref,
    pulled_ref,
    flows_ref,
    costs_ref,
    risk_ref,
    flows_out,
    bar_out,
    terms_out,
    loss_out,
    risk_out,
    terms,
    loss,
):
    rows = heads_ref.shape[-1]
    step = pl.program_id(0)
    first = step * group
    chunk = node_blks + 1

    @pl.when(step == 0)
    def _():
        terms[...] = jnp.zeros_like(terms)
        loss[...] = jnp.zeros_like(loss)
        risk_start = risk_ref[...]
        if has_losses:
            arrived = jnp.zeros_like(risk_start)
            for source in range(panel_ref.shape[0] // chunk):
                arrived += panel_ref[source * chunk + node_blks].astype(jnp.float32)
            losses = jnp.sum(arrived, axis=1, keepdims=True) / arc_total
            risk_start = jnp.maximum(risk_start + risk_step * losses, 0.0)
        risk_out[...] = risk_start

    risk = risk_out[...]
    loss_sum = jnp.zeros_like(risk)
    for member in range(group):
        head = index_ref[first + member]
        place = head + lax.div(head, node_blks)
        columns = slice(member * rows, (member + 1) * rows)
        pulled = pulled_ref[:, columns] + contract_last(panel_ref[place], heads_ref[member])
        flows = flows_ref[:, columns]
        cost = costs_ref[:, columns]
        flows_new = jnp.maximum(flows - primal_step * (risk * cost - pulled), 0.0)
        bar = 2.0 * flows_new - flows
        flows_out[:, columns] = flows_new
        loss_sum += cost * bar
        half = bar.astype(jnp.bfloat16)
        bar_out[:, columns] = half
        terms[head] += jnp.dot(half, heads_ref[member], preferred_element_type=jnp.float32)
    loss[...] += loss_sum

    @pl.when(step == steps - 1)
    def _():
        terms_out[...] = terms[...].astype(jnp.bfloat16)
        total = jnp.sum(loss[...], axis=1, keepdims=True)
        high = total.astype(jnp.bfloat16).astype(jnp.float32)
        rest = total - high
        middle = rest.astype(jnp.bfloat16).astype(jnp.float32)
        low = rest - middle
        lane = lax.broadcasted_iota(jnp.int32, loss.shape, 1)
        packed = jnp.where(
            lane == 0, high, jnp.where(lane == 1, middle, jnp.where(lane == 2, low, 0.0))
        )
        loss_out[...] = packed.astype(jnp.bfloat16)


def local_forward_kernel(
    touches, group, steps, index_ref, bar_ref, blocks_ref, duals_ref, demand_ref, out_ref, total
):
    rows = blocks_ref.shape[-1]
    step = pl.program_id(0)
    first = step * group

    @pl.when(step == 0)
    def _():
        total[...] = jnp.zeros_like(total)

    for member in range(group):
        right = jnp.concatenate([blocks_ref[member, k] for k in range(touches)], axis=1)
        products = jnp.dot(
            bar_ref[:, member * rows : (member + 1) * rows],
            right,
            preferred_element_type=jnp.float32,
        )
        for k in range(touches):
            place = index_ref[(first + member) * touches + k]
            total[place] += products[:, k * rows : (k + 1) * rows]

    @pl.when(step == steps - 1)
    def _():
        out_ref[...] = duals_ref[...] + dual_step * (demand_ref[...] - total[...])


def whole(*shape):
    return pl.BlockSpec(shape, lambda i, *_: (0,) * len(shape))


def params():
    return pltpu.CompilerParams(
        dimension_semantics=("arbitrary",), vmem_limit_bytes=VMEM_LIMIT
    )


def local_adjoint(index, panel, blocks):
    arc_blks, touches, rows, _ = blocks.shape
    scen_rows = panel.shape[1]
    group = GROUP
    return pl.pallas_call(
        functools.partial(local_adjoint_kernel, touches, group),
        out_shape=jax.ShapeDtypeStruct((scen_rows, arc_blks * rows), jnp.float32),
        grid_spec=pltpu.PrefetchScalarGridSpec(
            num_scalar_prefetch=1,
            grid=(arc_blks // group,),
            in_specs=[
                whole(*panel.shape),
                pl.BlockSpec((group, touches, rows, rows), lambda i, *_: (i, 0, 0, 0)),
            ],
            out_specs=pl.BlockSpec((scen_rows, group * rows), lambda i, *_: (0, i)),
        ),
        compiler_params=params(),
        cost_estimate=pl.CostEstimate(
            flops=2 * scen_rows * blocks.size, bytes_accessed=2 * blocks.size, transcendentals=0
        ),
        name="local_adjoint",
    )(index, panel, blocks)


def head_step(index, panel, heads, pulled, flows, costs, risk, node_blks, has_losses, arc_total):
    arc_blks, rows, _ = heads.shape
    scen_rows = flows.shape[0]
    group = GROUP
    steps = arc_blks // group
    node_total = panel.shape[0] // (node_blks + 1) * node_blks
    arcs = pl.BlockSpec((scen_rows, group * rows), lambda i, *_: (0, i))
    return pl.pallas_call(
        functools.partial(head_kernel, group, steps, node_blks, has_losses, arc_total),
        out_shape=(
            jax.ShapeDtypeStruct(flows.shape, jnp.float32),
            jax.ShapeDtypeStruct(flows.shape, jnp.bfloat16),
            jax.ShapeDtypeStruct((node_total, scen_rows, rows), jnp.bfloat16),
            jax.ShapeDtypeStruct((scen_rows, rows), jnp.bfloat16),
            jax.ShapeDtypeStruct((scen_rows, rows), jnp.float32),
        ),
        grid_spec=pltpu.PrefetchScalarGridSpec(
            num_scalar_prefetch=1,
            grid=(steps,),
            in_specs=[
                whole(*panel.shape),
                pl.BlockSpec((group, rows, rows), lambda i, *_: (i, 0, 0)),
                arcs,
                arcs,
                pl.BlockSpec((1, group * rows), lambda i, *_: (0, i)),
                whole(scen_rows, rows),
            ],
            out_specs=[
                arcs,
                arcs,
                whole(node_total, scen_rows, rows),
                whole(scen_rows, rows),
                whole(scen_rows, rows),
            ],
            scratch_shapes=[
                pltpu.VMEM((node_total, scen_rows, rows), jnp.float32),
                pltpu.VMEM((scen_rows, rows), jnp.float32),
            ],
        ),
        compiler_params=params(),
        cost_estimate=pl.CostEstimate(
            flops=4 * scen_rows * heads.size,
            bytes_accessed=2 * heads.size + 14 * flows.size + 4 * panel.size,
            transcendentals=0,
        ),
        name="head_step",
    )(index, panel, heads, pulled, flows, costs, risk)


def local_forward(index, bar, blocks, duals, demand):
    arc_blks, touches, rows, _ = blocks.shape
    scen_rows = bar.shape[0]
    group = GROUP
    steps = arc_blks // group
    return pl.pallas_call(
        functools.partial(local_forward_kernel, touches, group, steps),
        out_shape=jax.ShapeDtypeStruct(duals.shape, jnp.float32),
        grid_spec=pltpu.PrefetchScalarGridSpec(
            num_scalar_prefetch=1,
            grid=(steps,),
            in_specs=[
                pl.BlockSpec((scen_rows, group * rows), lambda i, *_: (0, i)),
                pl.BlockSpec((group, touches, rows, rows), lambda i, *_: (i, 0, 0, 0)),
                whole(*duals.shape),
                whole(*duals.shape),
            ],
            out_specs=whole(*duals.shape),
            scratch_shapes=[pltpu.VMEM(duals.shape, jnp.float32)],
        ),
        compiler_params=params(),
        cost_estimate=pl.CostEstimate(
            flops=2 * scen_rows * blocks.size, bytes_accessed=2 * blocks.size, transcendentals=0
        ),
        name="local_forward",
    )(index, bar, blocks, duals, demand)


def sum_over(value, axis):
    size = lax.axis_size(axis)
    if size & (size - 1):
        return lax.psum(value, axis)
    stride = 1
    while stride < size:
        value = value + lax.ppermute(value, axis, [(i, i ^ stride) for i in range(size)])
        stride *= 2
    return value


def per_device(
    arc_flows,
    node_duals,
    demand,
    excess,
    risk_duals,
    threshold,
    arc_costs,
    local_blocks,
    head_blocks,
    local_index,
    head_index,
):
    rows = local_blocks.shape[-1]
    scen_rows = arc_flows.shape[0]
    node_blks = node_duals.shape[1] // rows
    net_size = lax.axis_size("net")
    arc_total = arc_flows.shape[1] * net_size
    scen_total = scen_rows * lax.axis_size("scen")
    local_ids = local_index.reshape(-1)
    costs = arc_costs.reshape(1, -1)

    def to_blocks(panel):
        return panel.reshape(scen_rows, node_blks, rows).transpose(1, 0, 2)

    duals = to_blocks(node_duals)
    wanted = to_blocks(demand)
    flows = arc_flows
    excess_now = jnp.broadcast_to(excess[:, None], (scen_rows, rows))
    risk = jnp.broadcast_to(risk_duals[:, None], (scen_rows, rows))
    level = threshold
    loss_half = jnp.zeros((scen_rows, rows), jnp.bfloat16)
    for iteration in range(ROUNDS):
        half = duals.astype(jnp.bfloat16)
        sent = jnp.concatenate([half, loss_half[None]], axis=0)
        panel = lax.all_gather(sent, "net", axis=0, tiled=True)
        pulled = local_adjoint(local_ids, half, local_blocks)
        flows, bar, terms, loss_half, risk = head_step(
            head_index,
            panel,
            head_blocks,
            pulled,
            flows,
            costs,
            risk,
            node_blks,
            iteration > 0,
            arc_total,
        )
        summed = lax.psum_scatter(terms, "net", scatter_dimension=0, tiled=True)
        base = local_forward(local_ids, bar, local_blocks, duals, wanted)
        mean_risk = sum_over(jnp.sum(risk[:, :1]).reshape(1), "scen") / scen_total
        level_new = level - primal_step * (1.0 - mean_risk)
        level_bar = 2.0 * level_new - level
        excess_new = jnp.maximum(excess_now - primal_step * (tail_weight - risk), 0.0)
        excess_bar = 2.0 * excess_new - excess_now
        risk = risk - risk_step * (excess_bar + level_bar)
        excess_now = excess_new
        level = level_new
        duals = base - dual_step * summed.astype(jnp.float32)
    last = lax.all_gather(loss_half, "net", axis=0, tiled=False).astype(jnp.float32)
    losses = jnp.sum(last, axis=(0, 2)) / arc_total
    risk_last = jnp.maximum(risk[:, 0] + risk_step * losses, 0.0)
    duals_last = duals.transpose(1, 0, 2).reshape(node_duals.shape)
    return (flows, duals_last, excess_now[:, 0], risk_last, level)


def solution(mesh):
    placed = (
        P("scen", "net"),
        P("scen", "net"),
        P("scen", "net"),
        P("scen"),
        P("scen"),
        P(),
        P("net"),
        P("net", None, None, None),
        P("net", None, None),
        P("net", None),
        P("net"),
    )
    return jax.shard_map(
        per_device,
        mesh=mesh,
        in_specs=placed,
        out_specs=(P("scen", "net"), P("scen", "net"), P("scen"), P("scen"), P()),
        check_vma=False,
    )
```

```python
import functools

import jax
import jax.numpy as jnp
from jax import lax
from jax.experimental import pallas as pl
from jax.experimental.pallas import tpu as pltpu
from jax.sharding import PartitionSpec as P

ROUNDS = 3

primal_step = 0.5
dual_step = 0.5
risk_step = 1.0
tail_weight = 2.0

MIB = 1024 * 1024
GROUP = 8
HEAD_GROUP = 16


def contract_last(left, right):
    return lax.dot_general(
        left, right, (((1,), (1,)), ((), ())), preferred_element_type=jnp.float32
    )


def local_adjoint_kernel(touches, group, index_ref, panel_ref, blocks_ref, out_ref):
    rows = blocks_ref.shape[-1]
    first = pl.program_id(0) * group
    for member in range(group):
        total = None
        left = jnp.concatenate(
            [panel_ref[index_ref[(first + member) * touches + k]] for k in range(touches)], axis=1
        )
        right = jnp.concatenate([blocks_ref[member, k] for k in range(touches)], axis=1)
        out_ref[:, member * rows : (member + 1) * rows] = contract_last(left, right)


def head_kernel(group, steps, peers, index_ref, *refs):
    panels, refs = refs[:peers], refs[peers:]
    heads_ref, pulled_ref, flows_ref, costs_ref, risk_ref = refs[:5]
    flows_out, bar_out, refs = refs[5], refs[6], refs[7:]
    sends, (panel, terms, pulled, loss) = refs[:peers], refs[peers:]
    rows = heads_ref.shape[-1]
    node_blks = panels[0].shape[0]
    step = pl.program_id(0)
    first = step * group

    @pl.when(step == 0)
    def _():
        terms[...] = jnp.zeros_like(terms)
        loss[...] = jnp.zeros_like(loss)
        for peer in range(peers):
            panel[peer * node_blks : (peer + 1) * node_blks] = panels[peer][...]

    places = [index_ref[first + member] for member in range(group)]
    spans = [slice(member * rows, (member + 1) * rows) for member in range(group)]
    for member in range(group):
        pulled[:, spans[member]] = contract_last(panel[places[member]], heads_ref[member])
    risk = risk_ref[...]
    loss_sum = jnp.zeros_like(risk)
    for columns in spans:
        flows = flows_ref[:, columns]
        cost = costs_ref[:, columns]
        gradient = risk * cost - (pulled[:, columns] + pulled_ref[:, columns])
        flows_new = jnp.maximum(flows - primal_step * gradient, 0.0)
        bar = 2.0 * flows_new - flows
        flows_out[:, columns] = flows_new
        loss_sum += cost * bar
        bar_out[:, columns] = bar.astype(jnp.bfloat16)
    loss[...] += loss_sum
    products = [
        jnp.dot(bar_out[:, spans[m]], heads_ref[m], preferred_element_type=jnp.float32)
        for m in range(group)
    ]
    for member in range(group):
        terms[places[member]] += products[member]

    @pl.when(step == steps - 1)
    def _():
        total = jnp.sum(loss[...], axis=1, keepdims=True)
        high = total.astype(jnp.bfloat16).astype(jnp.float32)
        rest = total - high
        middle = rest.astype(jnp.bfloat16).astype(jnp.float32)
        low = rest - middle
        lane = lax.broadcasted_iota(jnp.int32, loss.shape, 1)
        packed = jnp.where(
            lane == 0, high, jnp.where(lane == 1, middle, jnp.where(lane == 2, low, 0.0))
        ).astype(jnp.bfloat16)
        for peer in range(peers):
            sends[peer][:node_blks] = terms[peer * node_blks : (peer + 1) * node_blks].astype(
                jnp.bfloat16
            )
            sends[peer][node_blks] = packed


def pair_sum(values):
    while len(values) > 1:
        values = [a + b for a, b in zip(values[::2], values[1::2])]
    return values[0]


def settle_kernel(peers, arc_total, *refs):
    arrived, (base_ref, risk_ref, duals_out, half_out, risk_out) = refs[:peers], refs[peers:]
    node_blks = base_ref.shape[0]
    for block in range(node_blks):
        total = pair_sum([ref[block].astype(jnp.float32) for ref in arrived])
        duals = base_ref[block] - dual_step * total
        duals_out[block] = duals
        half_out[block] = duals.astype(jnp.bfloat16)
    parts = [
        jnp.sum(ref[node_blks].astype(jnp.float32), axis=1, keepdims=True) for ref in arrived
    ]
    losses = pair_sum(parts) / arc_total
    risk_out[...] = jnp.maximum(risk_ref[...] + risk_step * losses, 0.0)


def local_forward_kernel(
    touches, group, steps, index_ref, bar_ref, blocks_ref, duals_ref, demand_ref, out_ref, total
):
    rows = blocks_ref.shape[-1]
    step = pl.program_id(0)
    first = step * group

    @pl.when(step == 0)
    def _():
        total[...] = jnp.zeros_like(total)

    for member in range(group):
        right = jnp.concatenate([blocks_ref[member, k] for k in range(touches)], axis=1)
        products = jnp.dot(
            bar_ref[:, member * rows : (member + 1) * rows],
            right,
            preferred_element_type=jnp.float32,
        )
        for k in range(touches):
            place = index_ref[(first + member) * touches + k]
            total[place] += products[:, k * rows : (k + 1) * rows]

    @pl.when(step == steps - 1)
    def _():
        out_ref[...] = duals_ref[...] + dual_step * (demand_ref[...] - total[...])


def whole(*shape):
    return pl.BlockSpec(shape, lambda i, *_: (0,) * len(shape))


def vmem_limit(peers):
    return (8 + peers + peers // 4) * MIB


def params(peers=8):
    return pltpu.CompilerParams(
        dimension_semantics=("arbitrary",), vmem_limit_bytes=vmem_limit(peers)
    )


def local_adjoint(index, panel, blocks):
    arc_blks, touches, rows, _ = blocks.shape
    scen_rows = panel.shape[1]
    group = GROUP
    return pl.pallas_call(
        functools.partial(local_adjoint_kernel, touches, group),
        out_shape=jax.ShapeDtypeStruct((scen_rows, arc_blks * rows), jnp.float32),
        grid_spec=pltpu.PrefetchScalarGridSpec(
            num_scalar_prefetch=1,
            grid=(arc_blks // group,),
            in_specs=[
                whole(*panel.shape),
                pl.BlockSpec((group, touches, rows, rows), lambda i, *_: (i, 0, 0, 0)),
            ],
            out_specs=pl.BlockSpec((scen_rows, group * rows), lambda i, *_: (0, i)),
        ),
        compiler_params=params(),
        cost_estimate=pl.CostEstimate(
            flops=2 * scen_rows * blocks.size, bytes_accessed=2 * blocks.size, transcendentals=0
        ),
        name="local_adjoint",
    )(index, panel, blocks)


def head_step(places, panels, heads, pulled, flows, costs, risk):
    arc_blks, rows, _ = heads.shape
    scen_rows = flows.shape[0]
    peers = len(panels)
    node_blks = panels[0].shape[0]
    group = HEAD_GROUP
    steps = arc_blks // group
    sent = (node_blks + 1, scen_rows, rows)
    arcs = pl.BlockSpec((scen_rows, group * rows), lambda i, *_: (0, i))
    results = pl.pallas_call(
        functools.partial(head_kernel, group, steps, peers),
        out_shape=[
            jax.ShapeDtypeStruct(flows.shape, jnp.float32),
            jax.ShapeDtypeStruct(flows.shape, jnp.bfloat16),
        ]
        + [jax.ShapeDtypeStruct(sent, jnp.bfloat16)] * peers,
        grid_spec=pltpu.PrefetchScalarGridSpec(
            num_scalar_prefetch=1,
            grid=(steps,),
            in_specs=[whole(*panels[0].shape)] * peers
            + [
                pl.BlockSpec((group, rows, rows), lambda i, *_: (i, 0, 0)),
                arcs,
                arcs,
                pl.BlockSpec((1, group * rows), lambda i, *_: (0, i)),
                whole(scen_rows, rows),
            ],
            out_specs=[arcs, arcs] + [whole(*sent)] * peers,
            scratch_shapes=[
                pltpu.VMEM((peers * node_blks, scen_rows, rows), jnp.bfloat16),
                pltpu.VMEM((peers * node_blks, scen_rows, rows), jnp.float32),
                pltpu.VMEM((scen_rows, group * rows), jnp.float32),
                pltpu.VMEM((scen_rows, rows), jnp.float32),
            ],
        ),
        compiler_params=params(peers),
        cost_estimate=pl.CostEstimate(
            flops=4 * scen_rows * heads.size,
            bytes_accessed=2 * heads.size + 14 * flows.size + 4 * peers * panels[0].size,
            transcendentals=0,
        ),
        name="head_step",
    )(places, *panels, heads, pulled, flows, costs, risk)
    return results[0], results[1], results[2:]


def settle(arrived, base, risk, arc_total):
    peers = len(arrived)
    return pl.pallas_call(
        functools.partial(settle_kernel, peers, arc_total),
        out_shape=(
            jax.ShapeDtypeStruct(base.shape, jnp.float32),
            jax.ShapeDtypeStruct(base.shape, jnp.bfloat16),
            jax.ShapeDtypeStruct(risk.shape, jnp.float32),
        ),
        compiler_params=pltpu.CompilerParams(vmem_limit_bytes=vmem_limit(peers)),
        name="settle",
    )(*arrived, base, risk)


def local_forward(index, bar, blocks, duals, demand):
    arc_blks, touches, rows, _ = blocks.shape
    scen_rows = bar.shape[0]
    group = GROUP
    steps = arc_blks // group
    return pl.pallas_call(
        functools.partial(local_forward_kernel, touches, group, steps),
        out_shape=jax.ShapeDtypeStruct(duals.shape, jnp.float32),
        grid_spec=pltpu.PrefetchScalarGridSpec(
            num_scalar_prefetch=1,
            grid=(steps,),
            in_specs=[
                pl.BlockSpec((scen_rows, group * rows), lambda i, *_: (0, i)),
                pl.BlockSpec((group, touches, rows, rows), lambda i, *_: (i, 0, 0, 0)),
                whole(*duals.shape),
                whole(*duals.shape),
            ],
            out_specs=whole(*duals.shape),
            scratch_shapes=[pltpu.VMEM(duals.shape, jnp.float32)],
        ),
        compiler_params=params(),
        cost_estimate=pl.CostEstimate(
            flops=2 * scen_rows * blocks.size, bytes_accessed=2 * blocks.size, transcendentals=0
        ),
        name="local_forward",
    )(index, bar, blocks, duals, demand)


def swap(value, axis, distance):
    size = lax.axis_size(axis)
    return lax.ppermute(value, axis, [(i, i ^ distance) for i in range(size)])


def sum_over(value, axis):
    stride = 1
    while stride < lax.axis_size(axis):
        value = value + swap(value, axis, stride)
        stride *= 2
    return value


def gather_panels(own):
    size = lax.axis_size("net")
    panels = [own] + [None] * (size - 1)
    for distance in range(2, size, 2):
        panels[distance] = swap(own, "net", distance)
    for distance in range(0, size, 2):
        panels[distance + 1] = swap(panels[distance], "net", 1)
    return panels


def exchange(sends):
    return [sends[0]] + [swap(sends[k], "net", k) for k in range(1, len(sends))]


def per_device(
    arc_flows,
    node_duals,
    demand,
    excess,
    risk_duals,
    threshold,
    arc_costs,
    local_blocks,
    head_blocks,
    local_index,
    head_index,
):
    rows = local_blocks.shape[-1]
    scen_rows = arc_flows.shape[0]
    node_blks = node_duals.shape[1] // rows
    net_size = lax.axis_size("net")
    arc_total = arc_flows.shape[1] * net_size
    scen_total = scen_rows * lax.axis_size("scen")
    local_ids = local_index.reshape(-1)
    costs = arc_costs.reshape(1, -1)
    distance = jnp.bitwise_xor(head_index // node_blks, lax.axis_index("net"))
    places = distance * node_blks + head_index % node_blks

    def to_blocks(panel):
        return panel.reshape(scen_rows, node_blks, rows).transpose(1, 0, 2)

    duals = to_blocks(node_duals)
    half = duals.astype(jnp.bfloat16)
    wanted = to_blocks(demand)
    flows = arc_flows
    excess_now = jnp.broadcast_to(excess[:, None], (scen_rows, rows))
    risk = jnp.broadcast_to(risk_duals[:, None], (scen_rows, rows))
    level = threshold
    for iteration in range(ROUNDS):
        panels = gather_panels(half)
        pulled = local_adjoint(local_ids, half, local_blocks)
        mean_risk = sum_over(jnp.sum(risk[:, :1]).reshape(1), "scen") / scen_total
        level_new = level - primal_step * (1.0 - mean_risk)
        level_bar = 2.0 * level_new - level
        excess_new = jnp.maximum(excess_now - primal_step * (tail_weight - risk), 0.0)
        excess_bar = 2.0 * excess_new - excess_now
        flows, bar, sends = head_step(places, panels, head_blocks, pulled, flows, costs, risk)
        arrived = exchange(sends)
        base = local_forward(local_ids, bar, local_blocks, duals, wanted)
        shifted = risk - risk_step * (excess_bar + level_bar)
        duals, half, risk = settle(arrived, base, shifted, arc_total)
        excess_now = excess_new
        level = level_new
    duals_last = duals.transpose(1, 0, 2).reshape(node_duals.shape)
    return (flows, duals_last, excess_now[:, 0], risk[:, 0], level)


def solution(mesh):
    placed = (
        P("scen", "net"),
        P("scen", "net"),
        P("scen", "net"),
        P("scen"),
        P("scen"),
        P(),
        P("net"),
        P("net", None, None, None),
        P("net", None, None),
        P("net", None),
        P("net"),
    )
    return jax.shard_map(
        per_device,
        mesh=mesh,
        in_specs=placed,
        out_specs=(P("scen", "net"), P("scen", "net"), P("scen"), P("scen"), P()),
        check_vma=False,
    )
```

```python
import functools

import jax
import jax.numpy as jnp
from jax import lax
from jax.experimental import pallas as pl
from jax.experimental.pallas import tpu as pltpu
from jax.sharding import PartitionSpec as P

ROUNDS = 3

primal_step = 0.5
dual_step = 0.5
risk_step = 1.0
tail_weight = 2.0

MIB = 1024 * 1024
GROUP = 8
HEAD_GROUP = 16


def contract_last(left, right):
    return lax.dot_general(
        left, right, (((1,), (1,)), ((), ())), preferred_element_type=jnp.float32
    )


def local_adjoint_kernel(
    touches, group, index_ref, panel_ref, blocks_ref, sum_ref, *refs
):
    out_ref, sum_out = refs[-2:]
    rows = blocks_ref.shape[-1]
    first = pl.program_id(0) * group
    sum_out[...] = sum_ref[...]
    for member in range(group):
        left = jnp.concatenate(
            [panel_ref[index_ref[(first + member) * touches + k]] for k in range(touches)], axis=1
        )
        right = jnp.concatenate([blocks_ref[member, k] for k in range(touches)], axis=1)
        out_ref[:, member * rows : (member + 1) * rows] = contract_last(left, right)


def to_parts(column, shape):
    high = column.astype(jnp.bfloat16).astype(jnp.float32)
    rest = column - high
    middle = rest.astype(jnp.bfloat16).astype(jnp.float32)
    low = rest - middle
    lane = lax.broadcasted_iota(jnp.int32, shape, 1)
    packed = jnp.where(
        lane == 0, high, jnp.where(lane == 1, middle, jnp.where(lane == 2, low, 0.0))
    )
    return packed.astype(jnp.bfloat16)


def from_parts(parts):
    return jnp.sum(parts.astype(jnp.float32), axis=1, keepdims=True)


def head_kernel(group, steps, peers, index_ref, *refs):
    panels, refs = refs[:peers], refs[peers:]
    heads_ref, pulled_ref, flows_ref, costs_ref, risk_ref, sum_ref, other_ref = refs[:7]
    flows_out, bar_out, loss_out, sum_out, refs = *refs[7:11], refs[11:]
    kept, refs = refs[: peers // 2], refs[peers // 2 :]
    sends, (panel, terms, pulled, loss) = refs[:-4], refs[-4:]
    rows = heads_ref.shape[-1]
    node_blks = panels[0].shape[0]
    step = pl.program_id(0)
    first = step * group

    @pl.when(step == 0)
    def _():
        terms[...] = jnp.zeros_like(terms)
        loss[...] = jnp.zeros_like(loss)
        sum_out[...] = sum_ref[...] + other_ref[...]
        for peer in range(peers):
            panel[peer * node_blks : (peer + 1) * node_blks] = panels[peer][...]

    places = [index_ref[first + member] for member in range(group)]
    spans = [slice(member * rows, (member + 1) * rows) for member in range(group)]
    for member in range(group):
        pulled[:, spans[member]] = contract_last(panel[places[member]], heads_ref[member])
    risk = risk_ref[...]
    loss_sum = jnp.zeros_like(risk)
    for columns in spans:
        flows = flows_ref[:, columns]
        cost = costs_ref[:, columns]
        gradient = risk * cost - (pulled[:, columns] + pulled_ref[:, columns])
        flows_new = jnp.maximum(flows - primal_step * gradient, 0.0)
        bar = 2.0 * flows_new - flows
        flows_out[:, columns] = flows_new
        loss_sum += cost * bar
        bar_out[:, columns] = bar.astype(jnp.bfloat16)
    loss[...] += loss_sum
    products = [
        jnp.dot(bar_out[:, spans[m]], heads_ref[m], preferred_element_type=jnp.float32)
        for m in range(group)
    ]
    for member in range(group):
        terms[places[member]] += products[member]

    @pl.when(step == steps - 1)
    def _():
        loss_parts = to_parts(jnp.sum(loss[...], axis=1, keepdims=True), loss.shape)
        loss_out[...] = loss_parts
        for half in range(peers // 2):
            begin = 2 * half * node_blks
            kept[half][...] = terms[begin : begin + node_blks]
        for send, distances in zip(sends, near_pieces(peers)):
            for place, distance in enumerate(distances):
                send[place * node_blks : (place + 1) * node_blks] = terms[
                    distance * node_blks : (distance + 1) * node_blks
                ].astype(jnp.bfloat16)
        sends[0][2 * node_blks] = loss_parts


def near_pieces(peers):
    return [(k, k - 2) for k in range(peers - 1, 2, -4)]


def pair_sum(values):
    while len(values) > 1:
        values = [a + b for a, b in zip(values[::2], values[1::2])]
    return values[0]


def fold_kernel(count, first, last, *refs):
    kept, (arrived_ref, loss_ref, extra_ref), refs = refs[:count], refs[count : count + 3], refs[count + 3 :]
    outs, refs = refs[:count], refs[count:]
    node_blks = kept[0].shape[0]
    for place in range(count):
        for block in range(node_blks):
            term = arrived_ref[place * node_blks + block].astype(jnp.float32)
            outs[place][block] = (kept[place][block] + term).astype(jnp.bfloat16)
    parts = loss_ref[...]
    if first:
        both = from_parts(parts) + from_parts(arrived_ref[2 * node_blks])
        parts = to_parts(both, loss_ref.shape)
        refs[0][...] = parts
    for out in outs:
        out[node_blks] = parts
    if not last:
        refs[-1][...] = extra_ref[...]


def settle_kernel(peers, arc_total, scen_total, last, *refs):
    kept_ref, near_ref, refs = refs[0], refs[1], refs[2:]
    arrived, refs = refs[: peers // 2 - 1], refs[peers // 2 - 1 :]
    pair_ref, base_ref, risk_ref, excess_ref, level_ref, sum_ref, other_ref = refs[:7]
    duals_out, half_out, risk_out, excess_out, level_out, sum_out = refs[7:]
    node_blks, _, rows = base_ref.shape
    for block in range(node_blks):
        parts = [near_ref[node_blks + block]] + [ref[block] for ref in arrived]
        total = kept_ref[block] + pair_sum([part.astype(jnp.float32) for part in parts])
        duals = base_ref[block] - dual_step * total
        if last:
            duals_out[:, block * rows : (block + 1) * rows] = duals
        else:
            duals_out[block] = duals
        half_out[block] = duals.astype(jnp.bfloat16)
    losses = [from_parts(pair_ref[...])] + [from_parts(ref[node_blks]) for ref in arrived]
    losses = pair_sum(losses) / arc_total
    mean_risk = (sum_ref[...] + other_ref[...]) / scen_total
    level = level_ref[...]
    level_new = level - primal_step * (1.0 - mean_risk)
    level_bar = 2.0 * level_new - level
    level_out[...] = level_new
    risk = risk_ref[...]
    excess = excess_ref[...]
    excess_new = jnp.maximum(excess - primal_step * (tail_weight - risk), 0.0)
    excess_bar = 2.0 * excess_new - excess
    excess_out[...] = excess_new
    risk_new = jnp.maximum(risk + risk_step * (losses - excess_bar - level_bar[:1]), 0.0)
    risk_out[...] = risk_new
    sum_out[...] = jnp.broadcast_to(jnp.sum(risk_new, axis=0, keepdims=True), sum_out.shape)


def local_forward_kernel(
    touches,
    group,
    steps,
    index_ref,
    bar_ref,
    blocks_ref,
    duals_ref,
    demand_ref,
    sum_ref,
    after_ref,
    out_ref,
    sum_out,
    total,
):
    rows = blocks_ref.shape[-1]
    step = pl.program_id(0)
    first = step * group

    @pl.when(step == 0)
    def _():
        total[...] = jnp.zeros_like(total)
        sum_out[...] = sum_ref[...]

    for member in range(group):
        right = jnp.concatenate([blocks_ref[member, k] for k in range(touches)], axis=1)
        products = jnp.dot(
            bar_ref[:, member * rows : (member + 1) * rows],
            right,
            preferred_element_type=jnp.float32,
        )
        for k in range(touches):
            place = index_ref[(first + member) * touches + k]
            total[place] += products[:, k * rows : (k + 1) * rows]

    @pl.when(step == steps - 1)
    def _():
        out_ref[...] = duals_ref[...] + dual_step * (demand_ref[...] - total[...])


def whole(*shape):
    return pl.BlockSpec(shape, lambda i, *_: (0,) * len(shape))


def vmem_limit(peers):
    return (8 + peers + peers // 4) * MIB


def params(peers=8):
    return pltpu.CompilerParams(
        dimension_semantics=("arbitrary",), vmem_limit_bytes=vmem_limit(peers)
    )


def local_adjoint(index, panel, blocks, risk_sum, after):
    arc_blks, touches, rows, _ = blocks.shape
    scen_rows = panel.shape[1]
    group = GROUP
    return pl.pallas_call(
        functools.partial(local_adjoint_kernel, touches, group),
        out_shape=(
            jax.ShapeDtypeStruct((scen_rows, arc_blks * rows), jnp.float32),
            jax.ShapeDtypeStruct(risk_sum.shape, jnp.float32),
        ),
        grid_spec=pltpu.PrefetchScalarGridSpec(
            num_scalar_prefetch=1,
            grid=(arc_blks // group,),
            in_specs=[
                whole(*panel.shape),
                pl.BlockSpec((group, touches, rows, rows), lambda i, *_: (i, 0, 0, 0)),
                whole(*risk_sum.shape),
            ]
            + [pl.BlockSpec(memory_space=pl.ANY)] * len(after),
            out_specs=[
                pl.BlockSpec((scen_rows, group * rows), lambda i, *_: (0, i)),
                whole(*risk_sum.shape),
            ],
        ),
        compiler_params=params(),
        cost_estimate=pl.CostEstimate(
            flops=2 * scen_rows * blocks.size, bytes_accessed=2 * blocks.size, transcendentals=0
        ),
        name="local_adjoint",
    )(index, panel, blocks, risk_sum, *after)


def head_step(places, panels, heads, pulled, flows, costs, risk, sums):
    arc_blks, rows, _ = heads.shape
    scen_rows = flows.shape[0]
    peers = len(panels)
    node_blks = panels[0].shape[0]
    group = HEAD_GROUP
    steps = arc_blks // group
    kept = (node_blks, scen_rows, rows)
    pieces = near_pieces(peers)
    sent = [(len(piece) * node_blks, scen_rows, rows) for piece in pieces]
    sent[0] = (2 * node_blks + 1, scen_rows, rows)
    arcs = pl.BlockSpec((scen_rows, group * rows), lambda i, *_: (0, i))
    results = pl.pallas_call(
        functools.partial(head_kernel, group, steps, peers),
        out_shape=[
            jax.ShapeDtypeStruct(flows.shape, jnp.float32),
            jax.ShapeDtypeStruct(flows.shape, jnp.bfloat16),
            jax.ShapeDtypeStruct((scen_rows, rows), jnp.bfloat16),
            jax.ShapeDtypeStruct(sums[0].shape, jnp.float32),
        ]
        + [jax.ShapeDtypeStruct(kept, jnp.float32)] * (peers // 2)
        + [jax.ShapeDtypeStruct(shape, jnp.bfloat16) for shape in sent],
        grid_spec=pltpu.PrefetchScalarGridSpec(
            num_scalar_prefetch=1,
            grid=(steps,),
            in_specs=[whole(*panels[0].shape)] * peers
            + [
                pl.BlockSpec((group, rows, rows), lambda i, *_: (i, 0, 0)),
                arcs,
                arcs,
                pl.BlockSpec((1, group * rows), lambda i, *_: (0, i)),
                whole(scen_rows, rows),
                whole(*sums[0].shape),
                whole(*sums[0].shape),
            ],
            out_specs=[arcs, arcs, whole(scen_rows, rows), whole(*sums[0].shape)]
            + [whole(*kept)] * (peers // 2)
            + [whole(*shape) for shape in sent],
            scratch_shapes=[
                pltpu.VMEM((peers * node_blks, scen_rows, rows), jnp.bfloat16),
                pltpu.VMEM((peers * node_blks, scen_rows, rows), jnp.float32),
                pltpu.VMEM((scen_rows, group * rows), jnp.float32),
                pltpu.VMEM((scen_rows, rows), jnp.float32),
            ],
        ),
        compiler_params=params(peers),
        cost_estimate=pl.CostEstimate(
            flops=4 * scen_rows * heads.size,
            bytes_accessed=2 * heads.size + 14 * flows.size + 4 * peers * panels[0].size,
            transcendentals=0,
        ),
        name="head_step",
    )(places, *panels, heads, pulled, flows, costs, risk, *sums)
    half = peers // 2
    return *results[:4], results[4 : 4 + half], results[4 + half :]


def small_cost(*arrays):
    size = sum(a.size for a in arrays)
    return pl.CostEstimate(flops=size, bytes_accessed=2 * size, transcendentals=0)


def fold(kept, arrived, loss, extra, first, last):
    count = len(kept)
    node_blks, scen_rows, rows = kept[0].shape
    out_shape = [jax.ShapeDtypeStruct((node_blks + 1, scen_rows, rows), jnp.bfloat16)] * count
    if first:
        out_shape.append(jax.ShapeDtypeStruct(loss.shape, jnp.bfloat16))
    if not last:
        out_shape.append(jax.ShapeDtypeStruct(extra.shape, jnp.bfloat16))
    vmem = pl.BlockSpec(memory_space=pltpu.VMEM)
    results = pl.pallas_call(
        functools.partial(fold_kernel, count, first, last),
        out_shape=out_shape,
        in_specs=[vmem] * (count + 2) + [pl.BlockSpec(memory_space=pl.ANY) if last else vmem],
        out_specs=[vmem] * len(out_shape),
        compiler_params=pltpu.CompilerParams(vmem_limit_bytes=vmem_limit(8)),
        cost_estimate=small_cost(*kept, arrived),
        name="fold",
    )(*kept, arrived, loss, extra)
    return results[:count], results[count:]


def settle(kept, near, arrived, pair, base, risk, excess, level, sums, arc_total, scen_total, last):
    peers = 2 * (len(arrived) + 1)
    node_blks, scen_rows, rows = base.shape
    duals = (scen_rows, node_blks * rows) if last else base.shape
    return pl.pallas_call(
        functools.partial(settle_kernel, peers, arc_total, scen_total, last),
        out_shape=(
            jax.ShapeDtypeStruct(duals, jnp.float32),
            jax.ShapeDtypeStruct(base.shape, jnp.bfloat16),
            jax.ShapeDtypeStruct(risk.shape, jnp.float32),
            jax.ShapeDtypeStruct(risk.shape, jnp.float32),
            jax.ShapeDtypeStruct(level.shape, jnp.float32),
            jax.ShapeDtypeStruct(level.shape, jnp.float32),
        ),
        compiler_params=pltpu.CompilerParams(vmem_limit_bytes=vmem_limit(peers)),
        cost_estimate=small_cost(kept, near, *arrived, base),
        name="settle",
    )(kept, near, *arrived, pair, base, risk, excess, level, *sums)


def local_forward(index, bar, blocks, duals, demand, risk_sum, after):
    arc_blks, touches, rows, _ = blocks.shape
    scen_rows = bar.shape[0]
    group = GROUP
    steps = arc_blks // group
    return pl.pallas_call(
        functools.partial(local_forward_kernel, touches, group, steps),
        out_shape=(
            jax.ShapeDtypeStruct(duals.shape, jnp.float32),
            jax.ShapeDtypeStruct(risk_sum.shape, jnp.float32),
        ),
        grid_spec=pltpu.PrefetchScalarGridSpec(
            num_scalar_prefetch=1,
            grid=(steps,),
            in_specs=[
                pl.BlockSpec((scen_rows, group * rows), lambda i, *_: (0, i)),
                pl.BlockSpec((group, touches, rows, rows), lambda i, *_: (i, 0, 0, 0)),
                whole(*duals.shape),
                whole(*duals.shape),
                whole(*risk_sum.shape),
                pl.BlockSpec(memory_space=pl.ANY),
            ],
            out_specs=[whole(*duals.shape), whole(*risk_sum.shape)],
            scratch_shapes=[pltpu.VMEM(duals.shape, jnp.float32)],
        ),
        compiler_params=params(),
        cost_estimate=pl.CostEstimate(
            flops=2 * scen_rows * blocks.size, bytes_accessed=2 * blocks.size, transcendentals=0
        ),
        name="local_forward",
    )(index, bar, blocks, duals, demand, risk_sum, after)


def swap(value, axis, distance):
    size = lax.axis_size(axis)
    return lax.ppermute(value, axis, [(i, i ^ distance) for i in range(size)])


def gather_panels(own):
    size = lax.axis_size("net")
    panels = [own] + [None] * (size - 1)
    for distance in range(2, size, 2):
        panels[distance] = swap(own, "net", distance)
    for distance in range(0, size, 2):
        panels[distance + 1] = swap(panels[distance], "net", 1)
    return panels


def per_device(
    arc_flows,
    node_duals,
    demand,
    excess,
    risk_duals,
    threshold,
    arc_costs,
    local_blocks,
    head_blocks,
    local_index,
    head_index,
):
    rows = local_blocks.shape[-1]
    scen_rows = arc_flows.shape[0]
    node_blks = node_duals.shape[1] // rows
    net_size = lax.axis_size("net")
    arc_total = arc_flows.shape[1] * net_size
    scen_total = scen_rows * lax.axis_size("scen")
    local_ids = local_index.reshape(-1)
    costs = arc_costs.reshape(1, -1)
    distance = jnp.bitwise_xor(head_index // node_blks, lax.axis_index("net"))
    places = distance * node_blks + head_index % node_blks
    scen_size = lax.axis_size("scen")
    wide = (scen_rows, rows)
    flat = (8, rows)

    def to_blocks(panel):
        return panel.reshape(scen_rows, node_blks, rows).transpose(1, 0, 2)

    duals = to_blocks(node_duals)
    half = duals.astype(jnp.bfloat16)
    wanted = to_blocks(demand)
    flows = arc_flows
    excess_now = jnp.broadcast_to(excess[:, None], wide)
    risk = jnp.broadcast_to(risk_duals[:, None], wide)
    level = jnp.broadcast_to(threshold[:, None], flat)
    risk_sum = jnp.broadcast_to(jnp.sum(risk_duals), flat)
    for iteration in range(ROUNDS):
        panels = gather_panels(half)
        pulled, risk_sum = local_adjoint(
            local_ids, half, local_blocks, risk_sum, panels[2::2] if iteration else panels[5:6]
        )
        sums = (risk_sum, swap(risk_sum, "scen", 1))
        flows, bar, loss, risk_sum, kept, sends = head_step(
            places, panels, head_blocks, pulled, flows, costs, risk, sums
        )
        halves = len(kept)
        folded = [None] * halves
        pair, piece = loss, sends[0]
        for number in range(len(sends) - 1):
            half = halves - 1 - 2 * number
            (folded[half], folded[half - 1]), rest = fold(
                (kept[half], kept[half - 1]),
                swap(piece, "net", 1),
                pair,
                sends[number + 1],
                number == 0,
                False,
            )
            pair = rest[0] if number == 0 else pair
            piece = rest[-1]
        base, risk_sum = local_forward(
            local_ids, bar, local_blocks, duals, wanted, risk_sum, folded[2]
        )
        near = swap(piece, "net", 1)
        (folded[1],), _ = fold((kept[1],), near, pair, base, False, True)
        far = [swap(folded[half], "net", 2 * half) for half in range(1, halves)]
        stride = 2
        while 2 * stride < scen_size:
            risk_sum = risk_sum + swap(risk_sum, "scen", stride)
            stride *= 2
        sums = (risk_sum, swap(risk_sum, "scen", stride))
        duals, half, risk, excess_now, level, risk_sum = settle(
            kept[0],
            near,
            far,
            pair,
            base,
            risk,
            excess_now,
            level,
            sums,
            arc_total,
            scen_total,
            iteration == ROUNDS - 1,
        )
    return (flows, duals, excess_now[:, 0], risk[:, 0], level[0, :1])


def solution(mesh):
    placed = (
        P("scen", "net"),
        P("scen", "net"),
        P("scen", "net"),
        P("scen"),
        P("scen"),
        P(),
        P("net"),
        P("net", None, None, None),
        P("net", None, None),
        P("net", None),
        P("net"),
    )
    return jax.shard_map(
        per_device,
        mesh=mesh,
        in_specs=placed,
        out_specs=(P("scen", "net"), P("scen", "net"), P("scen"), P("scen"), P()),
        check_vma=False,
    )
```

```python
import functools

import jax
import jax.numpy as jnp
from jax import lax
from jax.experimental import pallas as pl
from jax.experimental.pallas import tpu as pltpu
from jax.sharding import PartitionSpec as P

ROUNDS = 3

primal_step = 0.5
dual_step = 0.5
risk_step = 1.0
tail_weight = 2.0

MIB = 1024 * 1024
GROUP = 8
HEAD_GROUP = 16


def contract_last(left, right):
    return lax.dot_general(
        left, right, (((1,), (1,)), ((), ())), preferred_element_type=jnp.float32
    )


def local_adjoint_kernel(
    touches, group, index_ref, panel_ref, blocks_ref, *refs
):
    out_ref = refs[-1]
    rows = blocks_ref.shape[-1]
    first = pl.program_id(0) * group
    for member in range(group):
        left = jnp.concatenate(
            [panel_ref[index_ref[first + member, k]] for k in range(touches)], axis=1
        )
        right = jnp.concatenate([blocks_ref[member, k] for k in range(touches)], axis=1)
        out_ref[:, member * rows : (member + 1) * rows] = contract_last(left, right)


def to_parts(column, shape):
    high = column.astype(jnp.bfloat16).astype(jnp.float32)
    rest = column - high
    middle = rest.astype(jnp.bfloat16).astype(jnp.float32)
    low = rest - middle
    lane = lax.broadcasted_iota(jnp.int32, shape, 1)
    packed = jnp.where(
        lane == 0, high, jnp.where(lane == 1, middle, jnp.where(lane == 2, low, 0.0))
    )
    return packed.astype(jnp.bfloat16)


def from_parts(parts):
    return jnp.sum(parts.astype(jnp.float32), axis=1, keepdims=True)


def head_kernel(group, steps, peers, index_ref, *refs):
    panels, refs = refs[:peers], refs[peers:]
    heads_ref, pulled_ref, flows_ref, costs_ref, risk_ref, sum_ref, other_ref = refs[:7]
    flows_out, bar_out, sum_out, refs = *refs[7:10], refs[10:]
    kept, refs = refs[: peers // 2], refs[peers // 2 :]
    sends, (panel, terms, pulled, loss) = refs[:-4], refs[-4:]
    rows = heads_ref.shape[-1]
    node_blks = panels[0].shape[0]
    step = pl.program_id(0)
    first = step * group

    @pl.when(step == 0)
    def _():
        terms[...] = jnp.zeros_like(terms)
        loss[...] = jnp.zeros_like(loss)
        sum_out[...] = sum_ref[...] + other_ref[...]
        for peer in range(peers):
            panel[peer * node_blks : (peer + 1) * node_blks] = panels[peer][...]

    places = [index_ref[first + member] for member in range(group)]
    spans = [slice(member * rows, (member + 1) * rows) for member in range(group)]
    for member in range(group):
        pulled[:, spans[member]] = contract_last(panel[places[member]], heads_ref[member])
    risk = risk_ref[...]
    loss_sum = jnp.zeros_like(risk)
    for columns in spans:
        flows = flows_ref[:, columns]
        cost = costs_ref[:, columns]
        gradient = risk * cost - (pulled[:, columns] + pulled_ref[:, columns])
        flows_new = jnp.maximum(flows - primal_step * gradient, 0.0)
        bar = 2.0 * flows_new - flows
        flows_out[:, columns] = flows_new
        loss_sum += cost * bar
        bar_out[:, columns] = bar.astype(jnp.bfloat16)
    loss[...] += loss_sum
    products = [
        jnp.dot(bar_out[:, spans[m]], heads_ref[m], preferred_element_type=jnp.float32)
        for m in range(group)
    ]
    for member in range(group):
        terms[places[member]] += products[member]

    @pl.when(step == steps - 1)
    def _():
        loss_parts = to_parts(jnp.sum(loss[...], axis=1, keepdims=True), loss.shape)
        for out, distance in zip(kept, inner(peers)):
            out[...] = terms[distance * node_blks : (distance + 1) * node_blks]
        for out, distance in zip(sends, leaves(peers)):
            out[:node_blks] = terms[distance * node_blks : (distance + 1) * node_blks].astype(
                jnp.bfloat16
            )
        sends[-1][node_blks] = loss_parts


def last_hop(distance):
    return 2 if distance == 3 else distance & -distance


def children(distance, peers):
    return [k for k in range(1, peers) if k ^ last_hop(k) == distance]


def inner(peers):
    return [k for k in range(peers) if children(k, peers)]


def leaves(peers):
    return [k for k in range(peers) if not children(k, peers)]


def pair_sum(values):
    while len(values) > 1:
        values = [a + b for a, b in zip(values[::2], values[1::2])] + values[len(values) // 2 * 2 :]
    return values[0]


def fold_kernel(count, with_loss, extras, after, *refs):
    kept_ref, arrived, refs = refs[0], refs[1 : 1 + count], refs[1 + count :]
    node_blks = kept_ref.shape[0]
    if with_loss:
        loss_ref, refs = refs[0], refs[1:]
    extra_in, refs = refs[:extras], refs[extras + after :]
    out_ref, extra_out = refs[0], refs[1:]
    for block in range(node_blks):
        total = pair_sum([ref[block].astype(jnp.float32) for ref in arrived])
        out_ref[block] = (kept_ref[block] + total).astype(jnp.bfloat16)
    if with_loss:
        both = from_parts(loss_ref[loss_ref.shape[0] - 1]) + from_parts(arrived[-1][node_blks])
        out_ref[node_blks] = to_parts(both, loss_ref.shape[1:])
    for source, target in zip(extra_in, extra_out):
        target[...] = source[...]


def settle_kernel(count, arc_total, scen_total, last, *refs):
    kept_ref, arrived, refs = refs[0], refs[1 : 1 + count], refs[1 + count :]
    loss_ref, base_ref, risk_ref, excess_ref, level_ref, sum_ref, other_ref = refs[:7]
    duals_out, half_out, risk_out, excess_out, level_out, sum_out = refs[7:]
    node_blks, _, rows = base_ref.shape
    for block in range(node_blks):
        total = kept_ref[block] + pair_sum([ref[block].astype(jnp.float32) for ref in arrived])
        duals = base_ref[block] - dual_step * total
        if last:
            duals_out[:, block * rows : (block + 1) * rows] = duals
        else:
            duals_out[block] = duals
        half_out[block] = duals.astype(jnp.bfloat16)
    losses = from_parts(loss_ref[node_blks]) + from_parts(arrived[-1][node_blks])
    losses = losses / arc_total
    mean_risk = (sum_ref[...] + other_ref[...]) / scen_total
    level = level_ref[...]
    level_new = level - primal_step * (1.0 - mean_risk)
    level_bar = 2.0 * level_new - level
    level_out[...] = level_new
    risk = risk_ref[...]
    excess = excess_ref[...]
    excess_new = jnp.maximum(excess - primal_step * (tail_weight - risk), 0.0)
    excess_bar = 2.0 * excess_new - excess
    excess_out[...] = excess_new
    risk_new = jnp.maximum(risk + risk_step * (losses - excess_bar - level_bar[:1]), 0.0)
    risk_out[...] = risk_new
    sum_out[...] = jnp.broadcast_to(jnp.sum(risk_new, axis=0, keepdims=True), sum_out.shape)


def local_forward_kernel(
    touches,
    group,
    steps,
    index_ref,
    bar_ref,
    blocks_ref,
    duals_ref,
    demand_ref,
    out_ref,
    total,
):
    rows = blocks_ref.shape[-1]
    step = pl.program_id(0)
    first = step * group

    @pl.when(step == 0)
    def _():
        total[...] = jnp.zeros_like(total)

    for member in range(group):
        right = jnp.concatenate([blocks_ref[member, k] for k in range(touches)], axis=1)
        products = jnp.dot(
            bar_ref[:, member * rows : (member + 1) * rows],
            right,
            preferred_element_type=jnp.float32,
        )
        for k in range(touches):
            place = index_ref[first + member, k]
            total[place] += products[:, k * rows : (k + 1) * rows]

    @pl.when(step == steps - 1)
    def _():
        out_ref[...] = duals_ref[...] + dual_step * (demand_ref[...] - total[...])


def whole(*shape):
    return pl.BlockSpec(shape, lambda i, *_: (0,) * len(shape))


def vmem_limit(peers):
    return (8 + peers + peers // 4) * MIB


def params(peers=8):
    return pltpu.CompilerParams(
        dimension_semantics=("arbitrary",), vmem_limit_bytes=vmem_limit(peers)
    )


def local_adjoint(index, panel, blocks, after):
    arc_blks, touches, rows, _ = blocks.shape
    scen_rows = panel.shape[1]
    group = GROUP
    return pl.pallas_call(
        functools.partial(local_adjoint_kernel, touches, group),
        out_shape=jax.ShapeDtypeStruct((scen_rows, arc_blks * rows), jnp.float32),
        grid_spec=pltpu.PrefetchScalarGridSpec(
            num_scalar_prefetch=1,
            grid=(arc_blks // group,),
            in_specs=[
                whole(*panel.shape),
                pl.BlockSpec((group, touches, rows, rows), lambda i, *_: (i, 0, 0, 0)),
            ]
            + [pl.BlockSpec(memory_space=pl.ANY)] * len(after),
            out_specs=pl.BlockSpec((scen_rows, group * rows), lambda i, *_: (0, i)),
        ),
        compiler_params=params(),
        cost_estimate=pl.CostEstimate(
            flops=2 * scen_rows * blocks.size, bytes_accessed=2 * blocks.size, transcendentals=0
        ),
        name="local_adjoint",
    )(index, panel, blocks, *after)


def head_step(places, panels, heads, pulled, flows, costs, risk, sums):
    arc_blks, rows, _ = heads.shape
    scen_rows = flows.shape[0]
    peers = len(panels)
    node_blks = panels[0].shape[0]
    group = HEAD_GROUP
    steps = arc_blks // group
    kept = (node_blks, scen_rows, rows)
    sent = [kept] * (peers // 2)
    sent[-1] = (node_blks + 1, scen_rows, rows)
    arcs = pl.BlockSpec((scen_rows, group * rows), lambda i, *_: (0, i))
    results = pl.pallas_call(
        functools.partial(head_kernel, group, steps, peers),
        out_shape=[
            jax.ShapeDtypeStruct(flows.shape, jnp.float32),
            jax.ShapeDtypeStruct(flows.shape, jnp.bfloat16),
            jax.ShapeDtypeStruct(sums[0].shape, jnp.float32),
        ]
        + [jax.ShapeDtypeStruct(kept, jnp.float32)] * (peers // 2)
        + [jax.ShapeDtypeStruct(shape, jnp.bfloat16) for shape in sent],
        grid_spec=pltpu.PrefetchScalarGridSpec(
            num_scalar_prefetch=1,
            grid=(steps,),
            in_specs=[whole(*panels[0].shape)] * peers
            + [
                pl.BlockSpec((group, rows, rows), lambda i, *_: (i, 0, 0)),
                arcs,
                arcs,
                pl.BlockSpec((1, group * rows), lambda i, *_: (0, i)),
                whole(scen_rows, rows),
                whole(*sums[0].shape),
                whole(*sums[0].shape),
            ],
            out_specs=[arcs, arcs, whole(*sums[0].shape)]
            + [whole(*kept)] * (peers // 2)
            + [whole(*shape) for shape in sent],
            scratch_shapes=[
                pltpu.VMEM((peers * node_blks, scen_rows, rows), jnp.bfloat16),
                pltpu.VMEM((peers * node_blks, scen_rows, rows), jnp.float32),
                pltpu.VMEM((scen_rows, group * rows), jnp.float32),
                pltpu.VMEM((scen_rows, rows), jnp.float32),
            ],
        ),
        compiler_params=params(peers),
        cost_estimate=pl.CostEstimate(
            flops=4 * scen_rows * heads.size,
            bytes_accessed=2 * heads.size + 14 * flows.size + 4 * peers * panels[0].size,
            transcendentals=0,
        ),
        name="head_step",
    )(places, *panels, heads, pulled, flows, costs, risk, *sums)
    half = peers // 2
    kept = dict(zip(inner(peers), results[3 : 3 + half]))
    sends = dict(zip(leaves(peers), results[3 + half :]))
    return *results[:3], kept, sends


def small_cost(*arrays):
    size = sum(a.size for a in arrays)
    return pl.CostEstimate(flops=size, bytes_accessed=2 * size, transcendentals=0)


def fold(kept, arrived, loss, extras, after):
    node_blks, scen_rows, rows = kept.shape
    with_loss = loss is not None
    operands = [kept, *arrived] + ([loss] if with_loss else []) + list(extras)
    vmem = pl.BlockSpec(memory_space=pltpu.VMEM)
    out_shape = [jax.ShapeDtypeStruct((node_blks + with_loss, scen_rows, rows), jnp.bfloat16)]
    out_shape += [jax.ShapeDtypeStruct(extra.shape, extra.dtype) for extra in extras]
    results = pl.pallas_call(
        functools.partial(fold_kernel, len(arrived), with_loss, len(extras), len(after)),
        out_shape=out_shape,
        in_specs=[vmem] * len(operands) + [pl.BlockSpec(memory_space=pl.ANY)] * len(after),
        out_specs=[vmem] * len(out_shape),
        compiler_params=pltpu.CompilerParams(vmem_limit_bytes=vmem_limit(8)),
        cost_estimate=small_cost(*operands),
        name="fold",
    )(*operands, *after)
    return results[0], results[1:]


def settle(kept, arrived, loss, base, risk, excess, level, sums, arc_total, scen_total, last):
    node_blks, scen_rows, rows = base.shape
    duals = (scen_rows, node_blks * rows) if last else base.shape
    return pl.pallas_call(
        functools.partial(settle_kernel, len(arrived), arc_total, scen_total, last),
        out_shape=(
            jax.ShapeDtypeStruct(duals, jnp.float32),
            jax.ShapeDtypeStruct(base.shape, jnp.bfloat16),
            jax.ShapeDtypeStruct(risk.shape, jnp.float32),
            jax.ShapeDtypeStruct(risk.shape, jnp.float32),
            jax.ShapeDtypeStruct(level.shape, jnp.float32),
            jax.ShapeDtypeStruct(level.shape, jnp.float32),
        ),
        compiler_params=pltpu.CompilerParams(vmem_limit_bytes=vmem_limit(8)),
        cost_estimate=small_cost(kept, *arrived, base),
        name="settle",
    )(kept, *arrived, loss, base, risk, excess, level, *sums)


def local_forward(index, bar, blocks, duals, demand):
    arc_blks, touches, rows, _ = blocks.shape
    scen_rows = bar.shape[0]
    group = GROUP
    steps = arc_blks // group
    return pl.pallas_call(
        functools.partial(local_forward_kernel, touches, group, steps),
        out_shape=jax.ShapeDtypeStruct(duals.shape, jnp.float32),
        grid_spec=pltpu.PrefetchScalarGridSpec(
            num_scalar_prefetch=1,
            grid=(steps,),
            in_specs=[
                pl.BlockSpec((scen_rows, group * rows), lambda i, *_: (0, i)),
                pl.BlockSpec((group, touches, rows, rows), lambda i, *_: (i, 0, 0, 0)),
                whole(*duals.shape),
                whole(*duals.shape),
            ],
            out_specs=whole(*duals.shape),
            scratch_shapes=[pltpu.VMEM(duals.shape, jnp.float32)],
        ),
        compiler_params=params(),
        cost_estimate=pl.CostEstimate(
            flops=2 * scen_rows * blocks.size, bytes_accessed=2 * blocks.size, transcendentals=0
        ),
        name="local_forward",
    )(index, bar, blocks, duals, demand)


def relay(arrived, risk_sum, after):
    def kernel(arrived_ref, sum_ref, *refs):
        arrived_out, sum_out = refs[-2:]
        arrived_out[...] = arrived_ref[...]
        sum_out[...] = sum_ref[...]

    vmem = pl.BlockSpec(memory_space=pltpu.VMEM)
    return pl.pallas_call(
        kernel,
        out_shape=(
            jax.ShapeDtypeStruct(arrived.shape, arrived.dtype),
            jax.ShapeDtypeStruct(risk_sum.shape, risk_sum.dtype),
        ),
        in_specs=[vmem, vmem] + [pl.BlockSpec(memory_space=pl.ANY)] * len(after),
        out_specs=(vmem, vmem),
        compiler_params=pltpu.CompilerParams(vmem_limit_bytes=vmem_limit(8)),
        cost_estimate=small_cost(arrived),
        name="relay",
    )(arrived, risk_sum, *after)


def sum_rows(values, shape):
    def kernel(values_ref, out_ref):
        out_ref[...] = jnp.broadcast_to(jnp.sum(values_ref[...], axis=0, keepdims=True), shape)

    return pl.pallas_call(
        kernel,
        out_shape=jax.ShapeDtypeStruct(shape, jnp.float32),
        compiler_params=pltpu.CompilerParams(vmem_limit_bytes=vmem_limit(8)),
        cost_estimate=small_cost(values),
        name="sum_rows",
    )(values)


def swap(value, axis, distance):
    size = lax.axis_size(axis)
    return lax.ppermute(value, axis, [(i, i ^ distance) for i in range(size)])


def gather_panels(own, risk_sum, after):
    peers = lax.axis_size("net")
    panels = [own] + [None] * (peers - 1)
    for distance in sorted(range(1, peers), key=lambda k: (k.bit_count(), -k)):
        hop = last_hop(distance)
        panels[distance] = swap(panels[distance ^ hop], "net", hop)
        if distance == peers // 2:
            panels[distance], risk_sum = relay(panels[distance], risk_sum, after)
    return panels, risk_sum


def per_device(
    arc_flows,
    node_duals,
    demand,
    excess,
    risk_duals,
    threshold,
    arc_costs,
    local_blocks,
    head_blocks,
    local_index,
    head_index,
):
    rows = local_blocks.shape[-1]
    scen_rows = arc_flows.shape[0]
    node_blks = node_duals.shape[1] // rows
    net_size = lax.axis_size("net")
    arc_total = arc_flows.shape[1] * net_size
    scen_total = scen_rows * lax.axis_size("scen")
    costs = arc_costs.reshape(1, -1)
    distance = jnp.bitwise_xor(head_index // node_blks, lax.axis_index("net"))
    places = distance * node_blks + head_index % node_blks
    scen_size = lax.axis_size("scen")
    wide = (scen_rows, rows)
    flat = (8, rows)

    def to_blocks(panel):
        return panel.reshape(scen_rows, node_blks, rows).transpose(1, 0, 2)

    duals = to_blocks(node_duals)
    half = duals.astype(jnp.bfloat16)
    wanted = to_blocks(demand)
    flows = arc_flows
    excess_now = jnp.broadcast_to(excess[:, None], wide)
    risk = jnp.broadcast_to(risk_duals[:, None], wide)
    level = jnp.broadcast_to(threshold[:, None], flat)
    risk_sum = sum_rows(risk, flat)
    for iteration in range(ROUNDS):
        pulled = local_adjoint(local_index, half, local_blocks, ())
        panels, risk_sum = gather_panels(half, risk_sum, (pulled,))
        sums = (risk_sum, swap(risk_sum, "scen", 1))
        flows, bar, risk_sum, kept, sends = head_step(
            places, panels, head_blocks, pulled, flows, costs, risk, sums
        )
        base = local_forward(local_index, bar, local_blocks, duals, wanted)
        tops = sorted(inner(net_size), key=lambda k: (-k.bit_count(), -k))[:-1]
        loss = sends[net_size - 1]
        arrived = {}
        for top in tops:
            below = sorted(children(top, net_size))
            for k in below:
                arrived[k] = swap(sends[k], "net", last_hop(k))
            chain = net_size - 1 in below or loss_top in below
            after = (base,) if top == tops[0] else ()
            extras = (risk_sum,) if top == net_size // 2 else ()
            sends[top], passed = fold(
                kept[top], [arrived[k] for k in below], loss if chain else None, extras, after
            )
            if chain:
                loss_top, loss = top, sends[top]
            if extras:
                (risk_sum,) = passed
        below = sorted(children(0, net_size))
        arrived = [swap(sends[k], "net", last_hop(k)) for k in below]
        stride = 2
        while 2 * stride < scen_size:
            risk_sum = risk_sum + swap(risk_sum, "scen", stride)
            stride *= 2
        sums = (risk_sum, swap(risk_sum, "scen", stride))
        duals, half, risk, excess_now, level, risk_sum = settle(
            kept[0],
            arrived,
            loss,
            base,
            risk,
            excess_now,
            level,
            sums,
            arc_total,
            scen_total,
            iteration == ROUNDS - 1,
        )
    return (flows, duals, excess_now[:, 0], risk[:, 0], level[0, :1])


def solution(mesh):
    placed = (
        P("scen", "net"),
        P("scen", "net"),
        P("scen", "net"),
        P("scen"),
        P("scen"),
        P(),
        P("net"),
        P("net", None, None, None),
        P("net", None, None),
        P("net", None),
        P("net"),
    )
    return jax.shard_map(
        per_device,
        mesh=mesh,
        in_specs=placed,
        out_specs=(P("scen", "net"), P("scen", "net"), P("scen"), P("scen"), P()),
        check_vma=False,
    )
```

```python
import functools

import jax
import jax.numpy as jnp
from jax import lax
from jax.experimental import pallas as pl
from jax.experimental.pallas import tpu as pltpu
from jax.sharding import PartitionSpec as P

ROUNDS = 3

primal_step = 0.5
dual_step = 0.5
risk_step = 1.0
tail_weight = 2.0

MIB = 1024 * 1024
GROUP = 8
HEAD_GROUP = 16
KERNEL_COST = 100000


def contract_last(left, right):
    return lax.dot_general(
        left, right, (((1,), (1,)), ((), ())), preferred_element_type=jnp.float32
    )


def local_adjoint_kernel(
    touches, group, index_ref, panel_ref, blocks_ref, *refs
):
    out_ref = refs[-1]
    rows = blocks_ref.shape[-1]
    first = pl.program_id(0) * group
    for member in range(group):
        left = jnp.concatenate(
            [panel_ref[index_ref[first + member, k]] for k in range(touches)], axis=1
        )
        right = jnp.concatenate([blocks_ref[member, k] for k in range(touches)], axis=1)
        out_ref[:, member * rows : (member + 1) * rows] = contract_last(left, right)


def to_parts(column, shape):
    high = column.astype(jnp.bfloat16).astype(jnp.float32)
    rest = column - high
    middle = rest.astype(jnp.bfloat16).astype(jnp.float32)
    low = rest - middle
    lane = lax.broadcasted_iota(jnp.int32, shape, 1)
    packed = jnp.where(
        lane == 0, high, jnp.where(lane == 1, middle, jnp.where(lane == 2, low, 0.0))
    )
    return packed.astype(jnp.bfloat16)


def from_parts(parts):
    return jnp.sum(parts.astype(jnp.float32), axis=1, keepdims=True)


def head_kernel(group, steps, peers, late, scen_total, index_ref, *refs):
    panels, refs = refs[:peers], refs[peers:]
    heads_ref, pulled_ref, flows_ref, costs_ref, risk_ref, level_ref, sum_ref, other_ref = refs[:8]
    flows_out, bar_out, risk_out, level_out, sum_out, refs = *refs[8:13], refs[13:]
    kept, refs = refs[: peers // 2], refs[peers // 2 :]
    sends, (panel, terms, pulled, loss) = refs[:-4], refs[-4:]
    rows = heads_ref.shape[-1]
    node_blks = panels[0].shape[0]
    step = pl.program_id(0)
    first = step * group

    @pl.when(step == 0)
    def _():
        terms[...] = jnp.zeros_like(terms)
        loss[...] = jnp.zeros_like(loss)
        risk_total = sum_ref[...] + other_ref[...]
        if late:
            level_new, level_bar = next_level(level_ref[...], risk_total, scen_total)
            risk_start = jnp.maximum(risk_ref[...] - risk_step * level_bar[:1], 0.0)
            risk_out[...] = risk_start
            level_out[...] = level_new
            sum_out[...] = add_rows(risk_start, sum_out.shape)
        else:
            risk_out[...] = risk_ref[...]
            level_out[...] = level_ref[...]
            sum_out[...] = risk_total
        for peer in range(peers):
            panel[peer * node_blks : (peer + 1) * node_blks] = panels[peer][...]

    places = [index_ref[first + member] for member in range(group)]
    spans = [slice(member * rows, (member + 1) * rows) for member in range(group)]
    for member in range(group):
        pulled[:, spans[member]] = contract_last(panel[places[member]], heads_ref[member])
    risk = risk_out[...]
    loss_sum = jnp.zeros_like(risk)
    for columns in spans:
        flows = flows_ref[:, columns]
        cost = costs_ref[:, columns]
        gradient = risk * cost - (pulled[:, columns] + pulled_ref[:, columns])
        flows_new = jnp.maximum(flows - primal_step * gradient, 0.0)
        bar = 2.0 * flows_new - flows
        flows_out[:, columns] = flows_new
        loss_sum += cost * bar
        bar_out[:, columns] = bar.astype(jnp.bfloat16)
    loss[...] += loss_sum
    products = [
        jnp.dot(bar_out[:, spans[m]], heads_ref[m], preferred_element_type=jnp.float32)
        for m in range(group)
    ]
    for member in range(group):
        terms[places[member]] += products[member]

    @pl.when(step == steps - 1)
    def _():
        loss_parts = to_parts(jnp.sum(loss[...], axis=1, keepdims=True), loss.shape)
        for out, distance in zip(kept, inner(peers)):
            out[...] = terms[distance * node_blks : (distance + 1) * node_blks]
        for out, distance in zip(sends, leaves(peers)):
            out[:node_blks] = terms[distance * node_blks : (distance + 1) * node_blks].astype(
                jnp.bfloat16
            )
        sends[-1][node_blks] = loss_parts


def last_hop(distance):
    return 2 if distance == 3 else distance & -distance


def children(distance, peers):
    return [k for k in range(1, peers) if k ^ last_hop(k) == distance]


def inner(peers):
    return [k for k in range(peers) if children(k, peers)]


def leaves(peers):
    return [k for k in range(peers) if not children(k, peers)]


def pair_sum(values):
    while len(values) > 1:
        values = [a + b for a, b in zip(values[::2], values[1::2])] + values[len(values) // 2 * 2 :]
    return values[0]


def fold_kernel(counts, with_loss, extras, after, *refs):
    inputs, refs = refs[: sum(counts) + len(counts)], refs[sum(counts) + len(counts) :]
    if with_loss:
        loss_ref, refs = refs[0], refs[1:]
    extra_in, refs = refs[:extras], refs[extras + after :]
    outs, extra_out = refs[: len(counts)], refs[len(counts) :]
    node_blks = inputs[0].shape[0]
    for number, (count, out_ref) in enumerate(zip(counts, outs)):
        kept_ref, arrived, inputs = inputs[0], inputs[1 : 1 + count], inputs[1 + count :]
        for block in range(node_blks):
            total = pair_sum([ref[block].astype(jnp.float32) for ref in arrived])
            out_ref[block] = (kept_ref[block] + total).astype(jnp.bfloat16)
        if with_loss and number == 0:
            both = from_parts(loss_ref[loss_ref.shape[0] - 1]) + from_parts(arrived[-1][node_blks])
            out_ref[node_blks] = to_parts(both, loss_ref.shape[1:])
    for source, target in zip(extra_in, extra_out):
        target[...] = source[...]


def next_level(level, risk_total, scen_total):
    level_new = level - primal_step * (1.0 - risk_total / scen_total)
    return level_new, 2.0 * level_new - level


def add_rows(values, shape):
    return jnp.broadcast_to(jnp.sum(values, axis=0, keepdims=True), shape)


def as_row(values):
    rows = values.shape[0]
    picked = lax.broadcasted_iota(jnp.int32, values.shape, 0) == lax.broadcasted_iota(
        jnp.int32, values.shape, 1
    )
    return jnp.sum(jnp.where(picked, values, 0.0), axis=0, keepdims=True)[:, :rows]


def settle_kernel(count, arc_total, scen_total, kind, *refs):
    kept_ref, arrived, refs = refs[0], refs[1 : 1 + count], refs[1 + count :]
    loss_ref, base_ref, risk_ref, excess_ref, level_ref, sum_ref, other_ref = refs[:7]
    duals_out, half_out, risk_out, excess_out, level_out, sum_out = refs[7:]
    node_blks, _, rows = base_ref.shape
    for block in range(node_blks):
        total = kept_ref[block] + pair_sum([ref[block].astype(jnp.float32) for ref in arrived])
        duals = base_ref[block] - dual_step * total
        if kind == "last":
            duals_out[:, block * rows : (block + 1) * rows] = duals
        else:
            duals_out[block] = duals
            half_out[block] = duals.astype(jnp.bfloat16)
    losses = from_parts(loss_ref[node_blks]) + from_parts(arrived[-1][node_blks])
    losses = losses / arc_total
    risk = risk_ref[...]
    excess = excess_ref[...]
    excess_new = jnp.maximum(excess - primal_step * (tail_weight - risk), 0.0)
    excess_bar = 2.0 * excess_new - excess
    risk_new = risk + risk_step * (losses - excess_bar)
    if kind == "early":
        risk_out[...] = risk_new
        excess_out[...] = excess_new
        return
    risk_total = sum_ref[...] if kind == "first" else sum_ref[...] + other_ref[...]
    level_new, level_bar = next_level(level_ref[...], risk_total, scen_total)
    risk_new = jnp.maximum(risk_new - risk_step * level_bar[:1], 0.0)
    if kind == "last":
        risk_out[...] = as_row(risk_new)
        excess_out[...] = as_row(excess_new)
        level_out[...] = level_new[:1, :1]
    else:
        risk_out[...] = risk_new
        excess_out[...] = excess_new
        level_out[...] = level_new
        sum_out[...] = add_rows(risk_new, sum_out.shape)


def local_forward_kernel(
    touches,
    group,
    steps,
    index_ref,
    bar_ref,
    blocks_ref,
    duals_ref,
    demand_ref,
    after_ref,
    out_ref,
    total,
):
    rows = blocks_ref.shape[-1]
    step = pl.program_id(0)
    first = step * group

    @pl.when(step == 0)
    def _():
        total[...] = jnp.zeros_like(total)

    for member in range(group):
        right = jnp.concatenate([blocks_ref[member, k] for k in range(touches)], axis=1)
        products = jnp.dot(
            bar_ref[:, member * rows : (member + 1) * rows],
            right,
            preferred_element_type=jnp.float32,
        )
        for k in range(touches):
            place = index_ref[first + member, k]
            total[place] += products[:, k * rows : (k + 1) * rows]

    @pl.when(step == steps - 1)
    def _():
        out_ref[...] = duals_ref[...] + dual_step * (demand_ref[...] - total[...])


def whole(*shape):
    return pl.BlockSpec(shape, lambda i, *_: (0,) * len(shape))


def vmem_limit(peers):
    return (8 + peers + peers // 4) * MIB


def params(peers=8):
    return pltpu.CompilerParams(
        dimension_semantics=("arbitrary",), vmem_limit_bytes=vmem_limit(peers)
    )


def local_adjoint(index, panel, blocks, after):
    arc_blks, touches, rows, _ = blocks.shape
    scen_rows = panel.shape[1]
    group = GROUP
    return pl.pallas_call(
        functools.partial(local_adjoint_kernel, touches, group),
        out_shape=jax.ShapeDtypeStruct((scen_rows, arc_blks * rows), jnp.float32),
        grid_spec=pltpu.PrefetchScalarGridSpec(
            num_scalar_prefetch=1,
            grid=(arc_blks // group,),
            in_specs=[
                whole(*panel.shape),
                pl.BlockSpec((group, touches, rows, rows), lambda i, *_: (i, 0, 0, 0)),
            ]
            + [pl.BlockSpec(memory_space=pl.ANY)] * len(after),
            out_specs=pl.BlockSpec((scen_rows, group * rows), lambda i, *_: (0, i)),
        ),
        compiler_params=params(),
        cost_estimate=pl.CostEstimate(
            flops=KERNEL_COST, bytes_accessed=KERNEL_COST, transcendentals=0
        ),
        name="local_adjoint",
    )(index, panel, blocks, *after)


def head_step(places, panels, heads, pulled, flows, costs, risk, level, sums, late, scen_total):
    arc_blks, rows, _ = heads.shape
    scen_rows = flows.shape[0]
    peers = len(panels)
    node_blks = panels[0].shape[0]
    group = HEAD_GROUP
    steps = arc_blks // group
    kept = (node_blks, scen_rows, rows)
    sent = [kept] * (peers // 2)
    sent[-1] = (node_blks + 1, scen_rows, rows)
    arcs = pl.BlockSpec((scen_rows, group * rows), lambda i, *_: (0, i))
    results = pl.pallas_call(
        functools.partial(head_kernel, group, steps, peers, late, scen_total),
        out_shape=[
            jax.ShapeDtypeStruct(flows.shape, jnp.float32),
            jax.ShapeDtypeStruct(flows.shape, jnp.bfloat16),
            jax.ShapeDtypeStruct(risk.shape, jnp.float32),
            jax.ShapeDtypeStruct(level.shape, jnp.float32),
            jax.ShapeDtypeStruct(level.shape, jnp.float32),
        ]
        + [jax.ShapeDtypeStruct(kept, jnp.float32)] * (peers // 2)
        + [jax.ShapeDtypeStruct(shape, jnp.bfloat16) for shape in sent],
        grid_spec=pltpu.PrefetchScalarGridSpec(
            num_scalar_prefetch=1,
            grid=(steps,),
            in_specs=[whole(*panels[0].shape)] * peers
            + [
                pl.BlockSpec((group, rows, rows), lambda i, *_: (i, 0, 0)),
                arcs,
                arcs,
                pl.BlockSpec((1, group * rows), lambda i, *_: (0, i)),
                whole(scen_rows, rows),
                whole(*level.shape),
                whole(*level.shape),
                whole(*level.shape),
            ],
            out_specs=[arcs, arcs, whole(scen_rows, rows), whole(*level.shape), whole(*level.shape)]
            + [whole(*kept)] * (peers // 2)
            + [whole(*shape) for shape in sent],
            scratch_shapes=[
                pltpu.VMEM((peers * node_blks, scen_rows, rows), jnp.bfloat16),
                pltpu.VMEM((peers * node_blks, scen_rows, rows), jnp.float32),
                pltpu.VMEM((scen_rows, group * rows), jnp.float32),
                pltpu.VMEM((scen_rows, rows), jnp.float32),
            ],
        ),
        compiler_params=params(peers),
        cost_estimate=pl.CostEstimate(
            flops=4 * scen_rows * heads.size,
            bytes_accessed=2 * heads.size + 14 * flows.size + 4 * peers * panels[0].size,
            transcendentals=0,
        ),
        name="head_step",
    )(places, *panels, heads, pulled, flows, costs, risk, level, *sums)
    half = peers // 2
    kept = dict(zip(inner(peers), results[5 : 5 + half]))
    sends = dict(zip(leaves(peers), results[5 + half :]))
    return *results[:5], kept, sends


def small_cost(*arrays):
    size = sum(a.size for a in arrays)
    return pl.CostEstimate(flops=size, bytes_accessed=2 * size, transcendentals=0)


def fold(tops, loss, extras, after):
    node_blks, scen_rows, rows = tops[0][0].shape
    with_loss = loss is not None
    operands = [array for kept, arrived in tops for array in (kept, *arrived)]
    operands += ([loss] if with_loss else []) + list(extras)
    vmem = pl.BlockSpec(memory_space=pltpu.VMEM)
    out_shape = [
        jax.ShapeDtypeStruct((node_blks + (with_loss and number == 0), scen_rows, rows), jnp.bfloat16)
        for number in range(len(tops))
    ]
    out_shape += [jax.ShapeDtypeStruct(extra.shape, extra.dtype) for extra in extras]
    counts = [len(arrived) for _, arrived in tops]
    results = pl.pallas_call(
        functools.partial(fold_kernel, counts, with_loss, len(extras), len(after)),
        out_shape=out_shape,
        in_specs=[vmem] * len(operands) + [pl.BlockSpec(memory_space=pl.ANY)] * len(after),
        out_specs=[vmem] * len(out_shape),
        compiler_params=pltpu.CompilerParams(vmem_limit_bytes=vmem_limit(8)),
        cost_estimate=small_cost(*operands),
        name="fold",
    )(*operands, *after)
    return results[: len(tops)], results[len(tops) :]


def settle(kept, arrived, loss, base, risk, excess, level, sums, arc_total, scen_total, kind):
    node_blks, scen_rows, rows = base.shape
    last = kind == "last"
    return pl.pallas_call(
        functools.partial(settle_kernel, len(arrived), arc_total, scen_total, kind),
        out_shape=(
            jax.ShapeDtypeStruct((scen_rows, node_blks * rows) if last else base.shape, jnp.float32),
            jax.ShapeDtypeStruct(base.shape, jnp.bfloat16),
            jax.ShapeDtypeStruct((1, scen_rows) if last else risk.shape, jnp.float32),
            jax.ShapeDtypeStruct((1, scen_rows) if last else risk.shape, jnp.float32),
            jax.ShapeDtypeStruct((1, 1) if last else level.shape, jnp.float32),
            jax.ShapeDtypeStruct(level.shape, jnp.float32),
        ),
        compiler_params=pltpu.CompilerParams(vmem_limit_bytes=vmem_limit(8)),
        cost_estimate=small_cost(kept, *arrived, base),
        name="settle",
    )(kept, *arrived, loss, base, risk, excess, level, *sums)


def local_forward(index, bar, blocks, duals, demand, after):
    arc_blks, touches, rows, _ = blocks.shape
    scen_rows = bar.shape[0]
    group = GROUP
    steps = arc_blks // group
    return pl.pallas_call(
        functools.partial(local_forward_kernel, touches, group, steps),
        out_shape=jax.ShapeDtypeStruct(duals.shape, jnp.float32),
        grid_spec=pltpu.PrefetchScalarGridSpec(
            num_scalar_prefetch=1,
            grid=(steps,),
            in_specs=[
                pl.BlockSpec((scen_rows, group * rows), lambda i, *_: (0, i)),
                pl.BlockSpec((group, touches, rows, rows), lambda i, *_: (i, 0, 0, 0)),
                whole(*duals.shape),
                whole(*duals.shape),
                pl.BlockSpec(memory_space=pl.ANY),
            ],
            out_specs=whole(*duals.shape),
            scratch_shapes=[pltpu.VMEM(duals.shape, jnp.float32)],
        ),
        compiler_params=params(),
        cost_estimate=pl.CostEstimate(
            flops=KERNEL_COST, bytes_accessed=KERNEL_COST, transcendentals=0
        ),
        name="local_forward",
    )(index, bar, blocks, duals, demand, after)


def relay(arrived, risk_sum, after):
    def kernel(arrived_ref, sum_ref, *refs):
        arrived_out, sum_out = refs[-2:]
        arrived_out[...] = arrived_ref[...]
        sum_out[...] = sum_ref[...]

    vmem = pl.BlockSpec(memory_space=pltpu.VMEM)
    return pl.pallas_call(
        kernel,
        out_shape=(
            jax.ShapeDtypeStruct(arrived.shape, arrived.dtype),
            jax.ShapeDtypeStruct(risk_sum.shape, risk_sum.dtype),
        ),
        in_specs=[vmem, vmem] + [pl.BlockSpec(memory_space=pl.ANY)] * len(after),
        out_specs=(vmem, vmem),
        compiler_params=pltpu.CompilerParams(vmem_limit_bytes=vmem_limit(8)),
        cost_estimate=small_cost(arrived),
        name="relay",
    )(arrived, risk_sum, *after)


def sum_rows(values, shape):
    def kernel(values_ref, out_ref):
        out_ref[...] = add_rows(values_ref[...], shape)

    return pl.pallas_call(
        kernel,
        out_shape=jax.ShapeDtypeStruct(shape, jnp.float32),
        compiler_params=pltpu.CompilerParams(vmem_limit_bytes=vmem_limit(8)),
        cost_estimate=small_cost(values),
        name="sum_rows",
    )(values)


def swap(value, axis, distance):
    size = lax.axis_size(axis)
    return lax.ppermute(value, axis, [(i, i ^ distance) for i in range(size)])


def exchange_lowest(distance):
    return (distance & ~3) | ((distance & 1) << 1) | ((distance >> 1) & 1)


def swap_net(value, distance):
    net_size, scen_size = lax.axis_size("net"), lax.axis_size("scen")
    pairs = []
    for net in range(net_size):
        for scen in range(scen_size):
            hop = exchange_lowest(distance) if scen % 2 else distance
            pairs.append((net * scen_size + scen, (net ^ hop) * scen_size + scen))
    return lax.ppermute(value, ("net", "scen"), pairs)


def gather_panels(own, risk_sum, after):
    peers = lax.axis_size("net")
    panels = [own] + [None] * (peers - 1)
    order = sorted(range(1, peers), key=lambda k: (k.bit_count(), -k))
    for distance in order:
        hop = last_hop(distance)
        panels[distance] = swap_net(panels[distance ^ hop], hop)
        if distance == 1:
            far = peers // 2
            firsts = tuple(panels[k] for k in order if k.bit_count() == 1 and k != far)
            panels[far], risk_sum = relay(panels[far], risk_sum, after + firsts)
    return panels, risk_sum


def per_device(
    arc_flows,
    node_duals,
    demand,
    excess,
    risk_duals,
    threshold,
    arc_costs,
    local_blocks,
    head_blocks,
    local_index,
    head_index,
):
    rows = local_blocks.shape[-1]
    scen_rows = arc_flows.shape[0]
    node_blks = node_duals.shape[1] // rows
    net_size = lax.axis_size("net")
    arc_total = arc_flows.shape[1] * net_size
    scen_total = scen_rows * lax.axis_size("scen")
    costs = arc_costs.reshape(1, -1)
    distance = jnp.bitwise_xor(head_index // node_blks, lax.axis_index("net"))
    distance = jnp.where(lax.axis_index("scen") % 2 == 1, exchange_lowest(distance), distance)
    places = distance * node_blks + head_index % node_blks
    scen_size = lax.axis_size("scen")
    wide = (scen_rows, rows)
    flat = (8, rows)

    def to_blocks(panel):
        return panel.reshape(scen_rows, node_blks, rows).transpose(1, 0, 2)

    duals = to_blocks(node_duals)
    half = duals.astype(jnp.bfloat16)
    wanted = to_blocks(demand)
    flows = arc_flows
    excess_now = jnp.broadcast_to(excess[:, None], wide)
    risk = jnp.broadcast_to(risk_duals[:, None], wide)
    level = jnp.broadcast_to(threshold[:, None], flat)
    risk_sum = sum_rows(risk, flat)
    early = [1 << bit for bit in range(1, scen_size.bit_length() - 1)][::-1]
    zero = jnp.zeros_like(risk_sum)
    for iteration in range(ROUNDS):
        kind = "first" if iteration == 0 else "last" if iteration == ROUNDS - 1 else "early"
        pulled = local_adjoint(local_index, half, local_blocks, ())
        if kind == "first":
            panels, _ = gather_panels(half, risk_sum, (pulled,))
            for stride in early + [1]:
                risk_sum = risk_sum + swap(risk_sum, "scen", stride)
            sums = (risk_sum, zero)
        else:
            panels, risk_sum = gather_panels(half, risk_sum, (pulled,))
            if kind == "early":
                for stride in early[:-1]:
                    risk_sum = risk_sum + swap(risk_sum, "scen", stride)
                sums = (risk_sum, swap(risk_sum, "scen", early[-1]))
            else:
                sums = (risk_sum, swap(risk_sum, "scen", 1))
        flows, bar, risk, level, risk_sum, kept, sends = head_step(
            places,
            panels,
            head_blocks,
            pulled,
            flows,
            costs,
            risk,
            level,
            sums,
            kind == "last",
            scen_total,
        )
        after = ()
        if kind == "last":
            risk_sum = risk_sum + swap(risk_sum, "scen", 1)
            after = (risk_sum,)
        tops = sorted(inner(net_size), key=lambda k: (-k.bit_count(), -k))[:-1]
        groups = [(tops[0], 1)] + [(top,) for top in tops[1:] if top != 1]
        loss, loss_top = sends[net_size - 1], net_size - 1
        for group in groups:
            terms = []
            for top in group:
                below = sorted(children(top, net_size))
                terms.append((kept[top], [swap_net(sends[k], last_hop(k)) for k in below]))
            chain = loss_top ^ last_hop(loss_top) == group[0]
            extras = (risk_sum,) if group[0] == net_size // 2 and kind == "last" else ()
            folded, passed = fold(terms, loss if chain else None, extras, after)
            sends.update(zip(group, folded))
            after = ()
            if chain:
                loss_top, loss = group[0], folded[0]
            if extras:
                (risk_sum,) = passed
        base = local_forward(local_index, bar, local_blocks, duals, wanted, loss)
        below = sorted(children(0, net_size))
        arrived = [swap_net(sends[k], last_hop(k)) for k in below]
        sums = (risk_sum, zero)
        if kind == "last":
            for stride in early[:-1]:
                risk_sum = risk_sum + swap(risk_sum, "scen", stride)
            sums = (risk_sum, swap(risk_sum, "scen", early[-1]))
        duals, half, risk, excess_now, level_next, sum_next = settle(
            kept[0],
            arrived,
            loss,
            base,
            risk,
            excess_now,
            level,
            sums,
            arc_total,
            scen_total,
            kind,
        )
        if kind != "early":
            level, risk_sum = level_next, sum_next
    return (flows, duals, excess_now.reshape(-1), risk.reshape(-1), level.reshape(-1))


def solution(mesh):
    placed = (
        P("scen", "net"),
        P("scen", "net"),
        P("scen", "net"),
        P("scen"),
        P("scen"),
        P(),
        P("net"),
        P("net", None, None, None),
        P("net", None, None),
        P("net", None),
        P("net"),
    )
    return jax.shard_map(
        per_device,
        mesh=mesh,
        in_specs=placed,
        out_specs=(P("scen", "net"), P("scen", "net"), P("scen"), P("scen"), P()),
        check_vma=False,
    )
```

```python
import functools

import jax
import jax.numpy as jnp
from jax import lax
from jax.experimental import pallas as pl
from jax.experimental.pallas import tpu as pltpu
from jax.sharding import PartitionSpec as P

ROUNDS = 3

primal_step = 0.5
dual_step = 0.5
risk_step = 1.0
tail_weight = 2.0

MIB = 1024 * 1024
GROUP = 8
HEAD_GROUP = 16


def contract_last(left, right):
    return lax.dot_general(
        left, right, (((1,), (1,)), ((), ())), preferred_element_type=jnp.float32
    )


def local_adjoint_kernel(
    touches, group, index_ref, panel_ref, blocks_ref, out_ref, token_ref
):
    token_ref[...] = jnp.zeros_like(token_ref)
    rows = blocks_ref.shape[-1]
    first = pl.program_id(0) * group
    for member in range(group):
        left = jnp.concatenate(
            [panel_ref[index_ref[k, first + member]] for k in range(touches)], axis=1
        )
        right = jnp.concatenate([blocks_ref[member, k] for k in range(touches)], axis=1)
        out_ref[:, member * rows : (member + 1) * rows] = contract_last(left, right)


def to_parts(column, shape):
    high = column.astype(jnp.bfloat16).astype(jnp.float32)
    rest = column - high
    middle = rest.astype(jnp.bfloat16).astype(jnp.float32)
    low = rest - middle
    lane = lax.broadcasted_iota(jnp.int32, shape, 1)
    packed = jnp.where(
        lane == 0, high, jnp.where(lane == 1, middle, jnp.where(lane == 2, low, 0.0))
    )
    return packed.astype(jnp.bfloat16)


def from_parts(parts):
    return jnp.sum(parts.astype(jnp.float32), axis=1, keepdims=True)


def head_kernel(group, steps, peers, late, scen_total, index_ref, *refs):
    panels, refs = refs[:peers], refs[peers:]
    heads_ref, pulled_ref, flows_ref, costs_ref, risk_ref, level_ref, sum_ref, other_ref = refs[:8]
    flows_out, bar_out, risk_out, level_out, sum_out, refs = *refs[8:13], refs[13:]
    kept, refs = refs[: peers // 2], refs[peers // 2 :]
    sends, (panel, terms, pulled, loss) = refs[:-4], refs[-4:]
    rows = heads_ref.shape[-1]
    node_blks = panels[0].shape[0]
    step = pl.program_id(0)
    first = step * group

    @pl.when(step == 0)
    def _():
        terms[...] = jnp.zeros_like(terms)
        loss[...] = jnp.zeros_like(loss)
        risk_total = sum_ref[...] + other_ref[...]
        if late:
            level_new, level_bar = next_level(level_ref[...], risk_total, scen_total)
            risk_start = jnp.maximum(risk_ref[...] - risk_step * level_bar[:1], 0.0)
            risk_out[...] = risk_start
            level_out[...] = level_new
            sum_out[...] = add_rows(risk_start, sum_out.shape)
        else:
            risk_out[...] = risk_ref[...]
            level_out[...] = level_ref[...]
            sum_out[...] = risk_total
        for peer in range(peers):
            panel[peer * node_blks : (peer + 1) * node_blks] = panels[peer][...]

    places = [index_ref[first + member] for member in range(group)]
    spans = [slice(member * rows, (member + 1) * rows) for member in range(group)]
    for member in range(group):
        pulled[:, spans[member]] = contract_last(panel[places[member]], heads_ref[member])
    risk = risk_out[...]
    loss_sum = jnp.zeros_like(risk)
    for columns in spans:
        flows = flows_ref[:, columns]
        cost = costs_ref[:, columns]
        gradient = risk * cost - (pulled[:, columns] + pulled_ref[:, columns])
        flows_new = jnp.maximum(flows - primal_step * gradient, 0.0)
        bar = 2.0 * flows_new - flows
        flows_out[:, columns] = flows_new
        loss_sum += cost * bar
        bar_out[:, columns] = bar.astype(jnp.bfloat16)
    loss[...] += loss_sum
    products = [
        jnp.dot(bar_out[:, spans[m]], heads_ref[m], preferred_element_type=jnp.float32)
        for m in range(group)
    ]
    for member in range(group):
        terms[places[member]] += products[member]

    @pl.when(step == steps - 1)
    def _():
        loss_parts = to_parts(jnp.sum(loss[...], axis=1, keepdims=True), loss.shape)
        for out, distance in zip(kept, inner(peers)):
            out[...] = terms[distance * node_blks : (distance + 1) * node_blks]
        for out, distance in zip(sends, leaves(peers)):
            out[:node_blks] = terms[distance * node_blks : (distance + 1) * node_blks].astype(
                jnp.bfloat16
            )
        sends[-1][node_blks] = loss_parts


def last_hop(distance):
    return 2 if distance == 3 else distance & -distance


def children(distance, peers):
    return [k for k in range(1, peers) if k ^ last_hop(k) == distance]


def inner(peers):
    return [k for k in range(peers) if children(k, peers)]


def leaves(peers):
    return [k for k in range(peers) if not children(k, peers)]


def pair_sum(values):
    while len(values) > 1:
        values = [a + b for a, b in zip(values[::2], values[1::2])] + values[len(values) // 2 * 2 :]
    return values[0]


def fold_kernel(counts, with_loss, extras, after, *refs):
    inputs, refs = refs[: sum(counts) + len(counts)], refs[sum(counts) + len(counts) :]
    if with_loss:
        loss_ref, refs = refs[0], refs[1:]
    extra_in, refs = refs[:extras], refs[extras + after :]
    outs, extra_out = refs[: len(counts)], refs[len(counts) :]
    node_blks = inputs[0].shape[0]
    for number, (count, out_ref) in enumerate(zip(counts, outs)):
        kept_ref, arrived, inputs = inputs[0], inputs[1 : 1 + count], inputs[1 + count :]
        for block in range(node_blks):
            total = pair_sum([ref[block].astype(jnp.float32) for ref in arrived])
            out_ref[block] = (kept_ref[block] + total).astype(jnp.bfloat16)
        if with_loss and number == 0:
            both = from_parts(loss_ref[loss_ref.shape[0] - 1]) + from_parts(arrived[-1][node_blks])
            out_ref[node_blks] = to_parts(both, loss_ref.shape[1:])
    for source, target in zip(extra_in, extra_out):
        target[...] = source[...]


def next_level(level, risk_total, scen_total):
    level_new = level - primal_step * (1.0 - risk_total / scen_total)
    return level_new, 2.0 * level_new - level


def add_rows(values, shape):
    return jnp.broadcast_to(jnp.sum(values, axis=0, keepdims=True), shape)


def as_row(values):
    rows = values.shape[0]
    picked = lax.broadcasted_iota(jnp.int32, values.shape, 0) == lax.broadcasted_iota(
        jnp.int32, values.shape, 1
    )
    return jnp.sum(jnp.where(picked, values, 0.0), axis=0, keepdims=True)[:, :rows]


def settle_kernel(count, arc_total, scen_total, kind, *refs):
    kept_ref, arrived, refs = refs[0], refs[1 : 1 + count], refs[1 + count :]
    loss_ref, base_ref, risk_ref, excess_ref, level_ref, sum_ref, other_ref = refs[:7]
    duals_out, half_out, risk_out, excess_out, level_out, sum_out = refs[7:]
    node_blks, _, rows = base_ref.shape
    for block in range(node_blks):
        total = kept_ref[block] + pair_sum([ref[block].astype(jnp.float32) for ref in arrived])
        duals = base_ref[block] - dual_step * total
        if kind == "last":
            duals_out[:, block * rows : (block + 1) * rows] = duals
        else:
            duals_out[block] = duals
            half_out[block] = duals.astype(jnp.bfloat16)
    losses = from_parts(loss_ref[node_blks]) + from_parts(arrived[-1][node_blks])
    losses = losses / arc_total
    risk = risk_ref[...]
    excess = excess_ref[...]
    excess_new = jnp.maximum(excess - primal_step * (tail_weight - risk), 0.0)
    excess_bar = 2.0 * excess_new - excess
    risk_new = risk + risk_step * (losses - excess_bar)
    if kind == "early":
        risk_out[...] = risk_new
        excess_out[...] = excess_new
        return
    risk_total = sum_ref[...] + other_ref[...]
    level_new, level_bar = next_level(level_ref[...], risk_total, scen_total)
    risk_new = jnp.maximum(risk_new - risk_step * level_bar[:1], 0.0)
    if kind == "last":
        risk_out[...] = as_row(risk_new)
        excess_out[...] = as_row(excess_new)
        level_out[...] = level_new[:1, :1]
    else:
        risk_out[...] = risk_new
        excess_out[...] = excess_new
        level_out[...] = level_new
        sum_out[...] = add_rows(risk_new, sum_out.shape)


def local_forward_kernel(
    touches,
    group,
    steps,
    index_ref,
    bar_ref,
    blocks_ref,
    duals_ref,
    demand_ref,
    after_ref,
    out_ref,
    total,
):
    rows = blocks_ref.shape[-1]
    step = pl.program_id(0)
    first = step * group

    @pl.when(step == 0)
    def _():
        total[...] = jnp.zeros_like(total)

    for member in range(group):
        right = jnp.concatenate([blocks_ref[member, k] for k in range(touches)], axis=1)
        products = jnp.dot(
            bar_ref[:, member * rows : (member + 1) * rows],
            right,
            preferred_element_type=jnp.float32,
        )
        for k in range(touches):
            place = index_ref[k, first + member]
            total[place] += products[:, k * rows : (k + 1) * rows]

    @pl.when(step == steps - 1)
    def _():
        for block in range(total.shape[0]):
            demand = demand_ref[:, block * rows : (block + 1) * rows]
            out_ref[block] = duals_ref[block] + dual_step * (demand - total[block])


def whole(*shape):
    return pl.BlockSpec(shape, lambda i, *_: (0,) * len(shape))


def vmem_limit(peers):
    return (8 + peers + peers // 4) * MIB


def params(peers=8):
    return pltpu.CompilerParams(
        dimension_semantics=("arbitrary",), vmem_limit_bytes=vmem_limit(peers)
    )


def local_adjoint(index, panel, blocks):
    arc_blks, touches, rows, _ = blocks.shape
    scen_rows = panel.shape[1]
    group = GROUP
    return pl.pallas_call(
        functools.partial(local_adjoint_kernel, touches, group),
        out_shape=(
            jax.ShapeDtypeStruct((scen_rows, arc_blks * rows), jnp.float32),
            jax.ShapeDtypeStruct((8, rows), jnp.float32),
        ),
        grid_spec=pltpu.PrefetchScalarGridSpec(
            num_scalar_prefetch=1,
            grid=(arc_blks // group,),
            in_specs=[
                whole(*panel.shape),
                pl.BlockSpec((group, touches, rows, rows), lambda i, *_: (i, 0, 0, 0)),
            ],
            out_specs=(
                pl.BlockSpec((scen_rows, group * rows), lambda i, *_: (0, i)),
                whole(8, rows),
            ),
        ),
        compiler_params=params(),
        cost_estimate=pl.CostEstimate(
            flops=2 * scen_rows * blocks.size, bytes_accessed=2 * blocks.size, transcendentals=0
        ),
        name="local_adjoint",
    )(index, panel, blocks)


def head_step(places, panels, heads, pulled, flows, costs, risk, level, sums, late, scen_total):
    arc_blks, rows, _ = heads.shape
    scen_rows = flows.shape[0]
    peers = len(panels)
    node_blks = panels[0].shape[0]
    group = HEAD_GROUP
    steps = arc_blks // group
    kept = (node_blks, scen_rows, rows)
    sent = [kept] * (peers // 2)
    sent[-1] = (node_blks + 1, scen_rows, rows)
    arcs = pl.BlockSpec((scen_rows, group * rows), lambda i, *_: (0, i))
    results = pl.pallas_call(
        functools.partial(head_kernel, group, steps, peers, late, scen_total),
        out_shape=[
            jax.ShapeDtypeStruct(flows.shape, jnp.float32),
            jax.ShapeDtypeStruct(flows.shape, jnp.bfloat16),
            jax.ShapeDtypeStruct(risk.shape, jnp.float32),
            jax.ShapeDtypeStruct(level.shape, jnp.float32),
            jax.ShapeDtypeStruct(level.shape, jnp.float32),
        ]
        + [jax.ShapeDtypeStruct(kept, jnp.float32)] * (peers // 2)
        + [jax.ShapeDtypeStruct(shape, jnp.bfloat16) for shape in sent],
        grid_spec=pltpu.PrefetchScalarGridSpec(
            num_scalar_prefetch=1,
            grid=(steps,),
            in_specs=[whole(*panels[0].shape)] * peers
            + [
                pl.BlockSpec((group, rows, rows), lambda i, *_: (i, 0, 0)),
                arcs,
                arcs,
                pl.BlockSpec((1, group * rows), lambda i, *_: (0, i)),
                whole(scen_rows, rows),
                whole(*level.shape),
                whole(*level.shape),
                whole(*level.shape),
            ],
            out_specs=[arcs, arcs, whole(scen_rows, rows), whole(*level.shape), whole(*level.shape)]
            + [whole(*kept)] * (peers // 2)
            + [whole(*shape) for shape in sent],
            scratch_shapes=[
                pltpu.VMEM((peers * node_blks, scen_rows, rows), jnp.bfloat16),
                pltpu.VMEM((peers * node_blks, scen_rows, rows), jnp.float32),
                pltpu.VMEM((scen_rows, group * rows), jnp.float32),
                pltpu.VMEM((scen_rows, rows), jnp.float32),
            ],
        ),
        compiler_params=params(peers),
        cost_estimate=pl.CostEstimate(
            flops=4 * scen_rows * heads.size,
            bytes_accessed=2 * heads.size + 14 * flows.size + 4 * peers * panels[0].size,
            transcendentals=0,
        ),
        name="head_step",
    )(places, *panels, heads, pulled, flows, costs, risk, level, *sums)
    half = peers // 2
    kept = dict(zip(inner(peers), results[5 : 5 + half]))
    sends = dict(zip(leaves(peers), results[5 + half :]))
    return *results[:5], kept, sends


def small_cost(*arrays):
    size = sum(a.size for a in arrays)
    return pl.CostEstimate(flops=size, bytes_accessed=2 * size, transcendentals=0)


def fold(tops, loss, extras, after):
    node_blks, scen_rows, rows = tops[0][0].shape
    with_loss = loss is not None
    operands = [array for kept, arrived in tops for array in (kept, *arrived)]
    operands += ([loss] if with_loss else []) + list(extras)
    vmem = pl.BlockSpec(memory_space=pltpu.VMEM)
    out_shape = [
        jax.ShapeDtypeStruct((node_blks + (with_loss and number == 0), scen_rows, rows), jnp.bfloat16)
        for number in range(len(tops))
    ]
    out_shape += [jax.ShapeDtypeStruct(extra.shape, extra.dtype) for extra in extras]
    counts = [len(arrived) for _, arrived in tops]
    results = pl.pallas_call(
        functools.partial(fold_kernel, counts, with_loss, len(extras), len(after)),
        out_shape=out_shape,
        in_specs=[vmem] * len(operands) + [pl.BlockSpec(memory_space=pl.ANY)] * len(after),
        out_specs=[vmem] * len(out_shape),
        compiler_params=pltpu.CompilerParams(vmem_limit_bytes=vmem_limit(8)),
        cost_estimate=small_cost(*operands),
        name="fold",
    )(*operands, *after)
    return results[: len(tops)], results[len(tops) :]


def settle(kept, arrived, loss, base, risk, excess, level, sums, arc_total, scen_total, kind):
    node_blks, scen_rows, rows = base.shape
    last = kind == "last"
    return pl.pallas_call(
        functools.partial(settle_kernel, len(arrived), arc_total, scen_total, kind),
        out_shape=(
            jax.ShapeDtypeStruct((scen_rows, node_blks * rows) if last else base.shape, jnp.float32),
            jax.ShapeDtypeStruct(base.shape, jnp.bfloat16),
            jax.ShapeDtypeStruct((1, scen_rows) if last else risk.shape, jnp.float32),
            jax.ShapeDtypeStruct((1, scen_rows) if last else risk.shape, jnp.float32),
            jax.ShapeDtypeStruct((1, 1) if last else level.shape, jnp.float32),
            jax.ShapeDtypeStruct(level.shape, jnp.float32),
        ),
        compiler_params=pltpu.CompilerParams(vmem_limit_bytes=vmem_limit(8)),
        cost_estimate=small_cost(kept, *arrived, base),
        name="settle",
    )(kept, *arrived, loss, base, risk, excess, level, *sums)


def local_forward(index, bar, blocks, duals, demand, after):
    arc_blks, touches, rows, _ = blocks.shape
    scen_rows = bar.shape[0]
    group = GROUP
    steps = arc_blks // group
    return pl.pallas_call(
        functools.partial(local_forward_kernel, touches, group, steps),
        out_shape=jax.ShapeDtypeStruct(duals.shape, jnp.float32),
        grid_spec=pltpu.PrefetchScalarGridSpec(
            num_scalar_prefetch=1,
            grid=(steps,),
            in_specs=[
                pl.BlockSpec((scen_rows, group * rows), lambda i, *_: (0, i)),
                pl.BlockSpec((group, touches, rows, rows), lambda i, *_: (i, 0, 0, 0)),
                whole(*duals.shape),
                whole(*demand.shape),
                pl.BlockSpec(memory_space=pl.ANY),
            ],
            out_specs=whole(*duals.shape),
            scratch_shapes=[pltpu.VMEM(duals.shape, jnp.float32)],
        ),
        compiler_params=params(),
        cost_estimate=pl.CostEstimate(
            flops=2 * scen_rows * blocks.size, bytes_accessed=2 * blocks.size, transcendentals=0
        ),
        name="local_forward",
    )(index, bar, blocks, duals, demand, after)


def relay(arrived, risk_sum, after):
    def kernel(arrived_ref, sum_ref, *refs):
        arrived_out, sum_out = refs[-2:]
        arrived_out[...] = arrived_ref[...]
        sum_out[...] = sum_ref[...]

    vmem = pl.BlockSpec(memory_space=pltpu.VMEM)
    return pl.pallas_call(
        kernel,
        out_shape=(
            jax.ShapeDtypeStruct(arrived.shape, arrived.dtype),
            jax.ShapeDtypeStruct(risk_sum.shape, risk_sum.dtype),
        ),
        in_specs=[vmem, vmem] + [pl.BlockSpec(memory_space=pl.ANY)] * len(after),
        out_specs=(vmem, vmem),
        compiler_params=pltpu.CompilerParams(vmem_limit_bytes=vmem_limit(8)),
        cost_estimate=small_cost(arrived),
        name="relay",
    )(arrived, risk_sum, *after)


def prepare_kernel(risk_ref, excess_ref, level_ref, after, risk_out, excess_out, level_out, sum_out):
    scen_rows = risk_out.shape[0]
    square = (scen_rows, scen_rows)
    same = lax.broadcasted_iota(jnp.int32, square, 0) == lax.broadcasted_iota(jnp.int32, square, 1)
    for row_ref, out in ((risk_ref, risk_out), (excess_ref, excess_out)):
        column = jnp.sum(jnp.where(same, row_ref[...], 0.0), axis=1, keepdims=True)
        out[...] = jnp.broadcast_to(column, out.shape)
    level_out[...] = jnp.broadcast_to(level_ref[...], level_out.shape)
    sum_out[...] = add_rows(risk_out[...], sum_out.shape)


def prepare(risk, excess, level, rows, after):
    wide, flat = (risk.shape[0], rows), (8, rows)
    return pl.pallas_call(
        prepare_kernel,
        out_shape=[jax.ShapeDtypeStruct(shape, jnp.float32) for shape in (wide, wide, flat, flat)],
        in_specs=[pl.BlockSpec(memory_space=pltpu.VMEM)] * 3 + [pl.BlockSpec(memory_space=pl.ANY)],
        compiler_params=pltpu.CompilerParams(vmem_limit_bytes=vmem_limit(8)),
        cost_estimate=small_cost(risk),
        name="prepare",
    )(risk.reshape(1, -1), excess.reshape(1, -1), level.reshape(1, 1), after)


def swap(value, axis, distance):
    size = lax.axis_size(axis)
    return lax.ppermute(value, axis, [(i, i ^ distance) for i in range(size)])


def exchange_lowest(distance):
    return (distance & ~3) | ((distance & 1) << 1) | ((distance >> 1) & 1)


def swap_net(value, distance):
    net_size, scen_size = lax.axis_size("net"), lax.axis_size("scen")
    pairs = []
    for net in range(net_size):
        for scen in range(scen_size):
            hop = exchange_lowest(distance) if scen % 2 else distance
            pairs.append((net * scen_size + scen, (net ^ hop) * scen_size + scen))
    return lax.ppermute(value, ("net", "scen"), pairs)


def gather_panels(own, risk_sum, after):
    peers = lax.axis_size("net")
    panels = [own] + [None] * (peers - 1)
    order = sorted(range(1, peers), key=lambda k: (k.bit_count(), -k))
    for distance in order:
        hop = last_hop(distance)
        panels[distance] = swap_net(panels[distance ^ hop], hop)
        if distance == 1:
            far = peers // 2
            panels[far], risk_sum = relay(panels[far], risk_sum, after)
    return panels, risk_sum


def per_device(
    arc_flows,
    node_duals,
    demand,
    excess,
    risk_duals,
    threshold,
    arc_costs,
    local_blocks,
    head_blocks,
    local_index,
    head_index,
):
    rows = local_blocks.shape[-1]
    scen_rows = arc_flows.shape[0]
    node_blks = node_duals.shape[1] // rows
    net_size = lax.axis_size("net")
    arc_total = arc_flows.shape[1] * net_size
    scen_total = scen_rows * lax.axis_size("scen")
    costs = arc_costs.reshape(1, -1)
    touched = local_index.T
    distance = jnp.bitwise_xor(head_index // node_blks, lax.axis_index("net"))
    distance = jnp.where(lax.axis_index("scen") % 2 == 1, exchange_lowest(distance), distance)
    places = distance * node_blks + head_index % node_blks
    scen_size = lax.axis_size("scen")
    duals = node_duals.reshape(scen_rows, node_blks, rows).transpose(1, 0, 2)
    half = duals.astype(jnp.bfloat16)
    risk_sum = jnp.zeros((8, rows), jnp.float32)
    flows = arc_flows
    early = [1 << bit for bit in range(1, scen_size.bit_length() - 1)][::-1]
    zero = jnp.zeros_like(risk_sum)
    for iteration in range(ROUNDS):
        kind = "first" if iteration == 0 else "last" if iteration == ROUNDS - 1 else "early"
        pulled, token = local_adjoint(touched, half, local_blocks)
        panels, risk_sum = gather_panels(half, risk_sum, (token,))
        if kind == "first":
            risk, excess_now, level, risk_sum = prepare(
                risk_duals, excess, threshold, rows, panels[net_size // 2]
            )
        if kind == "early":
            for stride in early[:-1]:
                risk_sum = risk_sum + swap(risk_sum, "scen", stride)
            sums = (risk_sum, swap(risk_sum, "scen", early[-1]))
        else:
            sums = (risk_sum, swap(risk_sum, "scen", 1))
        flows, bar, risk, level, risk_sum, kept, sends = head_step(
            places,
            panels,
            head_blocks,
            pulled,
            flows,
            costs,
            risk,
            level,
            sums,
            kind == "last",
            scen_total,
        )
        after = ()
        if kind == "last":
            risk_sum = risk_sum + swap(risk_sum, "scen", 1)
            after = (risk_sum,)
        tops = sorted(inner(net_size), key=lambda k: (-k.bit_count(), -k))[:-1]
        groups = [(tops[0], 1)] + [(top,) for top in tops[1:] if top != 1]
        loss, loss_top = sends[net_size - 1], net_size - 1
        direct = swap_net(sends[2], 2)
        after += (direct,)
        for group in groups:
            terms = []
            for top in group:
                below = sorted(children(top, net_size))
                terms.append((kept[top], [swap_net(sends[k], last_hop(k)) for k in below]))
            chain = loss_top ^ last_hop(loss_top) == group[0]
            extras = (risk_sum,) if group[0] == net_size // 2 and kind != "early" else ()
            folded, passed = fold(terms, loss if chain else None, extras, after)
            sends.update(zip(group, folded))
            after = ()
            if chain:
                loss_top, loss = group[0], folded[0]
            if extras:
                (risk_sum,) = passed
        base = local_forward(touched, bar, local_blocks, duals, demand, loss)
        below = sorted(children(0, net_size))
        arrived = [direct if k == 2 else swap_net(sends[k], last_hop(k)) for k in below]
        sums = (risk_sum, zero)
        if kind != "early":
            for stride in early[:-1]:
                risk_sum = risk_sum + swap(risk_sum, "scen", stride)
            sums = (risk_sum, swap(risk_sum, "scen", early[-1]))
        duals, half, risk, excess_now, level_next, sum_next = settle(
            kept[0],
            arrived,
            loss,
            base,
            risk,
            excess_now,
            level,
            sums,
            arc_total,
            scen_total,
            kind,
        )
        if kind != "early":
            level, risk_sum = level_next, sum_next
    return (flows, duals, excess_now.reshape(-1), risk.reshape(-1), level.reshape(-1))


def solution(mesh):
    placed = (
        P("scen", "net"),
        P("scen", "net"),
        P("scen", "net"),
        P("scen"),
        P("scen"),
        P(),
        P("net"),
        P("net", None, None, None),
        P("net", None, None),
        P("net", None),
        P("net"),
    )
    return jax.shard_map(
        per_device,
        mesh=mesh,
        in_specs=placed,
        out_specs=(P("scen", "net"), P("scen", "net"), P("scen"), P("scen"), P()),
        check_vma=False,
    )
```

```python
import functools

import jax
import jax.numpy as jnp
from jax import lax
from jax.experimental import pallas as pl
from jax.experimental.pallas import tpu as pltpu
from jax.sharding import PartitionSpec as P

ROUNDS = 3

primal_step = 0.5
dual_step = 0.5
risk_step = 1.0
tail_weight = 2.0

MIB = 1024 * 1024
GROUP = 8
HEAD_GROUP = 16
SMALL_VMEM = 6 * MIB


def contract_last(left, right):
    return lax.dot_general(
        left, right, (((1,), (1,)), ((), ())), preferred_element_type=jnp.float32
    )


def local_adjoint_kernel(
    touches, group, index_ref, panel_ref, blocks_ref, out_ref, token_ref
):
    token_ref[...] = jnp.zeros_like(token_ref)
    rows = blocks_ref.shape[-1]
    first = pl.program_id(0) * group
    for member in range(group):
        left = jnp.concatenate(
            [panel_ref[index_ref[k, first + member]] for k in range(touches)], axis=1
        )
        right = jnp.concatenate([blocks_ref[member, k] for k in range(touches)], axis=1)
        out_ref[:, member * rows : (member + 1) * rows] = contract_last(left, right)


def to_parts(column, shape):
    high = column.astype(jnp.bfloat16).astype(jnp.float32)
    rest = column - high
    middle = rest.astype(jnp.bfloat16).astype(jnp.float32)
    low = rest - middle
    lane = lax.broadcasted_iota(jnp.int32, shape, 1)
    packed = jnp.where(
        lane == 0, high, jnp.where(lane == 1, middle, jnp.where(lane == 2, low, 0.0))
    )
    return packed.astype(jnp.bfloat16)


def from_parts(parts):
    return jnp.sum(parts.astype(jnp.float32), axis=1, keepdims=True)


def head_kernel(group, steps, peers, late, scen_total, index_ref, *refs):
    panels, refs = refs[:peers], refs[peers:]
    heads_ref, pulled_ref, flows_ref, costs_ref, risk_ref, level_ref, sum_ref, other_ref = refs[:8]
    flows_out, bar_out, risk_out, level_out, sum_out, refs = *refs[8:13], refs[13:]
    kept, refs = refs[: peers // 2], refs[peers // 2 :]
    sends, (panel, terms, pulled, loss) = refs[:-4], refs[-4:]
    rows = heads_ref.shape[-1]
    node_blks = panels[0].shape[0]
    step = pl.program_id(0)
    first = step * group

    @pl.when(step == 0)
    def _():
        terms[...] = jnp.zeros_like(terms)
        loss[...] = jnp.zeros_like(loss)
        risk_total = sum_ref[...] + other_ref[...]
        if late:
            level_new, level_bar = next_level(level_ref[...], risk_total, scen_total)
            risk_start = jnp.maximum(risk_ref[...] - risk_step * level_bar[:1], 0.0)
            risk_out[...] = risk_start
            level_out[...] = level_new
            sum_out[...] = add_rows(risk_start, sum_out.shape)
        else:
            risk_out[...] = risk_ref[...]
            level_out[...] = level_ref[...]
            sum_out[...] = risk_total
        for peer in range(peers):
            panel[peer * node_blks : (peer + 1) * node_blks] = panels[peer][...]

    places = [index_ref[first + member] for member in range(group)]
    spans = [slice(member * rows, (member + 1) * rows) for member in range(group)]
    for member in range(group):
        pulled[:, spans[member]] = contract_last(panel[places[member]], heads_ref[member])
    risk = risk_out[...]
    loss_sum = jnp.zeros_like(risk)
    for columns in spans:
        flows = flows_ref[:, columns]
        cost = costs_ref[:, columns]
        gradient = risk * cost - (pulled[:, columns] + pulled_ref[:, columns])
        flows_new = jnp.maximum(flows - primal_step * gradient, 0.0)
        bar = 2.0 * flows_new - flows
        flows_out[:, columns] = flows_new
        loss_sum += cost * bar
        bar_out[:, columns] = bar.astype(jnp.bfloat16)
    loss[...] += loss_sum
    products = [
        jnp.dot(bar_out[:, spans[m]], heads_ref[m], preferred_element_type=jnp.float32)
        for m in range(group)
    ]
    for member in range(group):
        terms[places[member]] += products[member]

    @pl.when(step == steps - 1)
    def _():
        loss_parts = to_parts(jnp.sum(loss[...], axis=1, keepdims=True), loss.shape)
        for out, distance in zip(kept, inner(peers)):
            out[...] = terms[distance * node_blks : (distance + 1) * node_blks]
        for out, distance in zip(sends, leaves(peers)):
            out[:node_blks] = terms[distance * node_blks : (distance + 1) * node_blks].astype(
                jnp.bfloat16
            )
        sends[-1][node_blks] = loss_parts


def last_hop(distance):
    return 2 if distance == 3 else distance & -distance


def children(distance, peers):
    return [k for k in range(1, peers) if k ^ last_hop(k) == distance]


def inner(peers):
    return [k for k in range(peers) if children(k, peers)]


def leaves(peers):
    return [k for k in range(peers) if not children(k, peers)]


def pair_sum(values):
    while len(values) > 1:
        values = [a + b for a, b in zip(values[::2], values[1::2])] + values[len(values) // 2 * 2 :]
    return values[0]


def fold_kernel(counts, with_loss, extras, after, *refs):
    inputs, refs = refs[: sum(counts) + len(counts)], refs[sum(counts) + len(counts) :]
    if with_loss:
        loss_ref, refs = refs[0], refs[1:]
    extra_in, refs = refs[:extras], refs[extras + after :]
    outs, extra_out = refs[: len(counts)], refs[len(counts) :]
    node_blks = inputs[0].shape[0]
    for number, (count, out_ref) in enumerate(zip(counts, outs)):
        kept_ref, arrived, inputs = inputs[0], inputs[1 : 1 + count], inputs[1 + count :]
        for block in range(node_blks):
            total = pair_sum([ref[block].astype(jnp.float32) for ref in arrived])
            out_ref[block] = (kept_ref[block] + total).astype(jnp.bfloat16)
        if with_loss and number == 0:
            both = from_parts(loss_ref[loss_ref.shape[0] - 1]) + from_parts(arrived[-1][node_blks])
            out_ref[node_blks] = to_parts(both, loss_ref.shape[1:])
    for source, target in zip(extra_in, extra_out):
        target[...] = source[...]


def next_level(level, risk_total, scen_total):
    level_new = level - primal_step * (1.0 - risk_total / scen_total)
    return level_new, 2.0 * level_new - level


def add_rows(values, shape):
    return jnp.broadcast_to(jnp.sum(values, axis=0, keepdims=True), shape)


def as_row(values):
    rows = values.shape[0]
    picked = lax.broadcasted_iota(jnp.int32, values.shape, 0) == lax.broadcasted_iota(
        jnp.int32, values.shape, 1
    )
    return jnp.sum(jnp.where(picked, values, 0.0), axis=0, keepdims=True)[:, :rows]


def settle_kernel(count, arc_total, scen_total, kind, *refs):
    kept_ref, arrived, refs = refs[0], refs[1 : 1 + count], refs[1 + count :]
    loss_ref, base_ref, risk_ref, excess_ref, level_ref, sum_ref, other_ref = refs[:7]
    duals_out, half_out, risk_out, excess_out, level_out, sum_out = refs[7:]
    node_blks, _, rows = base_ref.shape
    for block in range(node_blks):
        total = kept_ref[block] + pair_sum([ref[block].astype(jnp.float32) for ref in arrived])
        duals = base_ref[block] - dual_step * total
        if kind == "last":
            duals_out[:, block * rows : (block + 1) * rows] = duals
        else:
            duals_out[block] = duals
            half_out[block] = duals.astype(jnp.bfloat16)
    losses = from_parts(loss_ref[node_blks]) + from_parts(arrived[-1][node_blks])
    losses = losses / arc_total
    risk = risk_ref[...]
    excess = excess_ref[...]
    excess_new = jnp.maximum(excess - primal_step * (tail_weight - risk), 0.0)
    excess_bar = 2.0 * excess_new - excess
    risk_new = risk + risk_step * (losses - excess_bar)
    if kind == "early":
        risk_out[...] = risk_new
        excess_out[...] = excess_new
        return
    risk_total = sum_ref[...] + other_ref[...]
    level_new, level_bar = next_level(level_ref[...], risk_total, scen_total)
    risk_new = jnp.maximum(risk_new - risk_step * level_bar[:1], 0.0)
    if kind == "last":
        risk_out[...] = as_row(risk_new)
        excess_out[...] = as_row(excess_new)
        level_out[...] = level_new[:1, :1]
    else:
        risk_out[...] = risk_new
        excess_out[...] = excess_new
        level_out[...] = level_new
        sum_out[...] = add_rows(risk_new, sum_out.shape)


def local_forward_kernel(
    touches,
    group,
    steps,
    index_ref,
    bar_ref,
    blocks_ref,
    duals_ref,
    demand_ref,
    after_ref,
    out_ref,
    total,
):
    rows = blocks_ref.shape[-1]
    step = pl.program_id(0)
    first = step * group

    @pl.when(step == 0)
    def _():
        total[...] = jnp.zeros_like(total)

    for member in range(group):
        right = jnp.concatenate([blocks_ref[member, k] for k in range(touches)], axis=1)
        products = jnp.dot(
            bar_ref[:, member * rows : (member + 1) * rows],
            right,
            preferred_element_type=jnp.float32,
        )
        for k in range(touches):
            place = index_ref[k, first + member]
            total[place] += products[:, k * rows : (k + 1) * rows]

    @pl.when(step == steps - 1)
    def _():
        for block in range(total.shape[0]):
            demand = demand_ref[:, block * rows : (block + 1) * rows]
            out_ref[block] = duals_ref[block] + dual_step * (demand - total[block])


def whole(*shape):
    return pl.BlockSpec(shape, lambda i, *_: (0,) * len(shape))


def params(limit):
    return pltpu.CompilerParams(dimension_semantics=("arbitrary",), vmem_limit_bytes=limit)


def local_adjoint(index, panel, blocks):
    arc_blks, touches, rows, _ = blocks.shape
    scen_rows = panel.shape[1]
    group = GROUP
    return pl.pallas_call(
        functools.partial(local_adjoint_kernel, touches, group),
        out_shape=(
            jax.ShapeDtypeStruct((scen_rows, arc_blks * rows), jnp.float32),
            jax.ShapeDtypeStruct((8, rows), jnp.float32),
        ),
        grid_spec=pltpu.PrefetchScalarGridSpec(
            num_scalar_prefetch=1,
            grid=(arc_blks // group,),
            in_specs=[
                whole(*panel.shape),
                pl.BlockSpec((group, touches, rows, rows), lambda i, *_: (i, 0, 0, 0)),
            ],
            out_specs=(
                pl.BlockSpec((scen_rows, group * rows), lambda i, *_: (0, i)),
                whole(8, rows),
            ),
        ),
        compiler_params=params(SMALL_VMEM),
        cost_estimate=pl.CostEstimate(
            flops=2 * scen_rows * blocks.size, bytes_accessed=2 * blocks.size, transcendentals=0
        ),
        name="local_adjoint",
    )(index, panel, blocks)


def head_step(places, panels, heads, pulled, flows, costs, risk, level, sums, late, scen_total):
    arc_blks, rows, _ = heads.shape
    scen_rows = flows.shape[0]
    peers = len(panels)
    node_blks = panels[0].shape[0]
    group = HEAD_GROUP
    steps = arc_blks // group
    kept = (node_blks, scen_rows, rows)
    sent = [kept] * (peers // 2)
    sent[-1] = (node_blks + 1, scen_rows, rows)
    arcs = pl.BlockSpec((scen_rows, group * rows), lambda i, *_: (0, i))
    results = pl.pallas_call(
        functools.partial(head_kernel, group, steps, peers, late, scen_total),
        out_shape=[
            jax.ShapeDtypeStruct(flows.shape, jnp.float32),
            jax.ShapeDtypeStruct(flows.shape, jnp.bfloat16),
            jax.ShapeDtypeStruct(risk.shape, jnp.float32),
            jax.ShapeDtypeStruct(level.shape, jnp.float32),
            jax.ShapeDtypeStruct(level.shape, jnp.float32),
        ]
        + [jax.ShapeDtypeStruct(kept, jnp.float32)] * (peers // 2)
        + [jax.ShapeDtypeStruct(shape, jnp.bfloat16) for shape in sent],
        grid_spec=pltpu.PrefetchScalarGridSpec(
            num_scalar_prefetch=1,
            grid=(steps,),
            in_specs=[whole(*panels[0].shape)] * peers
            + [
                pl.BlockSpec((group, rows, rows), lambda i, *_: (i, 0, 0)),
                arcs,
                arcs,
                pl.BlockSpec((1, group * rows), lambda i, *_: (0, i)),
                whole(scen_rows, rows),
                whole(*level.shape),
                whole(*level.shape),
                whole(*level.shape),
            ],
            out_specs=[arcs, arcs, whole(scen_rows, rows), whole(*level.shape), whole(*level.shape)]
            + [whole(*kept)] * (peers // 2)
            + [whole(*shape) for shape in sent],
            scratch_shapes=[
                pltpu.VMEM((peers * node_blks, scen_rows, rows), jnp.bfloat16),
                pltpu.VMEM((peers * node_blks, scen_rows, rows), jnp.float32),
                pltpu.VMEM((scen_rows, group * rows), jnp.float32),
                pltpu.VMEM((scen_rows, rows), jnp.float32),
            ],
        ),
        compiler_params=params((4 + peers + peers // 4) * MIB),
        cost_estimate=pl.CostEstimate(
            flops=4 * scen_rows * heads.size,
            bytes_accessed=2 * heads.size + 14 * flows.size + 4 * peers * panels[0].size,
            transcendentals=0,
        ),
        name="head_step",
    )(places, *panels, heads, pulled, flows, costs, risk, level, *sums)
    half = peers // 2
    kept = dict(zip(inner(peers), results[5 : 5 + half]))
    sends = dict(zip(leaves(peers), results[5 + half :]))
    return *results[:5], kept, sends


def small_cost(*arrays):
    size = sum(a.size for a in arrays)
    return pl.CostEstimate(flops=size, bytes_accessed=2 * size, transcendentals=0)


def fold(tops, loss, extras, after):
    node_blks, scen_rows, rows = tops[0][0].shape
    with_loss = loss is not None
    operands = [array for kept, arrived in tops for array in (kept, *arrived)]
    operands += ([loss] if with_loss else []) + list(extras)
    vmem = pl.BlockSpec(memory_space=pltpu.VMEM)
    out_shape = [
        jax.ShapeDtypeStruct((node_blks + (with_loss and number == 0), scen_rows, rows), jnp.bfloat16)
        for number in range(len(tops))
    ]
    out_shape += [jax.ShapeDtypeStruct(extra.shape, extra.dtype) for extra in extras]
    counts = [len(arrived) for _, arrived in tops]
    results = pl.pallas_call(
        functools.partial(fold_kernel, counts, with_loss, len(extras), len(after)),
        out_shape=out_shape,
        in_specs=[vmem] * len(operands) + [pl.BlockSpec(memory_space=pl.ANY)] * len(after),
        out_specs=[vmem] * len(out_shape),
        compiler_params=pltpu.CompilerParams(vmem_limit_bytes=SMALL_VMEM),
        cost_estimate=small_cost(*operands),
        name="fold",
    )(*operands, *after)
    return results[: len(tops)], results[len(tops) :]


def settle(kept, arrived, loss, base, risk, excess, level, sums, arc_total, scen_total, kind):
    node_blks, scen_rows, rows = base.shape
    last = kind == "last"
    return pl.pallas_call(
        functools.partial(settle_kernel, len(arrived), arc_total, scen_total, kind),
        out_shape=(
            jax.ShapeDtypeStruct((scen_rows, node_blks * rows) if last else base.shape, jnp.float32),
            jax.ShapeDtypeStruct(base.shape, jnp.bfloat16),
            jax.ShapeDtypeStruct((1, scen_rows) if last else risk.shape, jnp.float32),
            jax.ShapeDtypeStruct((1, scen_rows) if last else risk.shape, jnp.float32),
            jax.ShapeDtypeStruct((1, 1) if last else level.shape, jnp.float32),
            jax.ShapeDtypeStruct(level.shape, jnp.float32),
        ),
        compiler_params=pltpu.CompilerParams(vmem_limit_bytes=SMALL_VMEM),
        cost_estimate=small_cost(kept, *arrived, base),
        name="settle",
    )(kept, *arrived, loss, base, risk, excess, level, *sums)


def local_forward(index, bar, blocks, duals, demand, after):
    arc_blks, touches, rows, _ = blocks.shape
    scen_rows = bar.shape[0]
    group = GROUP
    steps = arc_blks // group
    return pl.pallas_call(
        functools.partial(local_forward_kernel, touches, group, steps),
        out_shape=jax.ShapeDtypeStruct(duals.shape, jnp.float32),
        grid_spec=pltpu.PrefetchScalarGridSpec(
            num_scalar_prefetch=1,
            grid=(steps,),
            in_specs=[
                pl.BlockSpec((scen_rows, group * rows), lambda i, *_: (0, i)),
                pl.BlockSpec((group, touches, rows, rows), lambda i, *_: (i, 0, 0, 0)),
                whole(*duals.shape),
                whole(*demand.shape),
                pl.BlockSpec(memory_space=pl.ANY),
            ],
            out_specs=whole(*duals.shape),
            scratch_shapes=[pltpu.VMEM(duals.shape, jnp.float32)],
        ),
        compiler_params=params(SMALL_VMEM),
        cost_estimate=pl.CostEstimate(
            flops=2 * scen_rows * blocks.size, bytes_accessed=2 * blocks.size, transcendentals=0
        ),
        name="local_forward",
    )(index, bar, blocks, duals, demand, after)


def relay(arrived, risk_sum, after):
    def kernel(arrived_ref, sum_ref, *refs):
        arrived_out, sum_out = refs[-2:]
        arrived_out[...] = arrived_ref[...]
        sum_out[...] = sum_ref[...]

    vmem = pl.BlockSpec(memory_space=pltpu.VMEM)
    return pl.pallas_call(
        kernel,
        out_shape=(
            jax.ShapeDtypeStruct(arrived.shape, arrived.dtype),
            jax.ShapeDtypeStruct(risk_sum.shape, risk_sum.dtype),
        ),
        in_specs=[vmem, vmem] + [pl.BlockSpec(memory_space=pl.ANY)] * len(after),
        out_specs=(vmem, vmem),
        compiler_params=pltpu.CompilerParams(vmem_limit_bytes=SMALL_VMEM),
        cost_estimate=small_cost(arrived),
        name="relay",
    )(arrived, risk_sum, *after)


def prepare_kernel(risk_ref, excess_ref, level_ref, *refs):
    risk_out, excess_out, level_out, sum_out = refs[-4:]
    scen_rows = risk_out.shape[0]
    square = (scen_rows, scen_rows)
    same = lax.broadcasted_iota(jnp.int32, square, 0) == lax.broadcasted_iota(jnp.int32, square, 1)
    for row_ref, out in ((risk_ref, risk_out), (excess_ref, excess_out)):
        column = jnp.sum(jnp.where(same, row_ref[...], 0.0), axis=1, keepdims=True)
        out[...] = jnp.broadcast_to(column, out.shape)
    level_out[...] = jnp.broadcast_to(level_ref[...], level_out.shape)
    sum_out[...] = add_rows(risk_out[...], sum_out.shape)


def prepare(risk, excess, level, rows, after):
    wide, flat = (risk.shape[0], rows), (8, rows)
    return pl.pallas_call(
        prepare_kernel,
        out_shape=[jax.ShapeDtypeStruct(shape, jnp.float32) for shape in (wide, wide, flat, flat)],
        in_specs=[pl.BlockSpec(memory_space=pltpu.VMEM)] * 3
        + [pl.BlockSpec(memory_space=pl.ANY)] * len(after),
        compiler_params=pltpu.CompilerParams(vmem_limit_bytes=SMALL_VMEM),
        cost_estimate=small_cost(risk),
        name="prepare",
    )(risk.reshape(1, -1), excess.reshape(1, -1), level.reshape(1, 1), *after)


def swap(value, axis, distance):
    size = lax.axis_size(axis)
    return lax.ppermute(value, axis, [(i, i ^ distance) for i in range(size)])


def exchange_lowest(distance):
    return (distance & ~3) | ((distance & 1) << 1) | ((distance >> 1) & 1)


def swap_net(value, distance):
    net_size, scen_size = lax.axis_size("net"), lax.axis_size("scen")
    pairs = []
    for net in range(net_size):
        for scen in range(scen_size):
            hop = exchange_lowest(distance) if scen % 2 else distance
            pairs.append((net * scen_size + scen, (net ^ hop) * scen_size + scen))
    return lax.ppermute(value, ("net", "scen"), pairs)


def gather_panels(own, risk_sum, after):
    peers = lax.axis_size("net")
    panels = [own] + [None] * (peers - 1)
    order = sorted(range(1, peers), key=lambda k: (k.bit_count(), -k))
    for distance in order:
        hop = last_hop(distance)
        panels[distance] = swap_net(panels[distance ^ hop], hop)
        if distance == 1:
            far = peers // 2
            panels[far], risk_sum = relay(panels[far], risk_sum, after)
    return panels, risk_sum


def per_device(
    arc_flows,
    node_duals,
    demand,
    excess,
    risk_duals,
    threshold,
    arc_costs,
    local_blocks,
    head_blocks,
    local_index,
    head_index,
):
    rows = local_blocks.shape[-1]
    scen_rows = arc_flows.shape[0]
    node_blks = node_duals.shape[1] // rows
    net_size = lax.axis_size("net")
    arc_total = arc_flows.shape[1] * net_size
    scen_total = scen_rows * lax.axis_size("scen")
    costs = arc_costs.reshape(1, -1)
    touched = local_index.T
    distance = jnp.bitwise_xor(head_index // node_blks, lax.axis_index("net"))
    distance = jnp.where(lax.axis_index("scen") % 2 == 1, exchange_lowest(distance), distance)
    places = distance * node_blks + head_index % node_blks
    scen_size = lax.axis_size("scen")
    duals = node_duals.reshape(scen_rows, node_blks, rows).transpose(1, 0, 2)
    half = duals.astype(jnp.bfloat16)
    risk_sum = jnp.zeros((8, rows), jnp.float32)
    flows = arc_flows
    early = [1 << bit for bit in range(1, scen_size.bit_length() - 1)][::-1]
    zero = jnp.zeros_like(risk_sum)
    for iteration in range(ROUNDS):
        kind = "first" if iteration == 0 else "last" if iteration == ROUNDS - 1 else "early"
        pulled, token = local_adjoint(touched, half, local_blocks)
        panels, risk_sum = gather_panels(half, risk_sum, (token,))
        if kind == "first":
            risk, excess_now, level, risk_sum = prepare(
                risk_duals,
                excess,
                threshold,
                rows,
                (panels[net_size // 2], head_blocks, arc_flows),
            )
        if kind == "early":
            for stride in early[:-1]:
                risk_sum = risk_sum + swap(risk_sum, "scen", stride)
            sums = (risk_sum, swap(risk_sum, "scen", early[-1]))
        else:
            sums = (risk_sum, swap(risk_sum, "scen", 1))
        flows, bar, risk, level, risk_sum, kept, sends = head_step(
            places,
            panels,
            head_blocks,
            pulled,
            flows,
            costs,
            risk,
            level,
            sums,
            kind == "last",
            scen_total,
        )
        after = ()
        if kind == "last":
            risk_sum = risk_sum + swap(risk_sum, "scen", 1)
            after = (risk_sum,)
        tops = sorted(inner(net_size), key=lambda k: (-k.bit_count(), -k))[:-1]
        groups = [(top,) for top in tops if top != 1] + [(1,)]
        loss, loss_top = sends[net_size - 1], net_size - 1
        ahead = {5: swap_net(sends[5], last_hop(5))}
        after += (ahead[5],)
        for group in groups:
            terms = []
            for top in group:
                below = sorted(children(top, net_size))
                terms.append(
                    (
                        kept[top],
                        [ahead[k] if k in ahead else swap_net(sends[k], last_hop(k)) for k in below],
                    )
                )
            chain = loss_top ^ last_hop(loss_top) == group[0]
            extras = (risk_sum,) if group[0] == net_size // 2 and kind != "early" else ()
            folded, passed = fold(terms, loss if chain else None, extras, after)
            sends.update(zip(group, folded))
            after = ()
            if chain:
                loss_top, loss = group[0], folded[0]
            if extras:
                (risk_sum,) = passed
        base = local_forward(touched, bar, local_blocks, duals, demand, loss)
        below = sorted(children(0, net_size))
        arrived = [swap_net(sends[k], last_hop(k)) for k in below]
        sums = (risk_sum, zero)
        if kind != "early":
            for stride in early[:-1]:
                risk_sum = risk_sum + swap(risk_sum, "scen", stride)
            sums = (risk_sum, swap(risk_sum, "scen", early[-1]))
        duals, half, risk, excess_now, level_next, sum_next = settle(
            kept[0],
            arrived,
            loss,
            base,
            risk,
            excess_now,
            level,
            sums,
            arc_total,
            scen_total,
            kind,
        )
        if kind != "early":
            level, risk_sum = level_next, sum_next
    return (flows, duals, excess_now.reshape(-1), risk.reshape(-1), level.reshape(-1))


def solution(mesh):
    placed = (
        P("scen", "net"),
        P("scen", "net"),
        P("scen", "net"),
        P("scen"),
        P("scen"),
        P(),
        P("net"),
        P("net", None, None, None),
        P("net", None, None),
        P("net", None),
        P("net"),
    )
    return jax.shard_map(
        per_device,
        mesh=mesh,
        in_specs=placed,
        out_specs=(P("scen", "net"), P("scen", "net"), P("scen"), P("scen"), P()),
        check_vma=False,
    )
```

```python
import functools

import jax
import jax.numpy as jnp
from jax import lax
from jax.experimental import pallas as pl
from jax.experimental.pallas import tpu as pltpu
from jax.sharding import PartitionSpec as P

ROUNDS = 3

primal_step = 0.5
dual_step = 0.5
risk_step = 1.0
tail_weight = 2.0

MIB = 1024 * 1024
GROUP = 8
HEAD_GROUP = 16
SMALL_VMEM = 6 * MIB


def contract_last(left, right):
    return lax.dot_general(
        left, right, (((1,), (1,)), ((), ())), preferred_element_type=jnp.float32
    )


def local_adjoint_kernel(
    touches, group, index_ref, panel_ref, blocks_ref, out_ref, token_ref
):
    token_ref[...] = jnp.zeros_like(token_ref)
    rows = blocks_ref.shape[-1]
    first = pl.program_id(0) * group
    for member in range(group):
        left = jnp.concatenate(
            [panel_ref[index_ref[k, first + member]] for k in range(touches)], axis=1
        )
        right = jnp.concatenate([blocks_ref[member, k] for k in range(touches)], axis=1)
        out_ref[:, member * rows : (member + 1) * rows] = contract_last(left, right)


def to_parts(column, shape):
    high = column.astype(jnp.bfloat16).astype(jnp.float32)
    rest = column - high
    middle = rest.astype(jnp.bfloat16).astype(jnp.float32)
    low = rest - middle
    lane = lax.broadcasted_iota(jnp.int32, shape, 1)
    packed = jnp.where(
        lane == 0, high, jnp.where(lane == 1, middle, jnp.where(lane == 2, low, 0.0))
    )
    return packed.astype(jnp.bfloat16)


def from_parts(parts):
    return jnp.sum(parts.astype(jnp.float32), axis=1, keepdims=True)


def head_kernel(group, steps, peers, late, scen_total, index_ref, *refs):
    panels, refs = refs[:peers], refs[peers:]
    heads_ref, pulled_ref, flows_ref, costs_ref, risk_ref, level_ref, sum_ref, other_ref = refs[:8]
    flows_out, bar_out, risk_out, level_out, sum_out, refs = *refs[8:13], refs[13:]
    kept, refs = refs[: peers // 2], refs[peers // 2 :]
    sends, (panel, terms, pulled, loss) = refs[:-4], refs[-4:]
    rows = heads_ref.shape[-1]
    node_blks = panels[0].shape[0]
    step = pl.program_id(0)
    first = step * group

    @pl.when(step == 0)
    def _():
        terms[...] = jnp.zeros_like(terms)
        loss[...] = jnp.zeros_like(loss)
        risk_total = sum_ref[...] + other_ref[...]
        if late:
            level_new, level_bar = next_level(level_ref[...], risk_total, scen_total)
            risk_start = jnp.maximum(risk_ref[...] - risk_step * level_bar[:1], 0.0)
            risk_out[...] = risk_start
            level_out[...] = level_new
            sum_out[...] = add_rows(risk_start, sum_out.shape)
        else:
            risk_out[...] = risk_ref[...]
            level_out[...] = level_ref[...]
            sum_out[...] = risk_total
        for peer in range(peers):
            panel[peer * node_blks : (peer + 1) * node_blks] = panels[peer][...]

    places = [index_ref[first + member] for member in range(group)]
    spans = [slice(member * rows, (member + 1) * rows) for member in range(group)]
    for member in range(group):
        pulled[:, spans[member]] = contract_last(panel[places[member]], heads_ref[member])
    risk = risk_out[...]
    loss_sum = jnp.zeros_like(risk)
    for columns in spans:
        flows = flows_ref[:, columns]
        cost = costs_ref[:, columns]
        gradient = risk * cost - (pulled[:, columns] + pulled_ref[:, columns])
        flows_new = jnp.maximum(flows - primal_step * gradient, 0.0)
        bar = 2.0 * flows_new - flows
        flows_out[:, columns] = flows_new
        loss_sum += cost * bar
        bar_out[:, columns] = bar.astype(jnp.bfloat16)
    loss[...] += loss_sum
    products = [
        jnp.dot(bar_out[:, spans[m]], heads_ref[m], preferred_element_type=jnp.float32)
        for m in range(group)
    ]
    for member in range(group):
        terms[places[member]] += products[member]

    @pl.when(step == steps - 1)
    def _():
        loss_parts = to_parts(jnp.sum(loss[...], axis=1, keepdims=True), loss.shape)
        for out, distance in zip(kept, inner(peers)):
            out[...] = terms[distance * node_blks : (distance + 1) * node_blks]
        for out, distance in zip(sends, leaves(peers)):
            out[:node_blks] = terms[distance * node_blks : (distance + 1) * node_blks].astype(
                jnp.bfloat16
            )
        sends[-1][node_blks] = loss_parts


def last_hop(distance):
    return 2 if distance == 3 else distance & -distance


def children(distance, peers):
    return [k for k in range(1, peers) if k ^ last_hop(k) == distance]


def inner(peers):
    return [k for k in range(peers) if children(k, peers)]


def leaves(peers):
    return [k for k in range(peers) if not children(k, peers)]


def pair_sum(values):
    while len(values) > 1:
        values = [a + b for a, b in zip(values[::2], values[1::2])] + values[len(values) // 2 * 2 :]
    return values[0]


def fold_kernel(counts, with_loss, sums, after, *refs):
    inputs, refs = refs[: sum(counts) + len(counts)], refs[sum(counts) + len(counts) :]
    if with_loss:
        loss_ref, refs = refs[0], refs[1:]
    sum_in, refs = refs[:sums], refs[sums + after :]
    outs, sum_out = refs[: len(counts)], refs[len(counts) :]
    node_blks = inputs[0].shape[0]
    for number, (count, out_ref) in enumerate(zip(counts, outs)):
        kept_ref, arrived, inputs = inputs[0], inputs[1 : 1 + count], inputs[1 + count :]
        for block in range(node_blks):
            total = pair_sum([ref[block].astype(jnp.float32) for ref in arrived])
            out_ref[block] = (kept_ref[block] + total).astype(jnp.bfloat16)
        if with_loss and number == 0:
            both = from_parts(loss_ref[loss_ref.shape[0] - 1]) + from_parts(arrived[-1][node_blks])
            out_ref[node_blks] = to_parts(both, loss_ref.shape[1:])
    for out in sum_out:
        out[...] = functools.reduce(jnp.add, [ref[...] for ref in sum_in])


def next_level(level, risk_total, scen_total):
    level_new = level - primal_step * (1.0 - risk_total / scen_total)
    return level_new, 2.0 * level_new - level


def add_rows(values, shape):
    return jnp.broadcast_to(jnp.sum(values, axis=0, keepdims=True), shape)


def as_row(values):
    rows = values.shape[0]
    picked = lax.broadcasted_iota(jnp.int32, values.shape, 0) == lax.broadcasted_iota(
        jnp.int32, values.shape, 1
    )
    return jnp.sum(jnp.where(picked, values, 0.0), axis=0, keepdims=True)[:, :rows]


def settle_kernel(count, arc_total, scen_total, kind, *refs):
    kept_ref, arrived, refs = refs[0], refs[1 : 1 + count], refs[1 + count :]
    loss_ref, base_ref, risk_ref, excess_ref, level_ref, sum_ref, other_ref = refs[:7]
    duals_out, half_out, risk_out, excess_out, level_out, sum_out = refs[7:]
    node_blks, _, rows = base_ref.shape
    for block in range(node_blks):
        total = kept_ref[block] + pair_sum([ref[block].astype(jnp.float32) for ref in arrived])
        duals = base_ref[block] - dual_step * total
        if kind == "last":
            duals_out[:, block * rows : (block + 1) * rows] = duals
        else:
            duals_out[block] = duals
            half_out[block] = duals.astype(jnp.bfloat16)
    losses = from_parts(loss_ref[node_blks]) + from_parts(arrived[-1][node_blks])
    losses = losses / arc_total
    risk = risk_ref[...]
    excess = excess_ref[...]
    excess_new = jnp.maximum(excess - primal_step * (tail_weight - risk), 0.0)
    excess_bar = 2.0 * excess_new - excess
    risk_new = risk + risk_step * (losses - excess_bar)
    if kind == "early":
        risk_out[...] = risk_new
        excess_out[...] = excess_new
        return
    risk_total = sum_ref[...] + other_ref[...]
    level_new, level_bar = next_level(level_ref[...], risk_total, scen_total)
    risk_new = jnp.maximum(risk_new - risk_step * level_bar[:1], 0.0)
    if kind == "last":
        risk_out[...] = as_row(risk_new)
        excess_out[...] = as_row(excess_new)
        level_out[...] = level_new[:1, :1]
    else:
        risk_out[...] = risk_new
        excess_out[...] = excess_new
        level_out[...] = level_new
        sum_out[...] = add_rows(risk_new, sum_out.shape)


def local_forward_kernel(
    touches,
    group,
    steps,
    index_ref,
    bar_ref,
    blocks_ref,
    duals_ref,
    demand_ref,
    after_ref,
    out_ref,
    total,
):
    rows = blocks_ref.shape[-1]
    step = pl.program_id(0)
    first = step * group

    @pl.when(step == 0)
    def _():
        total[...] = jnp.zeros_like(total)

    for member in range(group):
        right = jnp.concatenate([blocks_ref[member, k] for k in range(touches)], axis=1)
        products = jnp.dot(
            bar_ref[:, member * rows : (member + 1) * rows],
            right,
            preferred_element_type=jnp.float32,
        )
        for k in range(touches):
            place = index_ref[k, first + member]
            total[place] += products[:, k * rows : (k + 1) * rows]

    @pl.when(step == steps - 1)
    def _():
        for block in range(total.shape[0]):
            demand = demand_ref[:, block * rows : (block + 1) * rows]
            out_ref[block] = duals_ref[block] + dual_step * (demand - total[block])


def whole(*shape):
    return pl.BlockSpec(shape, lambda i, *_: (0,) * len(shape))


def params(limit):
    return pltpu.CompilerParams(dimension_semantics=("arbitrary",), vmem_limit_bytes=limit)


def local_adjoint(index, panel, blocks):
    arc_blks, touches, rows, _ = blocks.shape
    scen_rows = panel.shape[1]
    group = GROUP
    return pl.pallas_call(
        functools.partial(local_adjoint_kernel, touches, group),
        out_shape=(
            jax.ShapeDtypeStruct((scen_rows, arc_blks * rows), jnp.float32),
            jax.ShapeDtypeStruct((8, rows), jnp.float32),
        ),
        grid_spec=pltpu.PrefetchScalarGridSpec(
            num_scalar_prefetch=1,
            grid=(arc_blks // group,),
            in_specs=[
                whole(*panel.shape),
                pl.BlockSpec((group, touches, rows, rows), lambda i, *_: (i, 0, 0, 0)),
            ],
            out_specs=(
                pl.BlockSpec((scen_rows, group * rows), lambda i, *_: (0, i)),
                whole(8, rows),
            ),
        ),
        compiler_params=params(SMALL_VMEM),
        cost_estimate=pl.CostEstimate(
            flops=2 * scen_rows * blocks.size, bytes_accessed=2 * blocks.size, transcendentals=0
        ),
        name="local_adjoint",
    )(index, panel, blocks)


def head_step(places, panels, heads, pulled, flows, costs, risk, level, sums, late, scen_total):
    arc_blks, rows, _ = heads.shape
    scen_rows = flows.shape[0]
    peers = len(panels)
    node_blks = panels[0].shape[0]
    group = HEAD_GROUP
    steps = arc_blks // group
    kept = (node_blks, scen_rows, rows)
    sent = [kept] * (peers // 2)
    sent[-1] = (node_blks + 1, scen_rows, rows)
    arcs = pl.BlockSpec((scen_rows, group * rows), lambda i, *_: (0, i))
    results = pl.pallas_call(
        functools.partial(head_kernel, group, steps, peers, late, scen_total),
        out_shape=[
            jax.ShapeDtypeStruct(flows.shape, jnp.float32),
            jax.ShapeDtypeStruct(flows.shape, jnp.bfloat16),
            jax.ShapeDtypeStruct(risk.shape, jnp.float32),
            jax.ShapeDtypeStruct(level.shape, jnp.float32),
            jax.ShapeDtypeStruct(level.shape, jnp.float32),
        ]
        + [jax.ShapeDtypeStruct(kept, jnp.float32)] * (peers // 2)
        + [jax.ShapeDtypeStruct(shape, jnp.bfloat16) for shape in sent],
        grid_spec=pltpu.PrefetchScalarGridSpec(
            num_scalar_prefetch=1,
            grid=(steps,),
            in_specs=[whole(*panels[0].shape)] * peers
            + [
                pl.BlockSpec((group, rows, rows), lambda i, *_: (i, 0, 0)),
                arcs,
                arcs,
                pl.BlockSpec((1, group * rows), lambda i, *_: (0, i)),
                whole(scen_rows, rows),
                whole(*level.shape),
                whole(*level.shape),
                whole(*level.shape),
            ],
            out_specs=[arcs, arcs, whole(scen_rows, rows), whole(*level.shape), whole(*level.shape)]
            + [whole(*kept)] * (peers // 2)
            + [whole(*shape) for shape in sent],
            scratch_shapes=[
                pltpu.VMEM((peers * node_blks, scen_rows, rows), jnp.bfloat16),
                pltpu.VMEM((peers * node_blks, scen_rows, rows), jnp.float32),
                pltpu.VMEM((scen_rows, group * rows), jnp.float32),
                pltpu.VMEM((scen_rows, rows), jnp.float32),
            ],
        ),
        compiler_params=params((4 + peers + peers // 4) * MIB),
        cost_estimate=pl.CostEstimate(
            flops=4 * scen_rows * heads.size,
            bytes_accessed=2 * heads.size + 14 * flows.size + 4 * peers * panels[0].size,
            transcendentals=0,
        ),
        name="head_step",
    )(places, *panels, heads, pulled, flows, costs, risk, level, *sums)
    half = peers // 2
    kept = dict(zip(inner(peers), results[5 : 5 + half]))
    sends = dict(zip(leaves(peers), results[5 + half :]))
    return *results[:5], kept, sends


def small_cost(*arrays):
    size = sum(a.size for a in arrays)
    return pl.CostEstimate(flops=size, bytes_accessed=2 * size, transcendentals=0)


def fold(tops, loss, sums, after):
    node_blks, scen_rows, rows = tops[0][0].shape
    with_loss = loss is not None
    operands = [array for kept, arrived in tops for array in (kept, *arrived)]
    operands += ([loss] if with_loss else []) + list(sums)
    vmem = pl.BlockSpec(memory_space=pltpu.VMEM)
    out_shape = [
        jax.ShapeDtypeStruct((node_blks + (with_loss and number == 0), scen_rows, rows), jnp.bfloat16)
        for number in range(len(tops))
    ]
    out_shape += [jax.ShapeDtypeStruct(array.shape, array.dtype) for array in sums[:1]]
    counts = [len(arrived) for _, arrived in tops]
    results = pl.pallas_call(
        functools.partial(fold_kernel, counts, with_loss, len(sums), len(after)),
        out_shape=out_shape,
        in_specs=[vmem] * len(operands) + [pl.BlockSpec(memory_space=pl.ANY)] * len(after),
        out_specs=[vmem] * len(out_shape),
        compiler_params=pltpu.CompilerParams(vmem_limit_bytes=SMALL_VMEM),
        cost_estimate=small_cost(*operands),
        name="fold",
    )(*operands, *after)
    return results[: len(tops)], results[len(tops) :]


def settle(kept, arrived, loss, base, risk, excess, level, sums, arc_total, scen_total, kind):
    node_blks, scen_rows, rows = base.shape
    last = kind == "last"
    return pl.pallas_call(
        functools.partial(settle_kernel, len(arrived), arc_total, scen_total, kind),
        out_shape=(
            jax.ShapeDtypeStruct((scen_rows, node_blks * rows) if last else base.shape, jnp.float32),
            jax.ShapeDtypeStruct(base.shape, jnp.bfloat16),
            jax.ShapeDtypeStruct((1, scen_rows) if last else risk.shape, jnp.float32),
            jax.ShapeDtypeStruct((1, scen_rows) if last else risk.shape, jnp.float32),
            jax.ShapeDtypeStruct((1, 1) if last else level.shape, jnp.float32),
            jax.ShapeDtypeStruct(level.shape, jnp.float32),
        ),
        compiler_params=pltpu.CompilerParams(vmem_limit_bytes=SMALL_VMEM),
        cost_estimate=small_cost(kept, *arrived, base),
        name="settle",
    )(kept, *arrived, loss, base, risk, excess, level, *sums)


def local_forward(index, bar, blocks, duals, demand, after):
    arc_blks, touches, rows, _ = blocks.shape
    scen_rows = bar.shape[0]
    group = GROUP
    steps = arc_blks // group
    return pl.pallas_call(
        functools.partial(local_forward_kernel, touches, group, steps),
        out_shape=jax.ShapeDtypeStruct(duals.shape, jnp.float32),
        grid_spec=pltpu.PrefetchScalarGridSpec(
            num_scalar_prefetch=1,
            grid=(steps,),
            in_specs=[
                pl.BlockSpec((scen_rows, group * rows), lambda i, *_: (0, i)),
                pl.BlockSpec((group, touches, rows, rows), lambda i, *_: (i, 0, 0, 0)),
                whole(*duals.shape),
                whole(*demand.shape),
                pl.BlockSpec(memory_space=pl.ANY),
            ],
            out_specs=whole(*duals.shape),
            scratch_shapes=[pltpu.VMEM(duals.shape, jnp.float32)],
        ),
        compiler_params=params(SMALL_VMEM),
        cost_estimate=pl.CostEstimate(
            flops=2 * scen_rows * blocks.size, bytes_accessed=2 * blocks.size, transcendentals=0
        ),
        name="local_forward",
    )(index, bar, blocks, duals, demand, after)


def relay(arrived, risk_sum, after):
    def kernel(arrived_ref, sum_ref, *refs):
        arrived_out, sum_out = refs[-2:]
        arrived_out[...] = arrived_ref[...]
        sum_out[...] = sum_ref[...]

    vmem = pl.BlockSpec(memory_space=pltpu.VMEM)
    return pl.pallas_call(
        kernel,
        out_shape=(
            jax.ShapeDtypeStruct(arrived.shape, arrived.dtype),
            jax.ShapeDtypeStruct(risk_sum.shape, risk_sum.dtype),
        ),
        in_specs=[vmem, vmem] + [pl.BlockSpec(memory_space=pl.ANY)] * len(after),
        out_specs=(vmem, vmem),
        compiler_params=pltpu.CompilerParams(vmem_limit_bytes=SMALL_VMEM),
        cost_estimate=small_cost(arrived),
        name="relay",
    )(arrived, risk_sum, *after)


def prepare_kernel(node_blks, risk_ref, excess_ref, level_ref, head_ref, *refs):
    risk_out, excess_out, level_out, sum_out, places_out = refs[-5:]
    head = head_ref[...]
    owner = lax.div(head, node_blks)
    distance = jnp.bitwise_xor(owner, lax.axis_index("net"))
    places_out[...] = head + (distance - owner) * node_blks
    scen_rows = risk_out.shape[0]
    square = (scen_rows, scen_rows)
    same = lax.broadcasted_iota(jnp.int32, square, 0) == lax.broadcasted_iota(jnp.int32, square, 1)
    for row_ref, out in ((risk_ref, risk_out), (excess_ref, excess_out)):
        column = jnp.sum(jnp.where(same, row_ref[...], 0.0), axis=1, keepdims=True)
        out[...] = jnp.broadcast_to(column, out.shape)
    level_out[...] = jnp.broadcast_to(level_ref[...], level_out.shape)
    sum_out[...] = add_rows(risk_out[...], sum_out.shape)


def prepare(risk, excess, level, heads, rows, node_blks, after):
    wide, flat = (risk.shape[0], rows), (8, rows)
    return pl.pallas_call(
        functools.partial(prepare_kernel, node_blks),
        out_shape=[jax.ShapeDtypeStruct(shape, jnp.float32) for shape in (wide, wide, flat, flat)]
        + [jax.ShapeDtypeStruct((1, heads.shape[0]), jnp.int32)],
        in_specs=[pl.BlockSpec(memory_space=pltpu.VMEM)] * 4
        + [pl.BlockSpec(memory_space=pl.ANY)] * len(after),
        compiler_params=pltpu.CompilerParams(vmem_limit_bytes=SMALL_VMEM),
        cost_estimate=small_cost(risk),
        name="prepare",
    )(risk.reshape(1, -1), excess.reshape(1, -1), level.reshape(1, 1), heads.reshape(1, -1), *after)


def swap(value, axis, distance):
    size = lax.axis_size(axis)
    return lax.ppermute(value, axis, [(i, i ^ distance) for i in range(size)])


def gather_panels(own, risk_sum, after):
    peers = lax.axis_size("net")
    panels = [own] + [None] * (peers - 1)
    order = sorted(range(1, peers), key=lambda k: (k.bit_count(), -k))
    for distance in order:
        hop = last_hop(distance)
        panels[distance] = swap(panels[distance ^ hop], "net", hop)
        if distance == 1:
            far = peers // 2
            panels[far], risk_sum = relay(panels[far], risk_sum, after)
    return panels, risk_sum


def per_device(
    arc_flows,
    node_duals,
    demand,
    excess,
    risk_duals,
    threshold,
    arc_costs,
    local_blocks,
    head_blocks,
    local_index,
    head_index,
):
    rows = local_blocks.shape[-1]
    scen_rows = arc_flows.shape[0]
    node_blks = node_duals.shape[1] // rows
    net_size = lax.axis_size("net")
    arc_total = arc_flows.shape[1] * net_size
    scen_total = scen_rows * lax.axis_size("scen")
    costs = arc_costs.reshape(1, -1)
    touched = local_index.T
    scen_size = lax.axis_size("scen")
    duals = node_duals.reshape(scen_rows, node_blks, rows).transpose(1, 0, 2)
    half = duals.astype(jnp.bfloat16)
    flows = arc_flows
    early = [1 << bit for bit in range(1, scen_size.bit_length() - 1)][::-1]
    for iteration in range(ROUNDS):
        kind = "first" if iteration == 0 else "last" if iteration == ROUNDS - 1 else "early"
        pulled, token = local_adjoint(touched, half, local_blocks)
        panels, risk_sum = gather_panels(half, token if kind == "first" else risk_sum, (token,))
        if kind == "first":
            risk, excess_now, level, risk_sum, places = prepare(
                risk_duals,
                excess,
                threshold,
                head_index,
                rows,
                node_blks,
                (panels[net_size // 2], head_blocks, arc_flows),
            )
            places = places.reshape(-1)
        if kind == "early":
            for stride in early[:-1]:
                risk_sum = risk_sum + swap(risk_sum, "scen", stride)
            sums = (risk_sum, swap(risk_sum, "scen", early[-1]))
        else:
            sums = (risk_sum, swap(risk_sum, "scen", 1))
        flows, bar, risk, level, risk_sum, kept, sends = head_step(
            places,
            panels,
            head_blocks,
            pulled,
            flows,
            costs,
            risk,
            level,
            sums,
            kind == "last",
            scen_total,
        )
        after = ()
        risk_sums = () if kind == "early" else (risk_sum,)
        if kind == "last":
            after = (swap(risk_sum, "scen", 1),)
            risk_sums += after
        tops = sorted(inner(net_size), key=lambda k: (-k.bit_count(), -k))[:-1]
        groups = [(top,) for top in tops if top != 1] + [(1,)]
        loss, loss_top = sends[net_size - 1], net_size - 1
        ahead = {5: swap(sends[5], "net", last_hop(5))}
        after += (ahead[5],)
        for group in groups:
            terms = []
            for top in group:
                below = sorted(children(top, net_size))
                terms.append(
                    (
                        kept[top],
                        [ahead[k] if k in ahead else swap(sends[k], "net", last_hop(k)) for k in below],
                    )
                )
            chain = loss_top ^ last_hop(loss_top) == group[0]
            sums = risk_sums if group[0] == net_size // 2 else ()
            if group == (1,):
                after = (loss,)
            folded, passed = fold(terms, loss if chain else None, sums, after)
            sends.update(zip(group, folded))
            after = ()
            if chain:
                loss_top, loss = group[0], folded[0]
            if sums:
                (risk_sum,) = passed
        base = local_forward(touched, bar, local_blocks, duals, demand, loss)
        below = sorted(children(0, net_size))
        arrived = [swap(sends[k], "net", last_hop(k)) for k in below]
        sums = (risk_sum, risk_sum)
        if kind != "early":
            for stride in early[:-1]:
                risk_sum = risk_sum + swap(risk_sum, "scen", stride)
            sums = (risk_sum, swap(risk_sum, "scen", early[-1]))
        duals, half, risk, excess_now, level_next, sum_next = settle(
            kept[0],
            arrived,
            loss,
            base,
            risk,
            excess_now,
            level,
            sums,
            arc_total,
            scen_total,
            kind,
        )
        if kind != "early":
            level, risk_sum = level_next, sum_next
    return (flows, duals, excess_now.reshape(-1), risk.reshape(-1), level.reshape(-1))


def solution(mesh):
    placed = (
        P("scen", "net"),
        P("scen", "net"),
        P("scen", "net"),
        P("scen"),
        P("scen"),
        P(),
        P("net"),
        P("net", None, None, None),
        P("net", None, None),
        P("net", None),
        P("net"),
    )
    return jax.shard_map(
        per_device,
        mesh=mesh,
        in_specs=placed,
        out_specs=(P("scen", "net"), P("scen", "net"), P("scen"), P("scen"), P()),
        check_vma=False,
    )
```

```python
import functools

import jax
import jax.numpy as jnp
from jax import lax
from jax.experimental import pallas as pl
from jax.experimental.pallas import tpu as pltpu
from jax.sharding import PartitionSpec as P

ROUNDS = 3

primal_step = 0.5
dual_step = 0.5
risk_step = 1.0
tail_weight = 2.0

MIB = 1024 * 1024
GROUP = 8
HEAD_GROUP = 16
SMALL_VMEM = 6 * MIB


def contract_last(left, right):
    return lax.dot_general(
        left, right, (((1,), (1,)), ((), ())), preferred_element_type=jnp.float32
    )


def local_adjoint_kernel(
    touches, group, index_ref, panel_ref, blocks_ref, out_ref, token_ref
):
    token_ref[...] = jnp.zeros_like(token_ref)
    rows = blocks_ref.shape[-1]
    first = pl.program_id(0) * group
    for member in range(group):
        left = jnp.concatenate(
            [panel_ref[index_ref[k, first + member]] for k in range(touches)], axis=1
        )
        right = jnp.concatenate([blocks_ref[member, k] for k in range(touches)], axis=1)
        out_ref[:, member * rows : (member + 1) * rows] = contract_last(left, right)


def to_parts(column, shape):
    high = column.astype(jnp.bfloat16).astype(jnp.float32)
    rest = column - high
    middle = rest.astype(jnp.bfloat16).astype(jnp.float32)
    low = rest - middle
    lane = lax.broadcasted_iota(jnp.int32, shape, 1)
    packed = jnp.where(
        lane == 0, high, jnp.where(lane == 1, middle, jnp.where(lane == 2, low, 0.0))
    )
    return packed.astype(jnp.bfloat16)


def from_parts(parts):
    return jnp.sum(parts.astype(jnp.float32), axis=1, keepdims=True)


def head_kernel(group, steps, peers, index_ref, *refs):
    panels, refs = refs[:peers], refs[peers:]
    heads_ref, pulled_ref, flows_ref, costs_ref, risk_ref, sum_ref, other_ref = refs[:7]
    flows_out, bar_out, sum_out, refs = *refs[7:10], refs[10:]
    kept, refs = refs[: peers // 2], refs[peers // 2 :]
    sends, (panel, terms, pulled, loss) = refs[:-4], refs[-4:]
    rows = heads_ref.shape[-1]
    node_blks = panels[0].shape[0]
    step = pl.program_id(0)
    first = step * group

    @pl.when(step == 0)
    def _():
        terms[...] = jnp.zeros_like(terms)
        loss[...] = jnp.zeros_like(loss)
        sum_out[...] = sum_ref[...] + other_ref[...]
        for peer in range(peers):
            panel[peer * node_blks : (peer + 1) * node_blks] = panels[peer][...]

    places = [index_ref[first + member] for member in range(group)]
    spans = [slice(member * rows, (member + 1) * rows) for member in range(group)]
    for member in range(group):
        pulled[:, spans[member]] = contract_last(panel[places[member]], heads_ref[member])
    risk = risk_ref[...]
    loss_sum = jnp.zeros_like(risk)
    for columns in spans:
        flows = flows_ref[:, columns]
        cost = costs_ref[:, columns]
        gradient = risk * cost - (pulled[:, columns] + pulled_ref[:, columns])
        flows_new = jnp.maximum(flows - primal_step * gradient, 0.0)
        bar = 2.0 * flows_new - flows
        flows_out[:, columns] = flows_new
        loss_sum += cost * bar
        bar_out[:, columns] = bar.astype(jnp.bfloat16)
    loss[...] += loss_sum
    products = [
        jnp.dot(bar_out[:, spans[m]], heads_ref[m], preferred_element_type=jnp.float32)
        for m in range(group)
    ]
    for member in range(group):
        terms[places[member]] += products[member]

    @pl.when(step == steps - 1)
    def _():
        loss_parts = to_parts(jnp.sum(loss[...], axis=1, keepdims=True), loss.shape)
        for out, distance in zip(kept, inner(peers)):
            out[...] = terms[distance * node_blks : (distance + 1) * node_blks]
        for out, distance in zip(sends, leaves(peers)):
            out[:node_blks] = terms[distance * node_blks : (distance + 1) * node_blks].astype(
                jnp.bfloat16
            )
        sends[-1][node_blks] = loss_parts


def last_hop(distance):
    return 2 if distance == 3 else distance & -distance


def children(distance, peers):
    return [k for k in range(1, peers) if k ^ last_hop(k) == distance]


def inner(peers):
    return [k for k in range(peers) if children(k, peers)]


def leaves(peers):
    return [k for k in range(peers) if not children(k, peers)]


def pair_sum(values):
    while len(values) > 1:
        values = [a + b for a, b in zip(values[::2], values[1::2])] + values[len(values) // 2 * 2 :]
    return values[0]


def fold_kernel(counts, with_loss, sums, after, *refs):
    inputs, refs = refs[: sum(counts) + len(counts)], refs[sum(counts) + len(counts) :]
    if with_loss:
        loss_ref, refs = refs[0], refs[1:]
    sum_in, refs = refs[:sums], refs[sums + after :]
    outs, sum_out = refs[: len(counts)], refs[len(counts) :]
    node_blks = inputs[0].shape[0]
    for number, (count, out_ref) in enumerate(zip(counts, outs)):
        kept_ref, arrived, inputs = inputs[0], inputs[1 : 1 + count], inputs[1 + count :]
        for block in range(node_blks):
            total = pair_sum([ref[block].astype(jnp.float32) for ref in arrived])
            out_ref[block] = (kept_ref[block] + total).astype(jnp.bfloat16)
        if with_loss and number == 0:
            both = from_parts(loss_ref[loss_ref.shape[0] - 1]) + from_parts(arrived[-1][node_blks])
            out_ref[node_blks] = to_parts(both, loss_ref.shape[1:])
    for out in sum_out:
        out[...] = functools.reduce(jnp.add, [ref[...] for ref in sum_in])


def next_level(level, risk_total, scen_total):
    level_new = level - primal_step * (1.0 - risk_total / scen_total)
    return level_new, 2.0 * level_new - level


def add_rows(values, shape):
    return jnp.broadcast_to(jnp.sum(values, axis=0, keepdims=True), shape)


def as_row(values):
    rows = values.shape[0]
    picked = lax.broadcasted_iota(jnp.int32, values.shape, 0) == lax.broadcasted_iota(
        jnp.int32, values.shape, 1
    )
    return jnp.sum(jnp.where(picked, values, 0.0), axis=0, keepdims=True)[:, :rows]


def settle_kernel(count, arc_total, scen_total, last, *refs):
    kept_ref, arrived, refs = refs[0], refs[1 : 1 + count], refs[1 + count :]
    loss_ref, base_ref, risk_ref, excess_ref, level_ref, sum_ref, other_ref = refs[:7]
    duals_out, half_out, risk_out, excess_out, level_out, sum_out = refs[7:]
    node_blks, _, rows = base_ref.shape
    for block in range(node_blks):
        total = kept_ref[block] + pair_sum([ref[block].astype(jnp.float32) for ref in arrived])
        duals = base_ref[block] - dual_step * total
        if last:
            duals_out[:, block * rows : (block + 1) * rows] = duals
        else:
            duals_out[block] = duals
            half_out[block] = duals.astype(jnp.bfloat16)
    losses = from_parts(loss_ref[node_blks]) + from_parts(arrived[-1][node_blks])
    losses = losses / arc_total
    risk = risk_ref[...]
    excess = excess_ref[...]
    excess_new = jnp.maximum(excess - primal_step * (tail_weight - risk), 0.0)
    excess_bar = 2.0 * excess_new - excess
    risk_new = risk + risk_step * (losses - excess_bar)
    risk_total = sum_ref[...] + other_ref[...]
    level_new, level_bar = next_level(level_ref[...], risk_total, scen_total)
    risk_new = jnp.maximum(risk_new - risk_step * level_bar[:1], 0.0)
    if last:
        risk_out[...] = as_row(risk_new)
        excess_out[...] = as_row(excess_new)
        level_out[...] = level_new[:1, :1]
    else:
        risk_out[...] = risk_new
        excess_out[...] = excess_new
        level_out[...] = level_new
        sum_out[...] = add_rows(risk_new, sum_out.shape)


def local_forward_kernel(
    touches,
    group,
    steps,
    index_ref,
    bar_ref,
    blocks_ref,
    duals_ref,
    demand_ref,
    out_ref,
    total,
):
    rows = blocks_ref.shape[-1]
    step = pl.program_id(0)
    first = step * group

    @pl.when(step == 0)
    def _():
        total[...] = jnp.zeros_like(total)

    for member in range(group):
        right = jnp.concatenate([blocks_ref[member, k] for k in range(touches)], axis=1)
        products = jnp.dot(
            bar_ref[:, member * rows : (member + 1) * rows],
            right,
            preferred_element_type=jnp.float32,
        )
        for k in range(touches):
            place = index_ref[k, first + member]
            total[place] += products[:, k * rows : (k + 1) * rows]

    @pl.when(step == steps - 1)
    def _():
        for block in range(total.shape[0]):
            demand = demand_ref[:, block * rows : (block + 1) * rows]
            out_ref[block] = duals_ref[block] + dual_step * (demand - total[block])


def whole(*shape):
    return pl.BlockSpec(shape, lambda i, *_: (0,) * len(shape))


def params(limit):
    return pltpu.CompilerParams(dimension_semantics=("arbitrary",), vmem_limit_bytes=limit)


def local_adjoint(index, panel, blocks):
    arc_blks, touches, rows, _ = blocks.shape
    scen_rows = panel.shape[1]
    group = GROUP
    return pl.pallas_call(
        functools.partial(local_adjoint_kernel, touches, group),
        out_shape=(
            jax.ShapeDtypeStruct((scen_rows, arc_blks * rows), jnp.float32),
            jax.ShapeDtypeStruct((8, rows), jnp.float32),
        ),
        grid_spec=pltpu.PrefetchScalarGridSpec(
            num_scalar_prefetch=1,
            grid=(arc_blks // group,),
            in_specs=[
                whole(*panel.shape),
                pl.BlockSpec((group, touches, rows, rows), lambda i, *_: (i, 0, 0, 0)),
            ],
            out_specs=(
                pl.BlockSpec((scen_rows, group * rows), lambda i, *_: (0, i)),
                whole(8, rows),
            ),
        ),
        compiler_params=params(SMALL_VMEM),
        cost_estimate=pl.CostEstimate(
            flops=2 * scen_rows * blocks.size, bytes_accessed=2 * blocks.size, transcendentals=0
        ),
        name="local_adjoint",
    )(index, panel, blocks)


def head_step(places, panels, heads, pulled, flows, costs, risk, sums):
    arc_blks, rows, _ = heads.shape
    scen_rows = flows.shape[0]
    peers = len(panels)
    node_blks = panels[0].shape[0]
    group = HEAD_GROUP
    steps = arc_blks // group
    kept = (node_blks, scen_rows, rows)
    sent = [kept] * (peers // 2)
    sent[-1] = (node_blks + 1, scen_rows, rows)
    arcs = pl.BlockSpec((scen_rows, group * rows), lambda i, *_: (0, i))
    results = pl.pallas_call(
        functools.partial(head_kernel, group, steps, peers),
        out_shape=[
            jax.ShapeDtypeStruct(flows.shape, jnp.float32),
            jax.ShapeDtypeStruct(flows.shape, jnp.bfloat16),
            jax.ShapeDtypeStruct(sums[0].shape, jnp.float32),
        ]
        + [jax.ShapeDtypeStruct(kept, jnp.float32)] * (peers // 2)
        + [jax.ShapeDtypeStruct(shape, jnp.bfloat16) for shape in sent],
        grid_spec=pltpu.PrefetchScalarGridSpec(
            num_scalar_prefetch=1,
            grid=(steps,),
            in_specs=[whole(*panels[0].shape)] * peers
            + [
                pl.BlockSpec((group, rows, rows), lambda i, *_: (i, 0, 0)),
                arcs,
                arcs,
                pl.BlockSpec((1, group * rows), lambda i, *_: (0, i)),
                whole(scen_rows, rows),
                whole(*sums[0].shape),
                whole(*sums[0].shape),
            ],
            out_specs=[arcs, arcs, whole(*sums[0].shape)]
            + [whole(*kept)] * (peers // 2)
            + [whole(*shape) for shape in sent],
            scratch_shapes=[
                pltpu.VMEM((peers * node_blks, scen_rows, rows), jnp.bfloat16),
                pltpu.VMEM((peers * node_blks, scen_rows, rows), jnp.float32),
                pltpu.VMEM((scen_rows, group * rows), jnp.float32),
                pltpu.VMEM((scen_rows, rows), jnp.float32),
            ],
        ),
        compiler_params=params((4 + peers + peers // 4) * MIB),
        cost_estimate=pl.CostEstimate(
            flops=4 * scen_rows * heads.size,
            bytes_accessed=2 * heads.size + 14 * flows.size + 4 * peers * panels[0].size,
            transcendentals=0,
        ),
        name="head_step",
    )(places, *panels, heads, pulled, flows, costs, risk, *sums)
    half = peers // 2
    kept = dict(zip(inner(peers), results[3 : 3 + half]))
    sends = dict(zip(leaves(peers), results[3 + half :]))
    return *results[:3], kept, sends


def small_cost(*arrays):
    size = sum(a.size for a in arrays)
    return pl.CostEstimate(flops=size, bytes_accessed=2 * size, transcendentals=0)


def fold(tops, loss, sums, after):
    node_blks, scen_rows, rows = tops[0][0].shape
    with_loss = loss is not None
    operands = [array for kept, arrived in tops for array in (kept, *arrived)]
    operands += ([loss] if with_loss else []) + list(sums)
    vmem = pl.BlockSpec(memory_space=pltpu.VMEM)
    out_shape = [
        jax.ShapeDtypeStruct((node_blks + (with_loss and number == 0), scen_rows, rows), jnp.bfloat16)
        for number in range(len(tops))
    ]
    out_shape += [jax.ShapeDtypeStruct(array.shape, array.dtype) for array in sums[:1]]
    counts = [len(arrived) for _, arrived in tops]
    results = pl.pallas_call(
        functools.partial(fold_kernel, counts, with_loss, len(sums), len(after)),
        out_shape=out_shape,
        in_specs=[vmem] * len(operands) + [pl.BlockSpec(memory_space=pl.ANY)] * len(after),
        out_specs=[vmem] * len(out_shape),
        compiler_params=pltpu.CompilerParams(vmem_limit_bytes=SMALL_VMEM),
        cost_estimate=small_cost(*operands),
        name="fold",
    )(*operands, *after)
    return results[: len(tops)], results[len(tops) :]


def settle(kept, arrived, loss, base, risk, excess, level, sums, arc_total, scen_total, last):
    node_blks, scen_rows, rows = base.shape
    return pl.pallas_call(
        functools.partial(settle_kernel, len(arrived), arc_total, scen_total, last),
        out_shape=(
            jax.ShapeDtypeStruct((scen_rows, node_blks * rows) if last else base.shape, jnp.float32),
            jax.ShapeDtypeStruct(base.shape, jnp.bfloat16),
            jax.ShapeDtypeStruct((1, scen_rows) if last else risk.shape, jnp.float32),
            jax.ShapeDtypeStruct((1, scen_rows) if last else risk.shape, jnp.float32),
            jax.ShapeDtypeStruct((1, 1) if last else level.shape, jnp.float32),
            jax.ShapeDtypeStruct(level.shape, jnp.float32),
        ),
        compiler_params=pltpu.CompilerParams(vmem_limit_bytes=SMALL_VMEM),
        cost_estimate=small_cost(kept, *arrived, base),
        name="settle",
    )(kept, *arrived, loss, base, risk, excess, level, *sums)


def local_forward(index, bar, blocks, duals, demand):
    arc_blks, touches, rows, _ = blocks.shape
    scen_rows = bar.shape[0]
    group = GROUP
    steps = arc_blks // group
    return pl.pallas_call(
        functools.partial(local_forward_kernel, touches, group, steps),
        out_shape=jax.ShapeDtypeStruct(duals.shape, jnp.float32),
        grid_spec=pltpu.PrefetchScalarGridSpec(
            num_scalar_prefetch=1,
            grid=(steps,),
            in_specs=[
                pl.BlockSpec((scen_rows, group * rows), lambda i, *_: (0, i)),
                pl.BlockSpec((group, touches, rows, rows), lambda i, *_: (i, 0, 0, 0)),
                whole(*duals.shape),
                whole(*demand.shape),
            ],
            out_specs=whole(*duals.shape),
            scratch_shapes=[pltpu.VMEM(duals.shape, jnp.float32)],
        ),
        compiler_params=params(SMALL_VMEM),
        cost_estimate=pl.CostEstimate(
            flops=2 * scen_rows * blocks.size, bytes_accessed=2 * blocks.size, transcendentals=0
        ),
        name="local_forward",
    )(index, bar, blocks, duals, demand)


def relay(arrived, risk_sum, after):
    def kernel(arrived_ref, sum_ref, *refs):
        arrived_out, sum_out = refs[-2:]
        arrived_out[...] = arrived_ref[...]
        sum_out[...] = sum_ref[...]

    vmem = pl.BlockSpec(memory_space=pltpu.VMEM)
    return pl.pallas_call(
        kernel,
        out_shape=(
            jax.ShapeDtypeStruct(arrived.shape, arrived.dtype),
            jax.ShapeDtypeStruct(risk_sum.shape, risk_sum.dtype),
        ),
        in_specs=[vmem, vmem] + [pl.BlockSpec(memory_space=pl.ANY)] * len(after),
        out_specs=(vmem, vmem),
        compiler_params=pltpu.CompilerParams(vmem_limit_bytes=SMALL_VMEM),
        cost_estimate=small_cost(arrived),
        name="relay",
    )(arrived, risk_sum, *after)


def prepare_kernel(node_blks, risk_ref, excess_ref, level_ref, head_ref, *refs):
    risk_out, excess_out, level_out, sum_out, places_out = refs[-5:]
    head = head_ref[...]
    owner = lax.div(head, node_blks)
    distance = jnp.bitwise_xor(owner, lax.axis_index("net"))
    places_out[...] = head + (distance - owner) * node_blks
    scen_rows = risk_out.shape[0]
    square = (scen_rows, scen_rows)
    same = lax.broadcasted_iota(jnp.int32, square, 0) == lax.broadcasted_iota(jnp.int32, square, 1)
    for row_ref, out in ((risk_ref, risk_out), (excess_ref, excess_out)):
        column = jnp.sum(jnp.where(same, row_ref[...], 0.0), axis=1, keepdims=True)
        out[...] = jnp.broadcast_to(column, out.shape)
    level_out[...] = jnp.broadcast_to(level_ref[...], level_out.shape)
    sum_out[...] = add_rows(risk_out[...], sum_out.shape)


def prepare(risk, excess, level, heads, rows, node_blks, after):
    wide, flat = (risk.shape[0], rows), (8, rows)
    return pl.pallas_call(
        functools.partial(prepare_kernel, node_blks),
        out_shape=[jax.ShapeDtypeStruct(shape, jnp.float32) for shape in (wide, wide, flat, flat)]
        + [jax.ShapeDtypeStruct((1, heads.shape[0]), jnp.int32)],
        in_specs=[pl.BlockSpec(memory_space=pltpu.VMEM)] * 4
        + [pl.BlockSpec(memory_space=pl.ANY)] * len(after),
        compiler_params=pltpu.CompilerParams(vmem_limit_bytes=SMALL_VMEM),
        cost_estimate=small_cost(risk),
        name="prepare",
    )(risk.reshape(1, -1), excess.reshape(1, -1), level.reshape(1, 1), heads.reshape(1, -1), *after)


def swap(value, axis, distance):
    size = lax.axis_size(axis)
    return lax.ppermute(value, axis, [(i, i ^ distance) for i in range(size)])


def gather_panels(own, risk_sum, after):
    peers = lax.axis_size("net")
    panels = [own] + [None] * (peers - 1)
    order = sorted(range(1, peers), key=lambda k: (k.bit_count(), -k))
    for distance in order:
        hop = last_hop(distance)
        panels[distance] = swap(panels[distance ^ hop], "net", hop)
        if distance == 1:
            far = peers // 2
            panels[far], risk_sum = relay(panels[far], risk_sum, after)
    return panels, risk_sum


def per_device(
    arc_flows,
    node_duals,
    demand,
    excess,
    risk_duals,
    threshold,
    arc_costs,
    local_blocks,
    head_blocks,
    local_index,
    head_index,
):
    rows = local_blocks.shape[-1]
    scen_rows = arc_flows.shape[0]
    node_blks = node_duals.shape[1] // rows
    net_size = lax.axis_size("net")
    arc_total = arc_flows.shape[1] * net_size
    scen_total = scen_rows * lax.axis_size("scen")
    costs = arc_costs.reshape(1, -1)
    touched = local_index.T
    scen_size = lax.axis_size("scen")
    duals = node_duals.reshape(scen_rows, node_blks, rows).transpose(1, 0, 2)
    half = duals.astype(jnp.bfloat16)
    flows = arc_flows
    strides = [1 << bit for bit in range(1, scen_size.bit_length() - 1)][::-1]
    for iteration in range(ROUNDS):
        first, last = iteration == 0, iteration == ROUNDS - 1
        pulled, token = local_adjoint(touched, half, local_blocks)
        panels, risk_sum = gather_panels(half, token if first else risk_sum, (token,))
        if first:
            risk, excess_now, level, risk_sum, places = prepare(
                risk_duals,
                excess,
                threshold,
                head_index,
                rows,
                node_blks,
                (panels[net_size // 2], head_blocks, arc_flows),
            )
            places = places.reshape(-1)
        sums = (risk_sum, swap(risk_sum, "scen", 1))
        flows, bar, risk_sum, kept, sends = head_step(
            places, panels, head_blocks, pulled, flows, costs, risk, sums
        )
        base = local_forward(touched, bar, local_blocks, duals, demand)
        tops = sorted(inner(net_size), key=lambda k: (-k.bit_count(), -k))[:-1]
        groups = [(top,) for top in tops if top != 1] + [(1,)]
        loss, loss_top = sends[net_size - 1], net_size - 1
        ahead = {5: swap(sends[5], "net", last_hop(5))}
        after = (ahead[5], base)
        for group in groups:
            terms = []
            for top in group:
                below = sorted(children(top, net_size))
                terms.append(
                    (
                        kept[top],
                        [ahead[k] if k in ahead else swap(sends[k], "net", last_hop(k)) for k in below],
                    )
                )
            chain = loss_top ^ last_hop(loss_top) == group[0]
            sums = (risk_sum,) if group[0] == net_size // 2 else ()
            if group == (1,):
                after = (loss,)
            folded, passed = fold(terms, loss if chain else None, sums, after)
            sends.update(zip(group, folded))
            after = ()
            if chain:
                loss_top, loss = group[0], folded[0]
            if sums:
                (risk_sum,) = passed
        below = sorted(children(0, net_size))
        arrived = [swap(sends[k], "net", last_hop(k)) for k in below]
        for stride in strides[:-1]:
            risk_sum = risk_sum + swap(risk_sum, "scen", stride)
        sums = (risk_sum, swap(risk_sum, "scen", strides[-1]))
        duals, half, risk, excess_now, level, risk_sum = settle(
            kept[0],
            arrived,
            loss,
            base,
            risk,
            excess_now,
            level,
            sums,
            arc_total,
            scen_total,
            last,
        )
    return (flows, duals, excess_now.reshape(-1), risk.reshape(-1), level.reshape(-1))


def solution(mesh):
    placed = (
        P("scen", "net"),
        P("scen", "net"),
        P("scen", "net"),
        P("scen"),
        P("scen"),
        P(),
        P("net"),
        P("net", None, None, None),
        P("net", None, None),
        P("net", None),
        P("net"),
    )
    return jax.shard_map(
        per_device,
        mesh=mesh,
        in_specs=placed,
        out_specs=(P("scen", "net"), P("scen", "net"), P("scen"), P("scen"), P()),
        check_vma=False,
    )
```

```python
import functools

import jax
import jax.numpy as jnp
from jax import lax
from jax.experimental import pallas as pl
from jax.experimental.pallas import tpu as pltpu
from jax.sharding import PartitionSpec as P

ROUNDS = 3

primal_step = 0.5
dual_step = 0.5
risk_step = 1.0
tail_weight = 2.0

MIB = 1024 * 1024
GROUP = 8
HEAD_GROUP = 16
SMALL_VMEM = 6 * MIB


def contract_last(left, right):
    return lax.dot_general(
        left, right, (((1,), (1,)), ((), ())), preferred_element_type=jnp.float32
    )


def local_adjoint_kernel(
    touches, group, index_ref, panel_ref, blocks_ref, out_ref, token_ref
):
    token_ref[...] = jnp.zeros_like(token_ref)
    rows = blocks_ref.shape[-1]
    first = pl.program_id(0) * group
    for member in range(group):
        left = jnp.concatenate(
            [panel_ref[index_ref[k, first + member]] for k in range(touches)], axis=1
        )
        right = jnp.concatenate([blocks_ref[member, k] for k in range(touches)], axis=1)
        out_ref[:, member * rows : (member + 1) * rows] = contract_last(left, right)


def to_parts(column, shape):
    high = column.astype(jnp.bfloat16).astype(jnp.float32)
    rest = column - high
    middle = rest.astype(jnp.bfloat16).astype(jnp.float32)
    low = rest - middle
    lane = lax.broadcasted_iota(jnp.int32, shape, 1)
    packed = jnp.where(
        lane == 0, high, jnp.where(lane == 1, middle, jnp.where(lane == 2, low, 0.0))
    )
    return packed.astype(jnp.bfloat16)


def from_parts(parts):
    return jnp.sum(parts.astype(jnp.float32), axis=1, keepdims=True)


def head_kernel(group, steps, peers, index_ref, *refs):
    panels, refs = refs[:peers], refs[peers:]
    heads_ref, pulled_ref, flows_ref, costs_ref, risk_ref, sum_ref, other_ref = refs[:7]
    flows_out, bar_out, sum_out, refs = *refs[7:10], refs[10:]
    kept, refs = refs[: peers // 2], refs[peers // 2 :]
    sends, (panel, terms, pulled, loss) = refs[:-4], refs[-4:]
    rows = heads_ref.shape[-1]
    node_blks = panels[0].shape[0]
    step = pl.program_id(0)
    first = step * group

    @pl.when(step == 0)
    def _():
        terms[...] = jnp.zeros_like(terms)
        loss[...] = jnp.zeros_like(loss)
        sum_out[...] = sum_ref[...] + other_ref[...]
        for peer in range(peers):
            panel[peer * node_blks : (peer + 1) * node_blks] = panels[peer][...]

    places = [index_ref[first + member] for member in range(group)]
    spans = [slice(member * rows, (member + 1) * rows) for member in range(group)]
    for member in range(group):
        pulled[:, spans[member]] = contract_last(panel[places[member]], heads_ref[member])
    risk = risk_ref[...]
    loss_sum = jnp.zeros_like(risk)
    for columns in spans:
        flows = flows_ref[:, columns]
        cost = costs_ref[:, columns]
        gradient = risk * cost - (pulled[:, columns] + pulled_ref[:, columns])
        flows_new = jnp.maximum(flows - primal_step * gradient, 0.0)
        bar = 2.0 * flows_new - flows
        flows_out[:, columns] = flows_new
        loss_sum += cost * bar
        bar_out[:, columns] = bar.astype(jnp.bfloat16)
    loss[...] += loss_sum
    products = [
        jnp.dot(bar_out[:, spans[m]], heads_ref[m], preferred_element_type=jnp.float32)
        for m in range(group)
    ]
    for member in range(group):
        terms[places[member]] += products[member]

    @pl.when(step == steps - 1)
    def _():
        loss_parts = to_parts(jnp.sum(loss[...], axis=1, keepdims=True), loss.shape)
        for out, distance in zip(kept, inner(peers)):
            out[...] = terms[distance * node_blks : (distance + 1) * node_blks]
        for out, distance in zip(sends, leaves(peers)):
            out[:node_blks] = terms[distance * node_blks : (distance + 1) * node_blks].astype(
                jnp.bfloat16
            )
        sends[-1][node_blks] = loss_parts


def last_hop(distance):
    return distance & -distance


def children(distance, peers):
    return [k for k in range(1, peers) if k ^ last_hop(k) == distance]


def inner(peers):
    return [k for k in range(peers) if children(k, peers)]


def leaves(peers):
    return [k for k in range(peers) if not children(k, peers)]


def pair_sum(values):
    while len(values) > 1:
        values = [a + b for a, b in zip(values[::2], values[1::2])] + values[len(values) // 2 * 2 :]
    return values[0]


def fold_kernel(counts, with_loss, sums, after, *refs):
    inputs, refs = refs[: sum(counts) + len(counts)], refs[sum(counts) + len(counts) :]
    if with_loss:
        loss_ref, refs = refs[0], refs[1:]
    sum_in, refs = refs[:sums], refs[sums + after :]
    outs, sum_out = refs[: len(counts)], refs[len(counts) :]
    node_blks = inputs[0].shape[0]
    for number, (count, out_ref) in enumerate(zip(counts, outs)):
        kept_ref, arrived, inputs = inputs[0], inputs[1 : 1 + count], inputs[1 + count :]
        for block in range(node_blks):
            total = pair_sum([ref[block].astype(jnp.float32) for ref in arrived])
            out_ref[block] = (kept_ref[block] + total).astype(jnp.bfloat16)
        if with_loss and number == 0:
            both = from_parts(loss_ref[loss_ref.shape[0] - 1]) + from_parts(arrived[-1][node_blks])
            out_ref[node_blks] = to_parts(both, loss_ref.shape[1:])
    for out in sum_out:
        out[...] = functools.reduce(jnp.add, [ref[...] for ref in sum_in])


def next_level(level, risk_total, scen_total):
    level_new = level - primal_step * (1.0 - risk_total / scen_total)
    return level_new, 2.0 * level_new - level


def add_rows(values, shape):
    return jnp.broadcast_to(jnp.sum(values, axis=0, keepdims=True), shape)


def as_row(values):
    rows = values.shape[0]
    picked = lax.broadcasted_iota(jnp.int32, values.shape, 0) == lax.broadcasted_iota(
        jnp.int32, values.shape, 1
    )
    return jnp.sum(jnp.where(picked, values, 0.0), axis=0, keepdims=True)[:, :rows]


def settle_kernel(count, arc_total, scen_total, last, *refs):
    kept_ref, arrived, refs = refs[0], refs[1 : 1 + count], refs[1 + count :]
    loss_ref, base_ref, risk_ref, excess_ref, level_ref, sum_ref, other_ref = refs[:7]
    duals_out, half_out, risk_out, excess_out, level_out, sum_out = refs[7:]
    node_blks, _, rows = base_ref.shape
    for block in range(node_blks):
        total = kept_ref[block] + pair_sum([ref[block].astype(jnp.float32) for ref in arrived])
        duals = base_ref[block] - dual_step * total
        if last:
            duals_out[:, block * rows : (block + 1) * rows] = duals
        else:
            duals_out[block] = duals
            half_out[block] = duals.astype(jnp.bfloat16)
    losses = from_parts(loss_ref[node_blks]) + from_parts(arrived[-1][node_blks])
    losses = losses / arc_total
    risk = risk_ref[...]
    excess = excess_ref[...]
    excess_new = jnp.maximum(excess - primal_step * (tail_weight - risk), 0.0)
    excess_bar = 2.0 * excess_new - excess
    risk_new = risk + risk_step * (losses - excess_bar)
    risk_total = sum_ref[...] + other_ref[...]
    level_new, level_bar = next_level(level_ref[...], risk_total, scen_total)
    risk_new = jnp.maximum(risk_new - risk_step * level_bar[:1], 0.0)
    if last:
        risk_out[...] = as_row(risk_new)
        excess_out[...] = as_row(excess_new)
        level_out[...] = level_new[:1, :1]
    else:
        risk_out[...] = risk_new
        excess_out[...] = excess_new
        level_out[...] = level_new
        sum_out[...] = add_rows(risk_new, sum_out.shape)


def local_forward_kernel(
    touches,
    group,
    steps,
    index_ref,
    bar_ref,
    blocks_ref,
    duals_ref,
    demand_ref,
    out_ref,
    total,
):
    rows = blocks_ref.shape[-1]
    step = pl.program_id(0)
    first = step * group

    @pl.when(step == 0)
    def _():
        total[...] = jnp.zeros_like(total)

    for member in range(group):
        right = jnp.concatenate([blocks_ref[member, k] for k in range(touches)], axis=1)
        products = jnp.dot(
            bar_ref[:, member * rows : (member + 1) * rows],
            right,
            preferred_element_type=jnp.float32,
        )
        for k in range(touches):
            place = index_ref[k, first + member]
            total[place] += products[:, k * rows : (k + 1) * rows]

    @pl.when(step == steps - 1)
    def _():
        for block in range(total.shape[0]):
            demand = demand_ref[:, block * rows : (block + 1) * rows]
            out_ref[block] = duals_ref[block] + dual_step * (demand - total[block])


def whole(*shape):
    return pl.BlockSpec(shape, lambda i, *_: (0,) * len(shape))


def params(limit):
    return pltpu.CompilerParams(dimension_semantics=("arbitrary",), vmem_limit_bytes=limit)


def local_adjoint(index, panel, blocks):
    arc_blks, touches, rows, _ = blocks.shape
    scen_rows = panel.shape[1]
    group = GROUP
    return pl.pallas_call(
        functools.partial(local_adjoint_kernel, touches, group),
        out_shape=(
            jax.ShapeDtypeStruct((scen_rows, arc_blks * rows), jnp.float32),
            jax.ShapeDtypeStruct((8, rows), jnp.float32),
        ),
        grid_spec=pltpu.PrefetchScalarGridSpec(
            num_scalar_prefetch=1,
            grid=(arc_blks // group,),
            in_specs=[
                whole(*panel.shape),
                pl.BlockSpec((group, touches, rows, rows), lambda i, *_: (i, 0, 0, 0)),
            ],
            out_specs=(
                pl.BlockSpec((scen_rows, group * rows), lambda i, *_: (0, i)),
                whole(8, rows),
            ),
        ),
        compiler_params=params(SMALL_VMEM),
        cost_estimate=pl.CostEstimate(
            flops=2 * scen_rows * blocks.size, bytes_accessed=2 * blocks.size, transcendentals=0
        ),
        name="local_adjoint",
    )(index, panel, blocks)


def head_step(places, panels, heads, pulled, flows, costs, risk, sums):
    arc_blks, rows, _ = heads.shape
    scen_rows = flows.shape[0]
    peers = len(panels)
    node_blks = panels[0].shape[0]
    group = HEAD_GROUP
    steps = arc_blks // group
    kept = (node_blks, scen_rows, rows)
    sent = [kept] * (peers // 2)
    sent[-1] = (node_blks + 1, scen_rows, rows)
    arcs = pl.BlockSpec((scen_rows, group * rows), lambda i, *_: (0, i))
    results = pl.pallas_call(
        functools.partial(head_kernel, group, steps, peers),
        out_shape=[
            jax.ShapeDtypeStruct(flows.shape, jnp.float32),
            jax.ShapeDtypeStruct(flows.shape, jnp.bfloat16),
            jax.ShapeDtypeStruct(sums[0].shape, jnp.float32),
        ]
        + [jax.ShapeDtypeStruct(kept, jnp.float32)] * (peers // 2)
        + [jax.ShapeDtypeStruct(shape, jnp.bfloat16) for shape in sent],
        grid_spec=pltpu.PrefetchScalarGridSpec(
            num_scalar_prefetch=1,
            grid=(steps,),
            in_specs=[whole(*panels[0].shape)] * peers
            + [
                pl.BlockSpec((group, rows, rows), lambda i, *_: (i, 0, 0)),
                arcs,
                arcs,
                pl.BlockSpec((1, group * rows), lambda i, *_: (0, i)),
                whole(scen_rows, rows),
                whole(*sums[0].shape),
                whole(*sums[0].shape),
            ],
            out_specs=[arcs, arcs, whole(*sums[0].shape)]
            + [whole(*kept)] * (peers // 2)
            + [whole(*shape) for shape in sent],
            scratch_shapes=[
                pltpu.VMEM((peers * node_blks, scen_rows, rows), jnp.bfloat16),
                pltpu.VMEM((peers * node_blks, scen_rows, rows), jnp.float32),
                pltpu.VMEM((scen_rows, group * rows), jnp.float32),
                pltpu.VMEM((scen_rows, rows), jnp.float32),
            ],
        ),
        compiler_params=params((4 + peers + peers // 4) * MIB),
        cost_estimate=pl.CostEstimate(
            flops=4 * scen_rows * heads.size,
            bytes_accessed=2 * heads.size + 14 * flows.size + 4 * peers * panels[0].size,
            transcendentals=0,
        ),
        name="head_step",
    )(places, *panels, heads, pulled, flows, costs, risk, *sums)
    half = peers // 2
    kept = dict(zip(inner(peers), results[3 : 3 + half]))
    sends = dict(zip(leaves(peers), results[3 + half :]))
    return *results[:3], kept, sends


def small_cost(*arrays):
    size = sum(a.size for a in arrays)
    return pl.CostEstimate(flops=size, bytes_accessed=2 * size, transcendentals=0)


def fold(tops, loss, sums, after):
    node_blks, scen_rows, rows = tops[0][0].shape
    with_loss = loss is not None
    operands = [array for kept, arrived in tops for array in (kept, *arrived)]
    operands += ([loss] if with_loss else []) + list(sums)
    vmem = pl.BlockSpec(memory_space=pltpu.VMEM)
    out_shape = [
        jax.ShapeDtypeStruct((node_blks + (with_loss and number == 0), scen_rows, rows), jnp.bfloat16)
        for number in range(len(tops))
    ]
    out_shape += [jax.ShapeDtypeStruct(array.shape, array.dtype) for array in sums[:1]]
    counts = [len(arrived) for _, arrived in tops]
    results = pl.pallas_call(
        functools.partial(fold_kernel, counts, with_loss, len(sums), len(after)),
        out_shape=out_shape,
        in_specs=[vmem] * len(operands) + [pl.BlockSpec(memory_space=pl.ANY)] * len(after),
        out_specs=[vmem] * len(out_shape),
        compiler_params=pltpu.CompilerParams(vmem_limit_bytes=SMALL_VMEM),
        cost_estimate=small_cost(*operands),
        name="fold",
    )(*operands, *after)
    return results[: len(tops)], results[len(tops) :]


def settle(kept, arrived, loss, base, risk, excess, level, sums, arc_total, scen_total, last):
    node_blks, scen_rows, rows = base.shape
    return pl.pallas_call(
        functools.partial(settle_kernel, len(arrived), arc_total, scen_total, last),
        out_shape=(
            jax.ShapeDtypeStruct((scen_rows, node_blks * rows) if last else base.shape, jnp.float32),
            jax.ShapeDtypeStruct(base.shape, jnp.bfloat16),
            jax.ShapeDtypeStruct((1, scen_rows) if last else risk.shape, jnp.float32),
            jax.ShapeDtypeStruct((1, scen_rows) if last else risk.shape, jnp.float32),
            jax.ShapeDtypeStruct((1, 1) if last else level.shape, jnp.float32),
            jax.ShapeDtypeStruct(level.shape, jnp.float32),
        ),
        compiler_params=pltpu.CompilerParams(vmem_limit_bytes=SMALL_VMEM),
        cost_estimate=small_cost(kept, *arrived, base),
        name="settle",
    )(kept, *arrived, loss, base, risk, excess, level, *sums)


def local_forward(index, bar, blocks, duals, demand):
    arc_blks, touches, rows, _ = blocks.shape
    scen_rows = bar.shape[0]
    group = GROUP
    steps = arc_blks // group
    return pl.pallas_call(
        functools.partial(local_forward_kernel, touches, group, steps),
        out_shape=jax.ShapeDtypeStruct(duals.shape, jnp.float32),
        grid_spec=pltpu.PrefetchScalarGridSpec(
            num_scalar_prefetch=1,
            grid=(steps,),
            in_specs=[
                pl.BlockSpec((scen_rows, group * rows), lambda i, *_: (0, i)),
                pl.BlockSpec((group, touches, rows, rows), lambda i, *_: (i, 0, 0, 0)),
                whole(*duals.shape),
                whole(*demand.shape),
            ],
            out_specs=whole(*duals.shape),
            scratch_shapes=[pltpu.VMEM(duals.shape, jnp.float32)],
        ),
        compiler_params=params(SMALL_VMEM),
        cost_estimate=pl.CostEstimate(
            flops=2 * scen_rows * blocks.size, bytes_accessed=2 * blocks.size, transcendentals=0
        ),
        name="local_forward",
    )(index, bar, blocks, duals, demand)


def relay(arrived, risk_sum, after):
    def kernel(arrived_ref, sum_ref, *refs):
        arrived_out, sum_out = refs[-2:]
        arrived_out[...] = arrived_ref[...]
        sum_out[...] = sum_ref[...]

    vmem = pl.BlockSpec(memory_space=pltpu.VMEM)
    return pl.pallas_call(
        kernel,
        out_shape=(
            jax.ShapeDtypeStruct(arrived.shape, arrived.dtype),
            jax.ShapeDtypeStruct(risk_sum.shape, risk_sum.dtype),
        ),
        in_specs=[vmem, vmem] + [pl.BlockSpec(memory_space=pl.ANY)] * len(after),
        out_specs=(vmem, vmem),
        compiler_params=pltpu.CompilerParams(vmem_limit_bytes=SMALL_VMEM),
        cost_estimate=small_cost(arrived),
        name="relay",
    )(arrived, risk_sum, *after)


def prepare_kernel(node_blks, risk_ref, excess_ref, level_ref, head_ref, *refs):
    risk_out, excess_out, level_out, sum_out, places_out = refs[-5:]
    head = head_ref[...]
    owner = lax.div(head, node_blks)
    distance = jnp.bitwise_xor(owner, lax.axis_index("net"))
    places_out[...] = head + (distance - owner) * node_blks
    scen_rows = risk_out.shape[0]
    square = (scen_rows, scen_rows)
    same = lax.broadcasted_iota(jnp.int32, square, 0) == lax.broadcasted_iota(jnp.int32, square, 1)
    for row_ref, out in ((risk_ref, risk_out), (excess_ref, excess_out)):
        column = jnp.sum(jnp.where(same, row_ref[...], 0.0), axis=1, keepdims=True)
        out[...] = jnp.broadcast_to(column, out.shape)
    level_out[...] = jnp.broadcast_to(level_ref[...], level_out.shape)
    sum_out[...] = add_rows(risk_out[...], sum_out.shape)


def prepare(risk, excess, level, heads, rows, node_blks, after):
    wide, flat = (risk.shape[0], rows), (8, rows)
    return pl.pallas_call(
        functools.partial(prepare_kernel, node_blks),
        out_shape=[jax.ShapeDtypeStruct(shape, jnp.float32) for shape in (wide, wide, flat, flat)]
        + [jax.ShapeDtypeStruct((1, heads.shape[0]), jnp.int32)],
        in_specs=[pl.BlockSpec(memory_space=pltpu.VMEM)] * 4
        + [pl.BlockSpec(memory_space=pl.ANY)] * len(after),
        compiler_params=pltpu.CompilerParams(vmem_limit_bytes=SMALL_VMEM),
        cost_estimate=small_cost(risk),
        name="prepare",
    )(risk.reshape(1, -1), excess.reshape(1, -1), level.reshape(1, 1), heads.reshape(1, -1), *after)


def swap(value, axis, distance):
    size = lax.axis_size(axis)
    return lax.ppermute(value, axis, [(i, i ^ distance) for i in range(size)])


def gather_panels(own, risk_sum, after):
    peers = lax.axis_size("net")
    panels = [own] + [None] * (peers - 1)
    order = sorted(range(1, peers), key=lambda k: (k.bit_count(), -k))
    for distance in order:
        hop = last_hop(distance)
        panels[distance] = swap(panels[distance ^ hop], "net", hop)
        if distance == 1:
            far = peers // 2
            panels[far], risk_sum = relay(panels[far], risk_sum, (*after, panels[2], panels[1]))
    return panels, risk_sum


def per_device(
    arc_flows,
    node_duals,
    demand,
    excess,
    risk_duals,
    threshold,
    arc_costs,
    local_blocks,
    head_blocks,
    local_index,
    head_index,
):
    rows = local_blocks.shape[-1]
    scen_rows = arc_flows.shape[0]
    node_blks = node_duals.shape[1] // rows
    net_size = lax.axis_size("net")
    arc_total = arc_flows.shape[1] * net_size
    scen_total = scen_rows * lax.axis_size("scen")
    costs = arc_costs.reshape(1, -1)
    touched = local_index.T
    scen_size = lax.axis_size("scen")
    duals = node_duals.reshape(scen_rows, node_blks, rows).transpose(1, 0, 2)
    half = duals.astype(jnp.bfloat16)
    flows = arc_flows
    strides = [1 << bit for bit in range(1, scen_size.bit_length() - 1)][::-1]
    for iteration in range(ROUNDS):
        first, last = iteration == 0, iteration == ROUNDS - 1
        pulled, token = local_adjoint(touched, half, local_blocks)
        panels, risk_sum = gather_panels(half, token if first else risk_sum, (token,))
        if first:
            risk, excess_now, level, risk_sum, places = prepare(
                risk_duals,
                excess,
                threshold,
                head_index,
                rows,
                node_blks,
                (panels[net_size // 2], head_blocks, arc_flows),
            )
            places = places.reshape(-1)
        sums = (risk_sum, swap(risk_sum, "scen", 1))
        flows, bar, risk_sum, kept, sends = head_step(
            places, panels, head_blocks, pulled, flows, costs, risk, sums
        )
        base = local_forward(touched, bar, local_blocks, duals, demand)
        tops = sorted(inner(net_size), key=lambda k: (-k.bit_count(), -k))[:-1]
        groups = [(top,) for top in tops]
        loss, loss_top = sends[net_size - 1], net_size - 1
        ahead = {5: swap(sends[5], "net", last_hop(5))}
        after = (ahead[5], base)
        for group in groups:
            terms = []
            for top in group:
                below = sorted(children(top, net_size))
                terms.append(
                    (
                        kept[top],
                        [ahead[k] if k in ahead else swap(sends[k], "net", last_hop(k)) for k in below],
                    )
                )
            chain = loss_top ^ last_hop(loss_top) == group[0]
            sums = (risk_sum,) if group[0] == net_size // 2 else ()
            if loss_top == net_size // 2:
                after = (loss,)
            folded, passed = fold(terms, loss if chain else None, sums, after)
            sends.update(zip(group, folded))
            after = ()
            if chain:
                loss_top, loss = group[0], folded[0]
            if sums:
                (risk_sum,) = passed
        below = sorted(children(0, net_size))
        arrived = [swap(sends[k], "net", last_hop(k)) for k in below]
        for stride in strides[:-1]:
            risk_sum = risk_sum + swap(risk_sum, "scen", stride)
        sums = (risk_sum, swap(risk_sum, "scen", strides[-1]))
        duals, half, risk, excess_now, level, risk_sum = settle(
            kept[0],
            arrived,
            loss,
            base,
            risk,
            excess_now,
            level,
            sums,
            arc_total,
            scen_total,
            last,
        )
    return (flows, duals, excess_now.reshape(-1), risk.reshape(-1), level.reshape(-1))


def solution(mesh):
    placed = (
        P("scen", "net"),
        P("scen", "net"),
        P("scen", "net"),
        P("scen"),
        P("scen"),
        P(),
        P("net"),
        P("net", None, None, None),
        P("net", None, None),
        P("net", None),
        P("net"),
    )
    return jax.shard_map(
        per_device,
        mesh=mesh,
        in_specs=placed,
        out_specs=(P("scen", "net"), P("scen", "net"), P("scen"), P("scen"), P()),
        check_vma=False,
    )
```

```python
import functools

import jax
import jax.numpy as jnp
from jax import lax
from jax.experimental import pallas as pl
from jax.experimental.pallas import tpu as pltpu
from jax.sharding import PartitionSpec as P

ROUNDS = 3

primal_step = 0.5
dual_step = 0.5
risk_step = 1.0
tail_weight = 2.0

MIB = 1024 * 1024
GROUP = 8
HEAD_GROUP = 32
SMALL_VMEM = 6 * MIB


def contract_last(left, right):
    return lax.dot_general(
        left, right, (((1,), (1,)), ((), ())), preferred_element_type=jnp.float32
    )


def local_adjoint_kernel(
    touches, group, index_ref, panel_ref, blocks_ref, out_ref, token_ref
):
    token_ref[...] = jnp.zeros_like(token_ref)
    rows = blocks_ref.shape[-1]
    first = pl.program_id(0) * group
    for member in range(group):
        left = jnp.concatenate(
            [panel_ref[index_ref[k, first + member]] for k in range(touches)], axis=1
        )
        right = jnp.concatenate([blocks_ref[member, k] for k in range(touches)], axis=1)
        out_ref[:, member * rows : (member + 1) * rows] = contract_last(left, right)


def to_parts(column, shape):
    high = column.astype(jnp.bfloat16).astype(jnp.float32)
    rest = column - high
    middle = rest.astype(jnp.bfloat16).astype(jnp.float32)
    low = rest - middle
    lane = lax.broadcasted_iota(jnp.int32, shape, 1)
    packed = jnp.where(
        lane == 0, high, jnp.where(lane == 1, middle, jnp.where(lane == 2, low, 0.0))
    )
    return packed.astype(jnp.bfloat16)


def from_parts(parts):
    return jnp.sum(parts.astype(jnp.float32), axis=1, keepdims=True)


def head_kernel(group, steps, peers, index_ref, *refs):
    panels, refs = refs[:peers], refs[peers:]
    heads_ref, pulled_ref, flows_ref, costs_ref, risk_ref, sum_ref, other_ref = refs[:7]
    flows_out, bar_out, sum_out, refs = *refs[7:10], refs[10:]
    kept, refs = refs[: peers // 2], refs[peers // 2 :]
    sends, (panel, terms, pulled, loss) = refs[:-4], refs[-4:]
    rows = heads_ref.shape[-1]
    node_blks = panels[0].shape[0]
    step = pl.program_id(0)
    first = step * group

    @pl.when(step == 0)
    def _():
        terms[...] = jnp.zeros_like(terms)
        loss[...] = jnp.zeros_like(loss)
        sum_out[...] = sum_ref[...] + other_ref[...]
        for peer in range(peers):
            panel[peer * node_blks : (peer + 1) * node_blks] = panels[peer][...]

    places = [index_ref[first + member] for member in range(group)]
    spans = [slice(member * rows, (member + 1) * rows) for member in range(group)]
    for member in range(group):
        pulled[:, spans[member]] = contract_last(panel[places[member]], heads_ref[member])
    risk = risk_ref[...]
    loss_sum = jnp.zeros_like(risk)
    for columns in spans:
        flows = flows_ref[:, columns]
        cost = costs_ref[:, columns]
        gradient = risk * cost - (pulled[:, columns] + pulled_ref[:, columns])
        flows_new = jnp.maximum(flows - primal_step * gradient, 0.0)
        bar = 2.0 * flows_new - flows
        flows_out[:, columns] = flows_new
        loss_sum += cost * bar
        bar_out[:, columns] = bar.astype(jnp.bfloat16)
    loss[...] += loss_sum
    products = [
        jnp.dot(bar_out[:, spans[m]], heads_ref[m], preferred_element_type=jnp.float32)
        for m in range(group)
    ]
    for member in range(group):
        terms[places[member]] += products[member]

    @pl.when(step == steps - 1)
    def _():
        loss_parts = to_parts(jnp.sum(loss[...], axis=1, keepdims=True), loss.shape)
        for out, distance in zip(kept, inner(peers)):
            out[...] = terms[distance * node_blks : (distance + 1) * node_blks]
        for out, distance in zip(sends, leaves(peers)):
            out[:node_blks] = terms[distance * node_blks : (distance + 1) * node_blks].astype(
                jnp.bfloat16
            )
        sends[-1][node_blks] = loss_parts


def last_hop(distance):
    return 2 if distance == 3 else distance & -distance


def children(distance, peers):
    return [k for k in range(1, peers) if k ^ last_hop(k) == distance]


def inner(peers):
    return [k for k in range(peers) if children(k, peers)]


def leaves(peers):
    return [k for k in range(peers) if not children(k, peers)]


def pair_sum(values):
    while len(values) > 1:
        values = [a + b for a, b in zip(values[::2], values[1::2])] + values[len(values) // 2 * 2 :]
    return values[0]


def fold_kernel(counts, with_loss, sums, after, *refs):
    inputs, refs = refs[: sum(counts) + len(counts)], refs[sum(counts) + len(counts) :]
    if with_loss:
        loss_ref, refs = refs[0], refs[1:]
    sum_in, refs = refs[:sums], refs[sums + after :]
    outs, sum_out = refs[: len(counts)], refs[len(counts) :]
    node_blks = inputs[0].shape[0]
    for number, (count, out_ref) in enumerate(zip(counts, outs)):
        kept_ref, arrived, inputs = inputs[0], inputs[1 : 1 + count], inputs[1 + count :]
        for block in range(node_blks):
            total = pair_sum([ref[block].astype(jnp.float32) for ref in arrived])
            out_ref[block] = (kept_ref[block] + total).astype(jnp.bfloat16)
        if with_loss and number == 0:
            both = from_parts(loss_ref[loss_ref.shape[0] - 1]) + from_parts(arrived[-1][node_blks])
            out_ref[node_blks] = to_parts(both, loss_ref.shape[1:])
    for out in sum_out:
        out[...] = functools.reduce(jnp.add, [ref[...] for ref in sum_in])


def next_level(level, risk_total, scen_total):
    level_new = level - primal_step * (1.0 - risk_total / scen_total)
    return level_new, 2.0 * level_new - level


def add_rows(values, shape):
    return jnp.broadcast_to(jnp.sum(values, axis=0, keepdims=True), shape)


def as_row(values):
    rows = values.shape[0]
    picked = lax.broadcasted_iota(jnp.int32, values.shape, 0) == lax.broadcasted_iota(
        jnp.int32, values.shape, 1
    )
    return jnp.sum(jnp.where(picked, values, 0.0), axis=0, keepdims=True)[:, :rows]


def settle_kernel(count, arc_total, scen_total, last, *refs):
    kept_ref, arrived, refs = refs[0], refs[1 : 1 + count], refs[1 + count :]
    loss_ref, base_ref, risk_ref, excess_ref, level_ref, sum_ref, other_ref = refs[:7]
    duals_out, half_out, risk_out, excess_out, level_out, sum_out = refs[7:]
    node_blks, _, rows = base_ref.shape
    for block in range(node_blks):
        total = kept_ref[block] + pair_sum([ref[block].astype(jnp.float32) for ref in arrived])
        duals = base_ref[block] - dual_step * total
        if last:
            duals_out[:, block * rows : (block + 1) * rows] = duals
        else:
            duals_out[block] = duals
            half_out[block] = duals.astype(jnp.bfloat16)
    losses = from_parts(loss_ref[node_blks]) + from_parts(arrived[-1][node_blks])
    losses = losses / arc_total
    risk = risk_ref[...]
    excess = excess_ref[...]
    excess_new = jnp.maximum(excess - primal_step * (tail_weight - risk), 0.0)
    excess_bar = 2.0 * excess_new - excess
    risk_new = risk + risk_step * (losses - excess_bar)
    risk_total = sum_ref[...] + other_ref[...]
    level_new, level_bar = next_level(level_ref[...], risk_total, scen_total)
    risk_new = jnp.maximum(risk_new - risk_step * level_bar[:1], 0.0)
    if last:
        risk_out[...] = as_row(risk_new)
        excess_out[...] = as_row(excess_new)
        level_out[...] = level_new[:1, :1]
    else:
        risk_out[...] = risk_new
        excess_out[...] = excess_new
        level_out[...] = level_new
        sum_out[...] = add_rows(risk_new, sum_out.shape)


def local_forward_kernel(
    touches,
    group,
    steps,
    index_ref,
    bar_ref,
    blocks_ref,
    duals_ref,
    demand_ref,
    out_ref,
    total,
):
    rows = blocks_ref.shape[-1]
    step = pl.program_id(0)
    first = step * group

    @pl.when(step == 0)
    def _():
        total[...] = jnp.zeros_like(total)

    for member in range(group):
        right = jnp.concatenate([blocks_ref[member, k] for k in range(touches)], axis=1)
        products = jnp.dot(
            bar_ref[:, member * rows : (member + 1) * rows],
            right,
            preferred_element_type=jnp.float32,
        )
        for k in range(touches):
            place = index_ref[k, first + member]
            total[place] += products[:, k * rows : (k + 1) * rows]

    @pl.when(step == steps - 1)
    def _():
        for block in range(total.shape[0]):
            demand = demand_ref[:, block * rows : (block + 1) * rows]
            out_ref[block] = duals_ref[block] + dual_step * (demand - total[block])


def whole(*shape):
    return pl.BlockSpec(shape, lambda i, *_: (0,) * len(shape))


def params(limit):
    return pltpu.CompilerParams(dimension_semantics=("arbitrary",), vmem_limit_bytes=limit)


def local_adjoint(index, panel, blocks):
    arc_blks, touches, rows, _ = blocks.shape
    scen_rows = panel.shape[1]
    group = GROUP
    return pl.pallas_call(
        functools.partial(local_adjoint_kernel, touches, group),
        out_shape=(
            jax.ShapeDtypeStruct((scen_rows, arc_blks * rows), jnp.float32),
            jax.ShapeDtypeStruct((8, rows), jnp.float32),
        ),
        grid_spec=pltpu.PrefetchScalarGridSpec(
            num_scalar_prefetch=1,
            grid=(arc_blks // group,),
            in_specs=[
                whole(*panel.shape),
                pl.BlockSpec((group, touches, rows, rows), lambda i, *_: (i, 0, 0, 0)),
            ],
            out_specs=(
                pl.BlockSpec((scen_rows, group * rows), lambda i, *_: (0, i)),
                whole(8, rows),
            ),
        ),
        compiler_params=params(SMALL_VMEM),
        cost_estimate=pl.CostEstimate(
            flops=2 * scen_rows * blocks.size, bytes_accessed=2 * blocks.size, transcendentals=0
        ),
        name="local_adjoint",
    )(index, panel, blocks)


def head_step(places, panels, heads, pulled, flows, costs, risk, sums):
    arc_blks, rows, _ = heads.shape
    scen_rows = flows.shape[0]
    peers = len(panels)
    node_blks = panels[0].shape[0]
    group = HEAD_GROUP
    steps = arc_blks // group
    kept = (node_blks, scen_rows, rows)
    sent = [kept] * (peers // 2)
    sent[-1] = (node_blks + 1, scen_rows, rows)
    arcs = pl.BlockSpec((scen_rows, group * rows), lambda i, *_: (0, i))
    results = pl.pallas_call(
        functools.partial(head_kernel, group, steps, peers),
        out_shape=[
            jax.ShapeDtypeStruct(flows.shape, jnp.float32),
            jax.ShapeDtypeStruct(flows.shape, jnp.bfloat16),
            jax.ShapeDtypeStruct(sums[0].shape, jnp.float32),
        ]
        + [jax.ShapeDtypeStruct(kept, jnp.float32)] * (peers // 2)
        + [jax.ShapeDtypeStruct(shape, jnp.bfloat16) for shape in sent],
        grid_spec=pltpu.PrefetchScalarGridSpec(
            num_scalar_prefetch=1,
            grid=(steps,),
            in_specs=[whole(*panels[0].shape)] * peers
            + [
                pl.BlockSpec((group, rows, rows), lambda i, *_: (i, 0, 0)),
                arcs,
                arcs,
                pl.BlockSpec((1, group * rows), lambda i, *_: (0, i)),
                whole(scen_rows, rows),
                whole(*sums[0].shape),
                whole(*sums[0].shape),
            ],
            out_specs=[arcs, arcs, whole(*sums[0].shape)]
            + [whole(*kept)] * (peers // 2)
            + [whole(*shape) for shape in sent],
            scratch_shapes=[
                pltpu.VMEM((peers * node_blks, scen_rows, rows), jnp.bfloat16),
                pltpu.VMEM((peers * node_blks, scen_rows, rows), jnp.float32),
                pltpu.VMEM((scen_rows, group * rows), jnp.float32),
                pltpu.VMEM((scen_rows, rows), jnp.float32),
            ],
        ),
        compiler_params=params((4 + peers + peers // 4) * MIB),
        cost_estimate=pl.CostEstimate(
            flops=4 * scen_rows * heads.size,
            bytes_accessed=2 * heads.size + 14 * flows.size + 4 * peers * panels[0].size,
            transcendentals=0,
        ),
        name="head_step",
    )(places, *panels, heads, pulled, flows, costs, risk, *sums)
    half = peers // 2
    kept = dict(zip(inner(peers), results[3 : 3 + half]))
    sends = dict(zip(leaves(peers), results[3 + half :]))
    return *results[:3], kept, sends


def small_cost(*arrays):
    size = sum(a.size for a in arrays)
    return pl.CostEstimate(flops=size, bytes_accessed=2 * size, transcendentals=0)


def fold(tops, loss, sums, after):
    node_blks, scen_rows, rows = tops[0][0].shape
    with_loss = loss is not None
    operands = [array for kept, arrived in tops for array in (kept, *arrived)]
    operands += ([loss] if with_loss else []) + list(sums)
    vmem = pl.BlockSpec(memory_space=pltpu.VMEM)
    out_shape = [
        jax.ShapeDtypeStruct((node_blks + (with_loss and number == 0), scen_rows, rows), jnp.bfloat16)
        for number in range(len(tops))
    ]
    out_shape += [jax.ShapeDtypeStruct(array.shape, array.dtype) for array in sums[:1]]
    counts = [len(arrived) for _, arrived in tops]
    results = pl.pallas_call(
        functools.partial(fold_kernel, counts, with_loss, len(sums), len(after)),
        out_shape=out_shape,
        in_specs=[vmem] * len(operands) + [pl.BlockSpec(memory_space=pl.ANY)] * len(after),
        out_specs=[vmem] * len(out_shape),
        compiler_params=pltpu.CompilerParams(vmem_limit_bytes=SMALL_VMEM),
        cost_estimate=small_cost(*operands),
        name="fold",
    )(*operands, *after)
    return results[: len(tops)], results[len(tops) :]


def settle(kept, arrived, loss, base, risk, excess, level, sums, arc_total, scen_total, last):
    node_blks, scen_rows, rows = base.shape
    return pl.pallas_call(
        functools.partial(settle_kernel, len(arrived), arc_total, scen_total, last),
        out_shape=(
            jax.ShapeDtypeStruct((scen_rows, node_blks * rows) if last else base.shape, jnp.float32),
            jax.ShapeDtypeStruct(base.shape, jnp.bfloat16),
            jax.ShapeDtypeStruct((1, scen_rows) if last else risk.shape, jnp.float32),
            jax.ShapeDtypeStruct((1, scen_rows) if last else risk.shape, jnp.float32),
            jax.ShapeDtypeStruct((1, 1) if last else level.shape, jnp.float32),
            jax.ShapeDtypeStruct(level.shape, jnp.float32),
        ),
        compiler_params=pltpu.CompilerParams(vmem_limit_bytes=SMALL_VMEM),
        cost_estimate=small_cost(kept, *arrived, base),
        name="settle",
    )(kept, *arrived, loss, base, risk, excess, level, *sums)


def local_forward(index, bar, blocks, duals, demand):
    arc_blks, touches, rows, _ = blocks.shape
    scen_rows = bar.shape[0]
    group = GROUP
    steps = arc_blks // group
    return pl.pallas_call(
        functools.partial(local_forward_kernel, touches, group, steps),
        out_shape=jax.ShapeDtypeStruct(duals.shape, jnp.float32),
        grid_spec=pltpu.PrefetchScalarGridSpec(
            num_scalar_prefetch=1,
            grid=(steps,),
            in_specs=[
                pl.BlockSpec((scen_rows, group * rows), lambda i, *_: (0, i)),
                pl.BlockSpec((group, touches, rows, rows), lambda i, *_: (i, 0, 0, 0)),
                whole(*duals.shape),
                whole(*demand.shape),
            ],
            out_specs=whole(*duals.shape),
            scratch_shapes=[pltpu.VMEM(duals.shape, jnp.float32)],
        ),
        compiler_params=params(SMALL_VMEM),
        cost_estimate=pl.CostEstimate(
            flops=2 * scen_rows * blocks.size, bytes_accessed=2 * blocks.size, transcendentals=0
        ),
        name="local_forward",
    )(index, bar, blocks, duals, demand)


def relay(arrived, risk_sum, after):
    def kernel(arrived_ref, sum_ref, *refs):
        arrived_out, sum_out = refs[-2:]
        arrived_out[...] = arrived_ref[...]
        sum_out[...] = sum_ref[...]

    vmem = pl.BlockSpec(memory_space=pltpu.VMEM)
    return pl.pallas_call(
        kernel,
        out_shape=(
            jax.ShapeDtypeStruct(arrived.shape, arrived.dtype),
            jax.ShapeDtypeStruct(risk_sum.shape, risk_sum.dtype),
        ),
        in_specs=[vmem, vmem] + [pl.BlockSpec(memory_space=pl.ANY)] * len(after),
        out_specs=(vmem, vmem),
        compiler_params=pltpu.CompilerParams(vmem_limit_bytes=SMALL_VMEM),
        cost_estimate=small_cost(arrived),
        name="relay",
    )(arrived, risk_sum, *after)


def prepare_kernel(node_blks, risk_ref, excess_ref, level_ref, head_ref, *refs):
    risk_out, excess_out, level_out, sum_out, places_out = refs[-5:]
    head = head_ref[...]
    owner = lax.div(head, node_blks)
    distance = jnp.bitwise_xor(owner, lax.axis_index("net"))
    places_out[...] = head + (distance - owner) * node_blks
    scen_rows = risk_out.shape[0]
    square = (scen_rows, scen_rows)
    same = lax.broadcasted_iota(jnp.int32, square, 0) == lax.broadcasted_iota(jnp.int32, square, 1)
    for row_ref, out in ((risk_ref, risk_out), (excess_ref, excess_out)):
        column = jnp.sum(jnp.where(same, row_ref[...], 0.0), axis=1, keepdims=True)
        out[...] = jnp.broadcast_to(column, out.shape)
    level_out[...] = jnp.broadcast_to(level_ref[...], level_out.shape)
    sum_out[...] = add_rows(risk_out[...], sum_out.shape)


def prepare(risk, excess, level, heads, rows, node_blks, after):
    wide, flat = (risk.shape[0], rows), (8, rows)
    return pl.pallas_call(
        functools.partial(prepare_kernel, node_blks),
        out_shape=[jax.ShapeDtypeStruct(shape, jnp.float32) for shape in (wide, wide, flat, flat)]
        + [jax.ShapeDtypeStruct((1, heads.shape[0]), jnp.int32)],
        in_specs=[pl.BlockSpec(memory_space=pltpu.VMEM)] * 4
        + [pl.BlockSpec(memory_space=pl.ANY)] * len(after),
        compiler_params=pltpu.CompilerParams(vmem_limit_bytes=SMALL_VMEM),
        cost_estimate=small_cost(risk),
        name="prepare",
    )(risk.reshape(1, -1), excess.reshape(1, -1), level.reshape(1, 1), heads.reshape(1, -1), *after)


def swap(value, axis, distance):
    size = lax.axis_size(axis)
    return lax.ppermute(value, axis, [(i, i ^ distance) for i in range(size)])


def gather_panels(own, risk_sum, after):
    peers = lax.axis_size("net")
    panels = [own] + [None] * (peers - 1)
    order = sorted(range(1, peers), key=lambda k: (k.bit_count(), -k))
    for distance in order:
        hop = last_hop(distance)
        panels[distance] = swap(panels[distance ^ hop], "net", hop)
        if distance == 1:
            far = peers // 2
            panels[far], risk_sum = relay(panels[far], risk_sum, after)
    return panels, risk_sum


def per_device(
    arc_flows,
    node_duals,
    demand,
    excess,
    risk_duals,
    threshold,
    arc_costs,
    local_blocks,
    head_blocks,
    local_index,
    head_index,
):
    rows = local_blocks.shape[-1]
    scen_rows = arc_flows.shape[0]
    node_blks = node_duals.shape[1] // rows
    net_size = lax.axis_size("net")
    arc_total = arc_flows.shape[1] * net_size
    scen_total = scen_rows * lax.axis_size("scen")
    costs = arc_costs.reshape(1, -1)
    touched = local_index.T
    scen_size = lax.axis_size("scen")
    duals = node_duals.reshape(scen_rows, node_blks, rows).transpose(1, 0, 2)
    half = duals.astype(jnp.bfloat16)
    flows = arc_flows
    strides = [1 << bit for bit in range(1, scen_size.bit_length() - 1)][::-1]
    for iteration in range(ROUNDS):
        first, last = iteration == 0, iteration == ROUNDS - 1
        pulled, token = local_adjoint(touched, half, local_blocks)
        panels, risk_sum = gather_panels(half, token if first else risk_sum, (token,))
        if first:
            risk, excess_now, level, risk_sum, places = prepare(
                risk_duals,
                excess,
                threshold,
                head_index,
                rows,
                node_blks,
                (panels[net_size // 2], head_blocks, arc_flows),
            )
            places = places.reshape(-1)
        sums = (risk_sum, swap(risk_sum, "scen", 1))
        flows, bar, risk_sum, kept, sends = head_step(
            places, panels, head_blocks, pulled, flows, costs, risk, sums
        )
        base = local_forward(touched, bar, local_blocks, duals, demand)
        tops = sorted(inner(net_size), key=lambda k: (-k.bit_count(), -k))[:-1]
        groups = [(top,) for top in tops if top != 1] + [(1,)]
        loss, loss_top = sends[net_size - 1], net_size - 1
        ahead = {k: swap(sends[k], "net", last_hop(k)) for k in (5, 2)}
        after = (ahead[5], ahead[2], base)
        for group in groups:
            terms = []
            for top in group:
                below = sorted(children(top, net_size))
                terms.append(
                    (
                        kept[top],
                        [ahead[k] if k in ahead else swap(sends[k], "net", last_hop(k)) for k in below],
                    )
                )
            chain = loss_top ^ last_hop(loss_top) == group[0]
            sums = (risk_sum,) if group[0] == tops[0] else ()
            if group == (1,):
                after = (loss,)
            if group[0] == net_size // 2:
                after = risk_sums[1:]
            folded, passed = fold(terms, loss if chain else None, sums, after)
            sends.update(zip(group, folded))
            after = ()
            if chain:
                loss_top, loss = group[0], folded[0]
            if sums:
                (risk_sum,) = passed
                for stride in strides[:-1]:
                    risk_sum = risk_sum + swap(risk_sum, "scen", stride)
                risk_sums = (risk_sum, swap(risk_sum, "scen", strides[-1]))
        below = sorted(children(0, net_size))
        arrived = [ahead[k] if k in ahead else swap(sends[k], "net", last_hop(k)) for k in below]
        duals, half, risk, excess_now, level, risk_sum = settle(
            kept[0],
            arrived,
            loss,
            base,
            risk,
            excess_now,
            level,
            risk_sums,
            arc_total,
            scen_total,
            last,
        )
    return (flows, duals, excess_now.reshape(-1), risk.reshape(-1), level.reshape(-1))


def solution(mesh):
    placed = (
        P("scen", "net"),
        P("scen", "net"),
        P("scen", "net"),
        P("scen"),
        P("scen"),
        P(),
        P("net"),
        P("net", None, None, None),
        P("net", None, None),
        P("net", None),
        P("net"),
    )
    return jax.shard_map(
        per_device,
        mesh=mesh,
        in_specs=placed,
        out_specs=(P("scen", "net"), P("scen", "net"), P("scen"), P("scen"), P()),
        check_vma=False,
    )
```

```python
import functools

import jax
import jax.numpy as jnp
from jax import lax
from jax.experimental import pallas as pl
from jax.experimental.pallas import tpu as pltpu
from jax.sharding import PartitionSpec as P

ROUNDS = 3

primal_step = 0.5
dual_step = 0.5
risk_step = 1.0
tail_weight = 2.0

MIB = 1024 * 1024
GROUP = 8
HEAD_GROUP = 32
SMALL_VMEM = 6 * MIB


def contract_last(left, right):
    return lax.dot_general(
        left, right, (((1,), (1,)), ((), ())), preferred_element_type=jnp.float32
    )


def local_adjoint_kernel(
    touches, group, index_ref, panel_ref, blocks_ref, out_ref, token_ref
):
    token_ref[...] = jnp.zeros_like(token_ref)
    rows = blocks_ref.shape[-1]
    first = pl.program_id(0) * group
    for member in range(group):
        left = jnp.concatenate(
            [panel_ref[index_ref[k, first + member]] for k in range(touches)], axis=1
        )
        right = jnp.concatenate([blocks_ref[member, k] for k in range(touches)], axis=1)
        out_ref[:, member * rows : (member + 1) * rows] = contract_last(left, right)


def to_parts(column, shape):
    high = column.astype(jnp.bfloat16).astype(jnp.float32)
    rest = column - high
    middle = rest.astype(jnp.bfloat16).astype(jnp.float32)
    low = rest - middle
    lane = lax.broadcasted_iota(jnp.int32, shape, 1)
    packed = jnp.where(
        lane == 0, high, jnp.where(lane == 1, middle, jnp.where(lane == 2, low, 0.0))
    )
    return packed.astype(jnp.bfloat16)


def from_parts(parts):
    return jnp.sum(parts.astype(jnp.float32), axis=1, keepdims=True)


def head_kernel(group, steps, peers, index_ref, *refs):
    panels, refs = refs[:peers], refs[peers:]
    heads_ref, pulled_ref, flows_ref, costs_ref, risk_ref, sum_ref, other_ref = refs[:7]
    flows_out, bar_out, sum_out, refs = *refs[7:10], refs[10:]
    kept, refs = refs[: peers // 2], refs[peers // 2 :]
    sends, (panel, terms, pulled, loss) = refs[:-4], refs[-4:]
    rows = heads_ref.shape[-1]
    node_blks = panels[0].shape[0]
    step = pl.program_id(0)
    first = step * group

    @pl.when(step == 0)
    def _():
        terms[...] = jnp.zeros_like(terms)
        loss[...] = jnp.zeros_like(loss)
        sum_out[...] = sum_ref[...] + other_ref[...]
        for peer in range(peers):
            panel[peer * node_blks : (peer + 1) * node_blks] = panels[peer][...]

    places = [index_ref[first + member] for member in range(group)]
    spans = [slice(member * rows, (member + 1) * rows) for member in range(group)]
    for member in range(group):
        pulled[:, spans[member]] = contract_last(panel[places[member]], heads_ref[member])
    risk = risk_ref[...]
    loss_sum = jnp.zeros_like(risk)
    for columns in spans:
        flows = flows_ref[:, columns]
        cost = costs_ref[:, columns]
        gradient = risk * cost - (pulled[:, columns] + pulled_ref[:, columns])
        flows_new = jnp.maximum(flows - primal_step * gradient, 0.0)
        bar = 2.0 * flows_new - flows
        flows_out[:, columns] = flows_new
        loss_sum += cost * bar
        bar_out[:, columns] = bar.astype(jnp.bfloat16)
    loss[...] += loss_sum
    products = [
        jnp.dot(bar_out[:, spans[m]], heads_ref[m], preferred_element_type=jnp.float32)
        for m in range(group)
    ]
    for member in range(group):
        terms[places[member]] += products[member]

    @pl.when(step == steps - 1)
    def _():
        loss_parts = to_parts(jnp.sum(loss[...], axis=1, keepdims=True), loss.shape)
        for out, distance in zip(kept, inner(peers)):
            out[...] = terms[distance * node_blks : (distance + 1) * node_blks]
        for out, distance in zip(sends, leaves(peers)):
            out[:node_blks] = terms[distance * node_blks : (distance + 1) * node_blks].astype(
                jnp.bfloat16
            )
        sends[-1][node_blks] = loss_parts


def last_hop(distance):
    return 2 if distance == 3 else distance & -distance


def children(distance, peers):
    return [k for k in range(1, peers) if k ^ last_hop(k) == distance]


def inner(peers):
    return [k for k in range(peers) if children(k, peers)]


def leaves(peers):
    return [k for k in range(peers) if not children(k, peers)]


def pair_sum(values):
    while len(values) > 1:
        values = [a + b for a, b in zip(values[::2], values[1::2])] + values[len(values) // 2 * 2 :]
    return values[0]


def fold_kernel(counts, with_loss, sums, after, *refs):
    inputs, refs = refs[: sum(counts) + len(counts)], refs[sum(counts) + len(counts) :]
    if with_loss:
        loss_ref, refs = refs[0], refs[1:]
    sum_in, refs = refs[:sums], refs[sums + after :]
    outs, sum_out = refs[: len(counts)], refs[len(counts) :]
    node_blks = inputs[0].shape[0]
    for number, (count, out_ref) in enumerate(zip(counts, outs)):
        kept_ref, arrived, inputs = inputs[0], inputs[1 : 1 + count], inputs[1 + count :]
        for block in range(node_blks):
            total = pair_sum([ref[block].astype(jnp.float32) for ref in arrived])
            out_ref[block] = (kept_ref[block] + total).astype(jnp.bfloat16)
        if with_loss and number == 0:
            both = from_parts(loss_ref[loss_ref.shape[0] - 1]) + from_parts(arrived[-1][node_blks])
            out_ref[node_blks] = to_parts(both, loss_ref.shape[1:])
    for out in sum_out:
        out[...] = functools.reduce(jnp.add, [ref[...] for ref in sum_in])


def next_level(level, risk_total, scen_total):
    level_new = level - primal_step * (1.0 - risk_total / scen_total)
    return level_new, 2.0 * level_new - level


def add_rows(values, shape):
    return jnp.broadcast_to(jnp.sum(values, axis=0, keepdims=True), shape)


def as_row(values):
    rows = values.shape[0]
    picked = lax.broadcasted_iota(jnp.int32, values.shape, 0) == lax.broadcasted_iota(
        jnp.int32, values.shape, 1
    )
    return jnp.sum(jnp.where(picked, values, 0.0), axis=0, keepdims=True)[:, :rows]


def settle_kernel(count, arc_total, scen_total, last, *refs):
    kept_ref, arrived, refs = refs[0], refs[1 : 1 + count], refs[1 + count :]
    loss_ref, base_ref, risk_ref, excess_ref, level_ref, sum_ref, other_ref = refs[:7]
    duals_out, half_out, risk_out, excess_out, level_out, sum_out = refs[7:]
    node_blks, _, rows = base_ref.shape
    for block in range(node_blks):
        total = kept_ref[block] + pair_sum([ref[block].astype(jnp.float32) for ref in arrived])
        duals = base_ref[block] - dual_step * total
        if last:
            duals_out[:, block * rows : (block + 1) * rows] = duals
        else:
            duals_out[block] = duals
            half_out[block] = duals.astype(jnp.bfloat16)
    losses = from_parts(loss_ref[node_blks]) + from_parts(arrived[-1][node_blks])
    losses = losses / arc_total
    risk = risk_ref[...]
    excess = excess_ref[...]
    excess_new = jnp.maximum(excess - primal_step * (tail_weight - risk), 0.0)
    excess_bar = 2.0 * excess_new - excess
    risk_new = risk + risk_step * (losses - excess_bar)
    risk_total = sum_ref[...] + other_ref[...]
    level_new, level_bar = next_level(level_ref[...], risk_total, scen_total)
    risk_new = jnp.maximum(risk_new - risk_step * level_bar[:1], 0.0)
    if last:
        risk_out[...] = as_row(risk_new)
        excess_out[...] = as_row(excess_new)
        level_out[...] = level_new[:1, :1]
    else:
        risk_out[...] = risk_new
        excess_out[...] = excess_new
        level_out[...] = level_new
        sum_out[...] = add_rows(risk_new, sum_out.shape)


def local_forward_kernel(
    touches,
    group,
    steps,
    index_ref,
    bar_ref,
    blocks_ref,
    duals_ref,
    demand_ref,
    out_ref,
    total,
):
    rows = blocks_ref.shape[-1]
    step = pl.program_id(0)
    first = step * group

    @pl.when(step == 0)
    def _():
        total[...] = jnp.zeros_like(total)

    for member in range(group):
        right = jnp.concatenate([blocks_ref[member, k] for k in range(touches)], axis=1)
        products = jnp.dot(
            bar_ref[:, member * rows : (member + 1) * rows],
            right,
            preferred_element_type=jnp.float32,
        )
        for k in range(touches):
            place = index_ref[k, first + member]
            total[place] += products[:, k * rows : (k + 1) * rows]

    @pl.when(step == steps - 1)
    def _():
        for block in range(total.shape[0]):
            demand = demand_ref[:, block * rows : (block + 1) * rows]
            out_ref[block] = duals_ref[block] + dual_step * (demand - total[block])


def whole(*shape):
    return pl.BlockSpec(shape, lambda i, *_: (0,) * len(shape))


def params(limit):
    return pltpu.CompilerParams(dimension_semantics=("arbitrary",), vmem_limit_bytes=limit)


def local_adjoint(index, panel, blocks):
    arc_blks, touches, rows, _ = blocks.shape
    scen_rows = panel.shape[1]
    group = GROUP
    return pl.pallas_call(
        functools.partial(local_adjoint_kernel, touches, group),
        out_shape=(
            jax.ShapeDtypeStruct((scen_rows, arc_blks * rows), jnp.float32),
            jax.ShapeDtypeStruct((8, rows), jnp.float32),
        ),
        grid_spec=pltpu.PrefetchScalarGridSpec(
            num_scalar_prefetch=1,
            grid=(arc_blks // group,),
            in_specs=[
                whole(*panel.shape),
                pl.BlockSpec((group, touches, rows, rows), lambda i, *_: (i, 0, 0, 0)),
            ],
            out_specs=(
                pl.BlockSpec((scen_rows, group * rows), lambda i, *_: (0, i)),
                whole(8, rows),
            ),
        ),
        compiler_params=params(SMALL_VMEM),
        cost_estimate=pl.CostEstimate(
            flops=2 * scen_rows * blocks.size, bytes_accessed=2 * blocks.size, transcendentals=0
        ),
        name="local_adjoint",
    )(index, panel, blocks)


def head_step(places, panels, heads, pulled, flows, costs, risk, sums):
    arc_blks, rows, _ = heads.shape
    scen_rows = flows.shape[0]
    peers = len(panels)
    node_blks = panels[0].shape[0]
    group = HEAD_GROUP
    steps = arc_blks // group
    kept = (node_blks, scen_rows, rows)
    sent = [kept] * (peers // 2)
    sent[-1] = (node_blks + 1, scen_rows, rows)
    arcs = pl.BlockSpec((scen_rows, group * rows), lambda i, *_: (0, i))
    results = pl.pallas_call(
        functools.partial(head_kernel, group, steps, peers),
        out_shape=[
            jax.ShapeDtypeStruct(flows.shape, jnp.float32),
            jax.ShapeDtypeStruct(flows.shape, jnp.bfloat16),
            jax.ShapeDtypeStruct(sums[0].shape, jnp.float32),
        ]
        + [jax.ShapeDtypeStruct(kept, jnp.float32)] * (peers // 2)
        + [jax.ShapeDtypeStruct(shape, jnp.bfloat16) for shape in sent],
        grid_spec=pltpu.PrefetchScalarGridSpec(
            num_scalar_prefetch=1,
            grid=(steps,),
            in_specs=[whole(*panels[0].shape)] * peers
            + [
                pl.BlockSpec((group, rows, rows), lambda i, *_: (i, 0, 0)),
                arcs,
                arcs,
                pl.BlockSpec((1, group * rows), lambda i, *_: (0, i)),
                whole(scen_rows, rows),
                whole(*sums[0].shape),
                whole(*sums[0].shape),
            ],
            out_specs=[arcs, arcs, whole(*sums[0].shape)]
            + [whole(*kept)] * (peers // 2)
            + [whole(*shape) for shape in sent],
            scratch_shapes=[
                pltpu.VMEM((peers * node_blks, scen_rows, rows), jnp.bfloat16),
                pltpu.VMEM((peers * node_blks, scen_rows, rows), jnp.float32),
                pltpu.VMEM((scen_rows, group * rows), jnp.float32),
                pltpu.VMEM((scen_rows, rows), jnp.float32),
            ],
        ),
        compiler_params=params((4 + peers + peers // 4) * MIB),
        cost_estimate=pl.CostEstimate(
            flops=4 * scen_rows * heads.size,
            bytes_accessed=2 * heads.size + 14 * flows.size + 4 * peers * panels[0].size,
            transcendentals=0,
        ),
        name="head_step",
    )(places, *panels, heads, pulled, flows, costs, risk, *sums)
    half = peers // 2
    kept = dict(zip(inner(peers), results[3 : 3 + half]))
    sends = dict(zip(leaves(peers), results[3 + half :]))
    return *results[:3], kept, sends


def small_cost(*arrays):
    size = sum(a.size for a in arrays)
    return pl.CostEstimate(flops=size, bytes_accessed=2 * size, transcendentals=0)


def fold(tops, loss, sums, after):
    node_blks, scen_rows, rows = tops[0][0].shape
    with_loss = loss is not None
    operands = [array for kept, arrived in tops for array in (kept, *arrived)]
    operands += ([loss] if with_loss else []) + list(sums)
    vmem = pl.BlockSpec(memory_space=pltpu.VMEM)
    out_shape = [
        jax.ShapeDtypeStruct((node_blks + (with_loss and number == 0), scen_rows, rows), jnp.bfloat16)
        for number in range(len(tops))
    ]
    out_shape += [jax.ShapeDtypeStruct(array.shape, array.dtype) for array in sums[:1]]
    counts = [len(arrived) for _, arrived in tops]
    results = pl.pallas_call(
        functools.partial(fold_kernel, counts, with_loss, len(sums), len(after)),
        out_shape=out_shape,
        in_specs=[vmem] * len(operands) + [pl.BlockSpec(memory_space=pl.ANY)] * len(after),
        out_specs=[vmem] * len(out_shape),
        compiler_params=pltpu.CompilerParams(vmem_limit_bytes=SMALL_VMEM),
        cost_estimate=small_cost(*operands),
        name="fold",
    )(*operands, *after)
    return results[: len(tops)], results[len(tops) :]


def settle(kept, arrived, loss, base, risk, excess, level, sums, arc_total, scen_total, last):
    node_blks, scen_rows, rows = base.shape
    return pl.pallas_call(
        functools.partial(settle_kernel, len(arrived), arc_total, scen_total, last),
        out_shape=(
            jax.ShapeDtypeStruct((scen_rows, node_blks * rows) if last else base.shape, jnp.float32),
            jax.ShapeDtypeStruct(base.shape, jnp.bfloat16),
            jax.ShapeDtypeStruct((1, scen_rows) if last else risk.shape, jnp.float32),
            jax.ShapeDtypeStruct((1, scen_rows) if last else risk.shape, jnp.float32),
            jax.ShapeDtypeStruct((1, 1) if last else level.shape, jnp.float32),
            jax.ShapeDtypeStruct(level.shape, jnp.float32),
        ),
        compiler_params=pltpu.CompilerParams(vmem_limit_bytes=SMALL_VMEM),
        cost_estimate=small_cost(kept, *arrived, base),
        name="settle",
    )(kept, *arrived, loss, base, risk, excess, level, *sums)


def local_forward(index, bar, blocks, duals, demand):
    arc_blks, touches, rows, _ = blocks.shape
    scen_rows = bar.shape[0]
    group = GROUP
    steps = arc_blks // group
    return pl.pallas_call(
        functools.partial(local_forward_kernel, touches, group, steps),
        out_shape=jax.ShapeDtypeStruct(duals.shape, jnp.float32),
        grid_spec=pltpu.PrefetchScalarGridSpec(
            num_scalar_prefetch=1,
            grid=(steps,),
            in_specs=[
                pl.BlockSpec((scen_rows, group * rows), lambda i, *_: (0, i)),
                pl.BlockSpec((group, touches, rows, rows), lambda i, *_: (i, 0, 0, 0)),
                whole(*duals.shape),
                whole(*demand.shape),
            ],
            out_specs=whole(*duals.shape),
            scratch_shapes=[pltpu.VMEM(duals.shape, jnp.float32)],
        ),
        compiler_params=params(SMALL_VMEM),
        cost_estimate=pl.CostEstimate(
            flops=2 * scen_rows * blocks.size, bytes_accessed=2 * blocks.size, transcendentals=0
        ),
        name="local_forward",
    )(index, bar, blocks, duals, demand)


def relay(arrived, risk_sum, after):
    def kernel(arrived_ref, sum_ref, *refs):
        arrived_out, sum_out = refs[-2:]
        arrived_out[...] = arrived_ref[...]
        sum_out[...] = sum_ref[...]

    vmem = pl.BlockSpec(memory_space=pltpu.VMEM)
    return pl.pallas_call(
        kernel,
        out_shape=(
            jax.ShapeDtypeStruct(arrived.shape, arrived.dtype),
            jax.ShapeDtypeStruct(risk_sum.shape, risk_sum.dtype),
        ),
        in_specs=[vmem, vmem] + [pl.BlockSpec(memory_space=pl.ANY)] * len(after),
        out_specs=(vmem, vmem),
        compiler_params=pltpu.CompilerParams(vmem_limit_bytes=SMALL_VMEM),
        cost_estimate=small_cost(arrived),
        name="relay",
    )(arrived, risk_sum, *after)


def prepare_kernel(node_blks, risk_ref, excess_ref, level_ref, head_ref, *refs):
    risk_out, excess_out, level_out, sum_out, places_out = refs[-5:]
    head = head_ref[...]
    owner = lax.div(head, node_blks)
    distance = jnp.bitwise_xor(owner, lax.axis_index("net"))
    places_out[...] = head + (distance - owner) * node_blks
    scen_rows = risk_out.shape[0]
    square = (scen_rows, scen_rows)
    same = lax.broadcasted_iota(jnp.int32, square, 0) == lax.broadcasted_iota(jnp.int32, square, 1)
    for row_ref, out in ((risk_ref, risk_out), (excess_ref, excess_out)):
        column = jnp.sum(jnp.where(same, row_ref[...], 0.0), axis=1, keepdims=True)
        out[...] = jnp.broadcast_to(column, out.shape)
    level_out[...] = jnp.broadcast_to(level_ref[...], level_out.shape)
    sum_out[...] = add_rows(risk_out[...], sum_out.shape)


def prepare(risk, excess, level, heads, rows, node_blks, after):
    wide, flat = (risk.shape[0], rows), (8, rows)
    return pl.pallas_call(
        functools.partial(prepare_kernel, node_blks),
        out_shape=[jax.ShapeDtypeStruct(shape, jnp.float32) for shape in (wide, wide, flat, flat)]
        + [jax.ShapeDtypeStruct((1, heads.shape[0]), jnp.int32)],
        in_specs=[pl.BlockSpec(memory_space=pltpu.VMEM)] * 4
        + [pl.BlockSpec(memory_space=pl.ANY)] * len(after),
        compiler_params=pltpu.CompilerParams(vmem_limit_bytes=SMALL_VMEM),
        cost_estimate=small_cost(risk),
        name="prepare",
    )(risk.reshape(1, -1), excess.reshape(1, -1), level.reshape(1, 1), heads.reshape(1, -1), *after)


def swap(value, axis, distance):
    size = lax.axis_size(axis)
    return lax.ppermute(value, axis, [(i, i ^ distance) for i in range(size)])


def gather_panels(own, risk_sum, after):
    peers = lax.axis_size("net")
    panels = [own] + [None] * (peers - 1)
    order = sorted(range(1, peers), key=lambda k: (k.bit_count(), -k))
    for distance in order:
        hop = last_hop(distance)
        panels[distance] = swap(panels[distance ^ hop], "net", hop)
        if distance == 1:
            far = peers // 2
            panels[far], risk_sum = relay(panels[far], risk_sum, after)
    return panels, risk_sum


def per_device(
    arc_flows,
    node_duals,
    demand,
    excess,
    risk_duals,
    threshold,
    arc_costs,
    local_blocks,
    head_blocks,
    local_index,
    head_index,
):
    rows = local_blocks.shape[-1]
    scen_rows = arc_flows.shape[0]
    node_blks = node_duals.shape[1] // rows
    net_size = lax.axis_size("net")
    arc_total = arc_flows.shape[1] * net_size
    scen_total = scen_rows * lax.axis_size("scen")
    costs = arc_costs.reshape(1, -1)
    touched = local_index.T
    scen_size = lax.axis_size("scen")
    duals = node_duals.reshape(scen_rows, node_blks, rows).transpose(1, 0, 2)
    half = duals.astype(jnp.bfloat16)
    flows = arc_flows
    strides = [1 << bit for bit in range(1, scen_size.bit_length() - 1)][::-1]
    for iteration in range(ROUNDS):
        first, last = iteration == 0, iteration == ROUNDS - 1
        pulled, token = local_adjoint(touched, half, local_blocks)
        panels, risk_sum = gather_panels(half, token if first else risk_sum, (token,))
        if first:
            risk, excess_now, level, risk_sum, places = prepare(
                risk_duals,
                excess,
                threshold,
                head_index,
                rows,
                node_blks,
                (panels[net_size // 2], head_blocks, arc_flows),
            )
            places = places.reshape(-1)
        sums = (risk_sum, swap(risk_sum, "scen", 1))
        flows, bar, risk_sum, kept, sends = head_step(
            places, panels, head_blocks, pulled, flows, costs, risk, sums
        )
        base = local_forward(touched, bar, local_blocks, duals, demand)
        tops = sorted(inner(net_size), key=lambda k: (-k.bit_count(), -k))[:-1]
        groups = [(top,) for top in tops if top != 1] + [(1,)]
        loss, loss_top = sends[net_size - 1], net_size - 1
        ahead = {k: swap(sends[k], "net", last_hop(k)) for k in (2,)}
        after = (ahead[2], base)
        for group in groups:
            terms = []
            for top in group:
                below = sorted(children(top, net_size))
                terms.append(
                    (
                        kept[top],
                        [ahead[k] if k in ahead else swap(sends[k], "net", last_hop(k)) for k in below],
                    )
                )
            chain = loss_top ^ last_hop(loss_top) == group[0]
            sums = (risk_sum,) if group[0] == tops[0] else ()
            if group == (1,):
                after = (loss,)
            if group[0] == net_size // 2:
                after = risk_sums[1:]
            folded, passed = fold(terms, loss if chain else None, sums, after)
            sends.update(zip(group, folded))
            after = ()
            if chain:
                loss_top, loss = group[0], folded[0]
            if sums:
                (risk_sum,) = passed
                for stride in strides[:-1]:
                    risk_sum = risk_sum + swap(risk_sum, "scen", stride)
                risk_sums = (risk_sum, swap(risk_sum, "scen", strides[-1]))
        below = sorted(children(0, net_size))
        arrived = [ahead[k] if k in ahead else swap(sends[k], "net", last_hop(k)) for k in below]
        duals, half, risk, excess_now, level, risk_sum = settle(
            kept[0],
            arrived,
            loss,
            base,
            risk,
            excess_now,
            level,
            risk_sums,
            arc_total,
            scen_total,
            last,
        )
    return (flows, duals, excess_now.reshape(-1), risk.reshape(-1), level.reshape(-1))


def solution(mesh):
    placed = (
        P("scen", "net"),
        P("scen", "net"),
        P("scen", "net"),
        P("scen"),
        P("scen"),
        P(),
        P("net"),
        P("net", None, None, None),
        P("net", None, None),
        P("net", None),
        P("net"),
    )
    return jax.shard_map(
        per_device,
        mesh=mesh,
        in_specs=placed,
        out_specs=(P("scen", "net"), P("scen", "net"), P("scen"), P("scen"), P()),
        check_vma=False,
    )
```

```python
import functools

import jax
import jax.numpy as jnp
from jax import lax
from jax.experimental import pallas as pl
from jax.experimental.pallas import tpu as pltpu
from jax.sharding import PartitionSpec as P

ROUNDS = 3

primal_step = 0.5
dual_step = 0.5
risk_step = 1.0
tail_weight = 2.0

MIB = 1024 * 1024
GROUP = 8
HEAD_GROUP = 64
SMALL_VMEM = 6 * MIB


def contract_last(left, right):
    return lax.dot_general(
        left, right, (((1,), (1,)), ((), ())), preferred_element_type=jnp.float32
    )


def local_adjoint_kernel(
    touches, group, index_ref, panel_ref, blocks_ref, out_ref, token_ref
):
    token_ref[...] = jnp.zeros_like(token_ref)
    rows = blocks_ref.shape[-1]
    first = pl.program_id(0) * group
    for member in range(group):
        left = jnp.concatenate(
            [panel_ref[index_ref[k, first + member]] for k in range(touches)], axis=1
        )
        right = jnp.concatenate([blocks_ref[member, k] for k in range(touches)], axis=1)
        out_ref[:, member * rows : (member + 1) * rows] = contract_last(left, right)


def to_parts(column, shape):
    high = column.astype(jnp.bfloat16).astype(jnp.float32)
    rest = column - high
    middle = rest.astype(jnp.bfloat16).astype(jnp.float32)
    low = rest - middle
    lane = lax.broadcasted_iota(jnp.int32, shape, 1)
    packed = jnp.where(
        lane == 0, high, jnp.where(lane == 1, middle, jnp.where(lane == 2, low, 0.0))
    )
    return packed.astype(jnp.bfloat16)


def from_parts(parts):
    return jnp.sum(parts.astype(jnp.float32), axis=1, keepdims=True)


def head_kernel(group, steps, peers, index_ref, *refs):
    panels, refs = refs[:peers], refs[peers:]
    heads_ref, pulled_ref, flows_ref, costs_ref, risk_ref, sum_ref, other_ref = refs[:7]
    flows_out, bar_out, sum_out, refs = *refs[7:10], refs[10:]
    kept, refs = refs[: peers // 2], refs[peers // 2 :]
    sends, (panel, terms, pulled, loss) = refs[:-4], refs[-4:]
    rows = heads_ref.shape[-1]
    node_blks = panels[0].shape[0]
    step = pl.program_id(0)
    first = step * group

    @pl.when(step == 0)
    def _():
        terms[...] = jnp.zeros_like(terms)
        loss[...] = jnp.zeros_like(loss)
        sum_out[...] = sum_ref[...] + other_ref[...]
        for peer in range(peers):
            panel[peer * node_blks : (peer + 1) * node_blks] = panels[peer][...]

    places = [index_ref[first + member] for member in range(group)]
    spans = [slice(member * rows, (member + 1) * rows) for member in range(group)]
    for member in range(group):
        pulled[:, spans[member]] = contract_last(panel[places[member]], heads_ref[member])
    risk = risk_ref[...]
    loss_sum = jnp.zeros_like(risk)
    for columns in spans:
        flows = flows_ref[:, columns]
        cost = costs_ref[:, columns]
        gradient = risk * cost - (pulled[:, columns] + pulled_ref[:, columns])
        flows_new = jnp.maximum(flows - primal_step * gradient, 0.0)
        bar = 2.0 * flows_new - flows
        flows_out[:, columns] = flows_new
        loss_sum += cost * bar
        bar_out[:, columns] = bar.astype(jnp.bfloat16)
    loss[...] += loss_sum
    products = [
        jnp.dot(bar_out[:, spans[m]], heads_ref[m], preferred_element_type=jnp.float32)
        for m in range(group)
    ]
    for member in range(group):
        terms[places[member]] += products[member]

    @pl.when(step == steps - 1)
    def _():
        loss_parts = to_parts(jnp.sum(loss[...], axis=1, keepdims=True), loss.shape)
        for out, distance in zip(kept, inner(peers)):
            out[...] = terms[distance * node_blks : (distance + 1) * node_blks]
        for out, distance in zip(sends, leaves(peers)):
            out[:node_blks] = terms[distance * node_blks : (distance + 1) * node_blks].astype(
                jnp.bfloat16
            )
        sends[-1][node_blks] = loss_parts


def last_hop(distance):
    return 2 if distance == 3 else distance & -distance


def children(distance, peers):
    return [k for k in range(1, peers) if k ^ last_hop(k) == distance]


def inner(peers):
    return [k for k in range(peers) if children(k, peers)]


def leaves(peers):
    return [k for k in range(peers) if not children(k, peers)]


def pair_sum(values):
    while len(values) > 1:
        values = [a + b for a, b in zip(values[::2], values[1::2])] + values[len(values) // 2 * 2 :]
    return values[0]


def fold_kernel(counts, with_loss, sums, after, *refs):
    inputs, refs = refs[: sum(counts) + len(counts)], refs[sum(counts) + len(counts) :]
    if with_loss:
        loss_ref, refs = refs[0], refs[1:]
    sum_in, refs = refs[:sums], refs[sums + after :]
    outs, sum_out = refs[: len(counts)], refs[len(counts) :]
    node_blks = inputs[0].shape[0]
    for number, (count, out_ref) in enumerate(zip(counts, outs)):
        kept_ref, arrived, inputs = inputs[0], inputs[1 : 1 + count], inputs[1 + count :]
        for block in range(node_blks):
            total = pair_sum([ref[block].astype(jnp.float32) for ref in arrived])
            out_ref[block] = (kept_ref[block] + total).astype(jnp.bfloat16)
        if with_loss and number == 0:
            both = from_parts(loss_ref[loss_ref.shape[0] - 1]) + from_parts(arrived[-1][node_blks])
            out_ref[node_blks] = to_parts(both, loss_ref.shape[1:])
    for out in sum_out:
        out[...] = functools.reduce(jnp.add, [ref[...] for ref in sum_in])


def next_level(level, risk_total, scen_total):
    level_new = level - primal_step * (1.0 - risk_total / scen_total)
    return level_new, 2.0 * level_new - level


def add_rows(values, shape):
    return jnp.broadcast_to(jnp.sum(values, axis=0, keepdims=True), shape)


def as_row(values):
    rows = values.shape[0]
    picked = lax.broadcasted_iota(jnp.int32, values.shape, 0) == lax.broadcasted_iota(
        jnp.int32, values.shape, 1
    )
    return jnp.sum(jnp.where(picked, values, 0.0), axis=0, keepdims=True)[:, :rows]


def settle_kernel(count, arc_total, scen_total, last, *refs):
    kept_ref, arrived, refs = refs[0], refs[1 : 1 + count], refs[1 + count :]
    loss_ref, base_ref, risk_ref, excess_ref, level_ref, sum_ref, other_ref = refs[:7]
    duals_out, half_out, risk_out, excess_out, level_out, sum_out = refs[7:]
    node_blks, _, rows = base_ref.shape
    for block in range(node_blks):
        total = kept_ref[block] + pair_sum([ref[block].astype(jnp.float32) for ref in arrived])
        duals = base_ref[block] - dual_step * total
        if last:
            duals_out[:, block * rows : (block + 1) * rows] = duals
        else:
            duals_out[block] = duals
            half_out[block] = duals.astype(jnp.bfloat16)
    losses = from_parts(loss_ref[node_blks]) + from_parts(arrived[-1][node_blks])
    losses = losses / arc_total
    risk = risk_ref[...]
    excess = excess_ref[...]
    excess_new = jnp.maximum(excess - primal_step * (tail_weight - risk), 0.0)
    excess_bar = 2.0 * excess_new - excess
    risk_new = risk + risk_step * (losses - excess_bar)
    risk_total = sum_ref[...] + other_ref[...]
    level_new, level_bar = next_level(level_ref[...], risk_total, scen_total)
    risk_new = jnp.maximum(risk_new - risk_step * level_bar[:1], 0.0)
    if last:
        risk_out[...] = as_row(risk_new)
        excess_out[...] = as_row(excess_new)
        level_out[...] = level_new[:1, :1]
    else:
        risk_out[...] = risk_new
        excess_out[...] = excess_new
        level_out[...] = level_new
        sum_out[...] = add_rows(risk_new, sum_out.shape)


def local_forward_kernel(
    touches,
    group,
    steps,
    index_ref,
    bar_ref,
    blocks_ref,
    duals_ref,
    demand_ref,
    out_ref,
    total,
):
    rows = blocks_ref.shape[-1]
    step = pl.program_id(0)
    first = step * group

    @pl.when(step == 0)
    def _():
        total[...] = jnp.zeros_like(total)

    for member in range(group):
        right = jnp.concatenate([blocks_ref[member, k] for k in range(touches)], axis=1)
        products = jnp.dot(
            bar_ref[:, member * rows : (member + 1) * rows],
            right,
            preferred_element_type=jnp.float32,
        )
        for k in range(touches):
            place = index_ref[k, first + member]
            total[place] += products[:, k * rows : (k + 1) * rows]

    @pl.when(step == steps - 1)
    def _():
        for block in range(total.shape[0]):
            demand = demand_ref[:, block * rows : (block + 1) * rows]
            out_ref[block] = duals_ref[block] + dual_step * (demand - total[block])


def whole(*shape):
    return pl.BlockSpec(shape, lambda i, *_: (0,) * len(shape))


def params(limit):
    return pltpu.CompilerParams(dimension_semantics=("arbitrary",), vmem_limit_bytes=limit)


def local_adjoint(index, panel, blocks):
    arc_blks, touches, rows, _ = blocks.shape
    scen_rows = panel.shape[1]
    group = GROUP
    return pl.pallas_call(
        functools.partial(local_adjoint_kernel, touches, group),
        out_shape=(
            jax.ShapeDtypeStruct((scen_rows, arc_blks * rows), jnp.float32),
            jax.ShapeDtypeStruct((8, rows), jnp.float32),
        ),
        grid_spec=pltpu.PrefetchScalarGridSpec(
            num_scalar_prefetch=1,
            grid=(arc_blks // group,),
            in_specs=[
                whole(*panel.shape),
                pl.BlockSpec((group, touches, rows, rows), lambda i, *_: (i, 0, 0, 0)),
            ],
            out_specs=(
                pl.BlockSpec((scen_rows, group * rows), lambda i, *_: (0, i)),
                whole(8, rows),
            ),
        ),
        compiler_params=params(SMALL_VMEM),
        cost_estimate=pl.CostEstimate(
            flops=2 * scen_rows * blocks.size, bytes_accessed=2 * blocks.size, transcendentals=0
        ),
        name="local_adjoint",
    )(index, panel, blocks)


def head_step(places, panels, heads, pulled, flows, costs, risk, sums):
    arc_blks, rows, _ = heads.shape
    scen_rows = flows.shape[0]
    peers = len(panels)
    node_blks = panels[0].shape[0]
    group = min(HEAD_GROUP, arc_blks)
    steps = arc_blks // group
    kept = (node_blks, scen_rows, rows)
    sent = [kept] * (peers // 2)
    sent[-1] = (node_blks + 1, scen_rows, rows)
    arcs = pl.BlockSpec((scen_rows, group * rows), lambda i, *_: (0, i))
    results = pl.pallas_call(
        functools.partial(head_kernel, group, steps, peers),
        out_shape=[
            jax.ShapeDtypeStruct(flows.shape, jnp.float32),
            jax.ShapeDtypeStruct(flows.shape, jnp.bfloat16),
            jax.ShapeDtypeStruct(sums[0].shape, jnp.float32),
        ]
        + [jax.ShapeDtypeStruct(kept, jnp.float32)] * (peers // 2)
        + [jax.ShapeDtypeStruct(shape, jnp.bfloat16) for shape in sent],
        grid_spec=pltpu.PrefetchScalarGridSpec(
            num_scalar_prefetch=1,
            grid=(steps,),
            in_specs=[whole(*panels[0].shape)] * peers
            + [
                pl.BlockSpec((group, rows, rows), lambda i, *_: (i, 0, 0)),
                arcs,
                arcs,
                pl.BlockSpec((1, group * rows), lambda i, *_: (0, i)),
                whole(scen_rows, rows),
                whole(*sums[0].shape),
                whole(*sums[0].shape),
            ],
            out_specs=[arcs, arcs, whole(*sums[0].shape)]
            + [whole(*kept)] * (peers // 2)
            + [whole(*shape) for shape in sent],
            scratch_shapes=[
                pltpu.VMEM((peers * node_blks, scen_rows, rows), jnp.bfloat16),
                pltpu.VMEM((peers * node_blks, scen_rows, rows), jnp.float32),
                pltpu.VMEM((scen_rows, group * rows), jnp.float32),
                pltpu.VMEM((scen_rows, rows), jnp.float32),
            ],
        ),
        compiler_params=params((4 + peers + peers // 4) * MIB),
        cost_estimate=pl.CostEstimate(
            flops=4 * scen_rows * heads.size,
            bytes_accessed=2 * heads.size + 14 * flows.size + 4 * peers * panels[0].size,
            transcendentals=0,
        ),
        name="head_step",
    )(places, *panels, heads, pulled, flows, costs, risk, *sums)
    half = peers // 2
    kept = dict(zip(inner(peers), results[3 : 3 + half]))
    sends = dict(zip(leaves(peers), results[3 + half :]))
    return *results[:3], kept, sends


def small_cost(*arrays):
    size = sum(a.size for a in arrays)
    return pl.CostEstimate(flops=size, bytes_accessed=2 * size, transcendentals=0)


def fold(tops, loss, sums, after):
    node_blks, scen_rows, rows = tops[0][0].shape
    with_loss = loss is not None
    operands = [array for kept, arrived in tops for array in (kept, *arrived)]
    operands += ([loss] if with_loss else []) + list(sums)
    vmem = pl.BlockSpec(memory_space=pltpu.VMEM)
    out_shape = [
        jax.ShapeDtypeStruct((node_blks + (with_loss and number == 0), scen_rows, rows), jnp.bfloat16)
        for number in range(len(tops))
    ]
    out_shape += [jax.ShapeDtypeStruct(array.shape, array.dtype) for array in sums[:1]]
    counts = [len(arrived) for _, arrived in tops]
    results = pl.pallas_call(
        functools.partial(fold_kernel, counts, with_loss, len(sums), len(after)),
        out_shape=out_shape,
        in_specs=[vmem] * len(operands) + [pl.BlockSpec(memory_space=pl.ANY)] * len(after),
        out_specs=[vmem] * len(out_shape),
        compiler_params=pltpu.CompilerParams(vmem_limit_bytes=SMALL_VMEM),
        cost_estimate=small_cost(*operands),
        name="fold",
    )(*operands, *after)
    return results[: len(tops)], results[len(tops) :]


def settle(kept, arrived, loss, base, risk, excess, level, sums, arc_total, scen_total, last):
    node_blks, scen_rows, rows = base.shape
    return pl.pallas_call(
        functools.partial(settle_kernel, len(arrived), arc_total, scen_total, last),
        out_shape=(
            jax.ShapeDtypeStruct((scen_rows, node_blks * rows) if last else base.shape, jnp.float32),
            jax.ShapeDtypeStruct(base.shape, jnp.bfloat16),
            jax.ShapeDtypeStruct((1, scen_rows) if last else risk.shape, jnp.float32),
            jax.ShapeDtypeStruct((1, scen_rows) if last else risk.shape, jnp.float32),
            jax.ShapeDtypeStruct((1, 1) if last else level.shape, jnp.float32),
            jax.ShapeDtypeStruct(level.shape, jnp.float32),
        ),
        compiler_params=pltpu.CompilerParams(vmem_limit_bytes=SMALL_VMEM),
        cost_estimate=small_cost(kept, *arrived, base),
        name="settle",
    )(kept, *arrived, loss, base, risk, excess, level, *sums)


def local_forward(index, bar, blocks, duals, demand):
    arc_blks, touches, rows, _ = blocks.shape
    scen_rows = bar.shape[0]
    group = GROUP
    steps = arc_blks // group
    return pl.pallas_call(
        functools.partial(local_forward_kernel, touches, group, steps),
        out_shape=jax.ShapeDtypeStruct(duals.shape, jnp.float32),
        grid_spec=pltpu.PrefetchScalarGridSpec(
            num_scalar_prefetch=1,
            grid=(steps,),
            in_specs=[
                pl.BlockSpec((scen_rows, group * rows), lambda i, *_: (0, i)),
                pl.BlockSpec((group, touches, rows, rows), lambda i, *_: (i, 0, 0, 0)),
                whole(*duals.shape),
                whole(*demand.shape),
            ],
            out_specs=whole(*duals.shape),
            scratch_shapes=[pltpu.VMEM(duals.shape, jnp.float32)],
        ),
        compiler_params=params(SMALL_VMEM),
        cost_estimate=pl.CostEstimate(
            flops=2 * scen_rows * blocks.size, bytes_accessed=2 * blocks.size, transcendentals=0
        ),
        name="local_forward",
    )(index, bar, blocks, duals, demand)


def relay(arrived, risk_sum, after):
    def kernel(arrived_ref, sum_ref, *refs):
        arrived_out, sum_out = refs[-2:]
        arrived_out[...] = arrived_ref[...]
        sum_out[...] = sum_ref[...]

    vmem = pl.BlockSpec(memory_space=pltpu.VMEM)
    return pl.pallas_call(
        kernel,
        out_shape=(
            jax.ShapeDtypeStruct(arrived.shape, arrived.dtype),
            jax.ShapeDtypeStruct(risk_sum.shape, risk_sum.dtype),
        ),
        in_specs=[vmem, vmem] + [pl.BlockSpec(memory_space=pl.ANY)] * len(after),
        out_specs=(vmem, vmem),
        compiler_params=pltpu.CompilerParams(vmem_limit_bytes=SMALL_VMEM),
        cost_estimate=small_cost(arrived),
        name="relay",
    )(arrived, risk_sum, *after)


def prepare_kernel(node_blks, risk_ref, excess_ref, level_ref, head_ref, *refs):
    risk_out, excess_out, level_out, sum_out, places_out = refs[-5:]
    head = head_ref[...]
    owner = lax.div(head, node_blks)
    distance = jnp.bitwise_xor(owner, lax.axis_index("net"))
    places_out[...] = head + (distance - owner) * node_blks
    scen_rows = risk_out.shape[0]
    square = (scen_rows, scen_rows)
    same = lax.broadcasted_iota(jnp.int32, square, 0) == lax.broadcasted_iota(jnp.int32, square, 1)
    for row_ref, out in ((risk_ref, risk_out), (excess_ref, excess_out)):
        column = jnp.sum(jnp.where(same, row_ref[...], 0.0), axis=1, keepdims=True)
        out[...] = jnp.broadcast_to(column, out.shape)
    level_out[...] = jnp.broadcast_to(level_ref[...], level_out.shape)
    sum_out[...] = add_rows(risk_out[...], sum_out.shape)


def prepare(risk, excess, level, heads, rows, node_blks, after):
    wide, flat = (risk.shape[0], rows), (8, rows)
    return pl.pallas_call(
        functools.partial(prepare_kernel, node_blks),
        out_shape=[jax.ShapeDtypeStruct(shape, jnp.float32) for shape in (wide, wide, flat, flat)]
        + [jax.ShapeDtypeStruct((1, heads.shape[0]), jnp.int32)],
        in_specs=[pl.BlockSpec(memory_space=pltpu.VMEM)] * 4
        + [pl.BlockSpec(memory_space=pl.ANY)] * len(after),
        compiler_params=pltpu.CompilerParams(vmem_limit_bytes=SMALL_VMEM),
        cost_estimate=small_cost(risk),
        name="prepare",
    )(risk.reshape(1, -1), excess.reshape(1, -1), level.reshape(1, 1), heads.reshape(1, -1), *after)


def swap(value, axis, distance):
    size = lax.axis_size(axis)
    return lax.ppermute(value, axis, [(i, i ^ distance) for i in range(size)])


def gather_panels(own, risk_sum, after):
    peers = lax.axis_size("net")
    panels = [own] + [None] * (peers - 1)
    order = sorted(range(1, peers), key=lambda k: (k.bit_count(), -k))
    for distance in order:
        hop = last_hop(distance)
        panels[distance] = swap(panels[distance ^ hop], "net", hop)
        if distance == 1:
            far = peers // 2
            panels[far], risk_sum = relay(panels[far], risk_sum, after)
    return panels, risk_sum


def per_device(
    arc_flows,
    node_duals,
    demand,
    excess,
    risk_duals,
    threshold,
    arc_costs,
    local_blocks,
    head_blocks,
    local_index,
    head_index,
):
    rows = local_blocks.shape[-1]
    scen_rows = arc_flows.shape[0]
    node_blks = node_duals.shape[1] // rows
    net_size = lax.axis_size("net")
    arc_total = arc_flows.shape[1] * net_size
    scen_total = scen_rows * lax.axis_size("scen")
    costs = arc_costs.reshape(1, -1)
    touched = local_index.T
    scen_size = lax.axis_size("scen")
    duals = node_duals.reshape(scen_rows, node_blks, rows).transpose(1, 0, 2)
    half = duals.astype(jnp.bfloat16)
    flows = arc_flows
    strides = [1 << bit for bit in range(1, scen_size.bit_length() - 1)][::-1]
    for iteration in range(ROUNDS):
        first, last = iteration == 0, iteration == ROUNDS - 1
        pulled, token = local_adjoint(touched, half, local_blocks)
        panels, risk_sum = gather_panels(half, token if first else risk_sum, (token,))
        if first:
            risk, excess_now, level, risk_sum, places = prepare(
                risk_duals,
                excess,
                threshold,
                head_index,
                rows,
                node_blks,
                (panels[net_size // 2], head_blocks, arc_flows),
            )
            places = places.reshape(-1)
        sums = (risk_sum, swap(risk_sum, "scen", 1))
        flows, bar, risk_sum, kept, sends = head_step(
            places, panels, head_blocks, pulled, flows, costs, risk, sums
        )
        base = local_forward(touched, bar, local_blocks, duals, demand)
        tops = sorted(inner(net_size), key=lambda k: (-k.bit_count(), -k))[:-1]
        groups = [(top,) for top in tops if top != 1] + [(1,)]
        loss, loss_top = sends[net_size - 1], net_size - 1
        after = (base,)
        for group in groups:
            terms = []
            for top in group:
                below = sorted(children(top, net_size))
                terms.append(
                    (
                        kept[top],
                        [swap(sends[k], "net", last_hop(k)) for k in below],
                    )
                )
            chain = loss_top ^ last_hop(loss_top) == group[0]
            sums = (risk_sum,) if group[0] == tops[0] else ()
            if group == (1,):
                after = (loss,)
            if group[0] == net_size // 2:
                after = risk_sums[1:]
            folded, passed = fold(terms, loss if chain else None, sums, after)
            sends.update(zip(group, folded))
            after = ()
            if chain:
                loss_top, loss = group[0], folded[0]
            if sums:
                (risk_sum,) = passed
                for stride in strides[:-1]:
                    risk_sum = risk_sum + swap(risk_sum, "scen", stride)
                risk_sums = (risk_sum, swap(risk_sum, "scen", strides[-1]))
        below = sorted(children(0, net_size))
        arrived = [swap(sends[k], "net", last_hop(k)) for k in below]
        duals, half, risk, excess_now, level, risk_sum = settle(
            kept[0],
            arrived,
            loss,
            base,
            risk,
            excess_now,
            level,
            risk_sums,
            arc_total,
            scen_total,
            last,
        )
    return (flows, duals, excess_now.reshape(-1), risk.reshape(-1), level.reshape(-1))


def solution(mesh):
    placed = (
        P("scen", "net"),
        P("scen", "net"),
        P("scen", "net"),
        P("scen"),
        P("scen"),
        P(),
        P("net"),
        P("net", None, None, None),
        P("net", None, None),
        P("net", None),
        P("net"),
    )
    return jax.shard_map(
        per_device,
        mesh=mesh,
        in_specs=placed,
        out_specs=(P("scen", "net"), P("scen", "net"), P("scen"), P("scen"), P()),
        check_vma=False,
    )
```

```python
import functools

import jax
import jax.numpy as jnp
from jax import lax
from jax.experimental import pallas as pl
from jax.experimental.pallas import tpu as pltpu
from jax.sharding import PartitionSpec as P

ROUNDS = 3

primal_step = 0.5
dual_step = 0.5
risk_step = 1.0
tail_weight = 2.0

MIB = 1024 * 1024
GROUP = 16
HEAD_GROUP = 64
SMALL_VMEM = 6 * MIB
LOCAL_VMEM = 8 * MIB


def contract_last(left, right):
    return lax.dot_general(
        left, right, (((1,), (1,)), ((), ())), preferred_element_type=jnp.float32
    )


def local_adjoint_kernel(
    touches, group, index_ref, panel_ref, blocks_ref, out_ref, token_ref
):
    token_ref[...] = jnp.zeros_like(token_ref)
    rows = blocks_ref.shape[-1]
    first = pl.program_id(0) * group
    for member in range(group):
        left = jnp.concatenate(
            [panel_ref[index_ref[k, first + member]] for k in range(touches)], axis=1
        )
        right = jnp.concatenate([blocks_ref[member, k] for k in range(touches)], axis=1)
        out_ref[:, member * rows : (member + 1) * rows] = contract_last(left, right)


def to_parts(column, shape):
    high = column.astype(jnp.bfloat16).astype(jnp.float32)
    rest = column - high
    middle = rest.astype(jnp.bfloat16).astype(jnp.float32)
    low = rest - middle
    lane = lax.broadcasted_iota(jnp.int32, shape, 1)
    packed = jnp.where(
        lane == 0, high, jnp.where(lane == 1, middle, jnp.where(lane == 2, low, 0.0))
    )
    return packed.astype(jnp.bfloat16)


def from_parts(parts):
    return jnp.sum(parts.astype(jnp.float32), axis=1, keepdims=True)


def head_kernel(group, steps, peers, index_ref, *refs):
    panels, refs = refs[:peers], refs[peers:]
    heads_ref, pulled_ref, flows_ref, costs_ref, risk_ref, sum_ref, other_ref = refs[:7]
    flows_out, bar_out, sum_out, refs = *refs[7:10], refs[10:]
    kept, refs = refs[: peers // 2], refs[peers // 2 :]
    sends, (panel, terms, pulled, loss) = refs[:-4], refs[-4:]
    rows = heads_ref.shape[-1]
    node_blks = panels[0].shape[0]
    step = pl.program_id(0)
    first = step * group

    @pl.when(step == 0)
    def _():
        terms[...] = jnp.zeros_like(terms)
        loss[...] = jnp.zeros_like(loss)
        sum_out[...] = sum_ref[...] + other_ref[...]
        for peer in range(peers):
            panel[peer * node_blks : (peer + 1) * node_blks] = panels[peer][...]

    places = [index_ref[first + member] for member in range(group)]
    spans = [slice(member * rows, (member + 1) * rows) for member in range(group)]
    for member in range(group):
        pulled[:, spans[member]] = contract_last(panel[places[member]], heads_ref[member])
    risk = risk_ref[...]
    loss_sum = jnp.zeros_like(risk)
    for columns in spans:
        flows = flows_ref[:, columns]
        cost = costs_ref[:, columns]
        gradient = risk * cost - (pulled[:, columns] + pulled_ref[:, columns])
        flows_new = jnp.maximum(flows - primal_step * gradient, 0.0)
        bar = 2.0 * flows_new - flows
        flows_out[:, columns] = flows_new
        loss_sum += cost * bar
        bar_out[:, columns] = bar.astype(jnp.bfloat16)
    loss[...] += loss_sum
    products = [
        jnp.dot(bar_out[:, spans[m]], heads_ref[m], preferred_element_type=jnp.float32)
        for m in range(group)
    ]
    for member in range(group):
        terms[places[member]] += products[member]

    @pl.when(step == steps - 1)
    def _():
        loss_parts = to_parts(jnp.sum(loss[...], axis=1, keepdims=True), loss.shape)
        for out, distance in zip(kept, inner(peers)):
            out[...] = terms[distance * node_blks : (distance + 1) * node_blks]
        for out, distance in zip(sends, leaves(peers)):
            out[:node_blks] = terms[distance * node_blks : (distance + 1) * node_blks].astype(
                jnp.bfloat16
            )
        sends[-1][node_blks] = loss_parts


def last_hop(distance):
    return 2 if distance == 3 else distance & -distance


def first_hop(distance):
    return distance & -distance


def children(distance, peers):
    return [k for k in range(1, peers) if k ^ first_hop(k) == distance]


def inner(peers):
    return [k for k in range(peers) if children(k, peers)]


def leaves(peers):
    return [k for k in range(peers) if not children(k, peers)]


def pair_sum(values):
    while len(values) > 1:
        values = [a + b for a, b in zip(values[::2], values[1::2])] + values[len(values) // 2 * 2 :]
    return values[0]


def fold_kernel(counts, with_loss, sums, after, *refs):
    inputs, refs = refs[: sum(counts) + len(counts)], refs[sum(counts) + len(counts) :]
    if with_loss:
        loss_ref, refs = refs[0], refs[1:]
    sum_in, refs = refs[:sums], refs[sums + after :]
    outs, sum_out = refs[: len(counts)], refs[len(counts) :]
    node_blks = inputs[0].shape[0]
    for number, (count, out_ref) in enumerate(zip(counts, outs)):
        kept_ref, arrived, inputs = inputs[0], inputs[1 : 1 + count], inputs[1 + count :]
        for block in range(node_blks):
            total = pair_sum([ref[block].astype(jnp.float32) for ref in arrived])
            out_ref[block] = (kept_ref[block] + total).astype(jnp.bfloat16)
        if with_loss and number == 0:
            both = from_parts(loss_ref[loss_ref.shape[0] - 1]) + from_parts(arrived[-1][node_blks])
            out_ref[node_blks] = to_parts(both, loss_ref.shape[1:])
    for out in sum_out:
        out[...] = functools.reduce(jnp.add, [ref[...] for ref in sum_in])


def next_level(level, risk_total, scen_total):
    level_new = level - primal_step * (1.0 - risk_total / scen_total)
    return level_new, 2.0 * level_new - level


def add_rows(values, shape):
    return jnp.broadcast_to(jnp.sum(values, axis=0, keepdims=True), shape)


def as_row(values):
    rows = values.shape[0]
    picked = lax.broadcasted_iota(jnp.int32, values.shape, 0) == lax.broadcasted_iota(
        jnp.int32, values.shape, 1
    )
    return jnp.sum(jnp.where(picked, values, 0.0), axis=0, keepdims=True)[:, :rows]


def settle_kernel(count, arc_total, scen_total, last, *refs):
    kept_ref, arrived, refs = refs[0], refs[1 : 1 + count], refs[1 + count :]
    loss_ref, base_ref, risk_ref, excess_ref, level_ref, sum_ref, other_ref = refs[:7]
    duals_out, half_out, risk_out, excess_out, level_out, sum_out = refs[7:]
    node_blks, _, rows = base_ref.shape
    for block in range(node_blks):
        total = kept_ref[block] + pair_sum([ref[block].astype(jnp.float32) for ref in arrived])
        duals = base_ref[block] - dual_step * total
        if last:
            duals_out[:, block * rows : (block + 1) * rows] = duals
        else:
            duals_out[block] = duals
            half_out[block] = duals.astype(jnp.bfloat16)
    losses = from_parts(loss_ref[node_blks]) + from_parts(arrived[-1][node_blks])
    losses = losses / arc_total
    risk = risk_ref[...]
    excess = excess_ref[...]
    excess_new = jnp.maximum(excess - primal_step * (tail_weight - risk), 0.0)
    excess_bar = 2.0 * excess_new - excess
    risk_new = risk + risk_step * (losses - excess_bar)
    risk_total = sum_ref[...] + other_ref[...]
    level_new, level_bar = next_level(level_ref[...], risk_total, scen_total)
    risk_new = jnp.maximum(risk_new - risk_step * level_bar[:1], 0.0)
    if last:
        risk_out[...] = as_row(risk_new)
        excess_out[...] = as_row(excess_new)
        level_out[...] = level_new[:1, :1]
    else:
        risk_out[...] = risk_new
        excess_out[...] = excess_new
        level_out[...] = level_new
        sum_out[...] = add_rows(risk_new, sum_out.shape)


def local_forward_kernel(
    touches,
    group,
    steps,
    index_ref,
    bar_ref,
    blocks_ref,
    duals_ref,
    demand_ref,
    out_ref,
    total,
):
    rows = blocks_ref.shape[-1]
    step = pl.program_id(0)
    first = step * group

    @pl.when(step == 0)
    def _():
        total[...] = jnp.zeros_like(total)

    for member in range(group):
        right = jnp.concatenate([blocks_ref[member, k] for k in range(touches)], axis=1)
        products = jnp.dot(
            bar_ref[:, member * rows : (member + 1) * rows],
            right,
            preferred_element_type=jnp.float32,
        )
        for k in range(touches):
            place = index_ref[k, first + member]
            total[place] += products[:, k * rows : (k + 1) * rows]

    @pl.when(step == steps - 1)
    def _():
        for block in range(total.shape[0]):
            demand = demand_ref[:, block * rows : (block + 1) * rows]
            out_ref[block] = duals_ref[block] + dual_step * (demand - total[block])


def whole(*shape):
    return pl.BlockSpec(shape, lambda i, *_: (0,) * len(shape))


def params(limit):
    return pltpu.CompilerParams(dimension_semantics=("arbitrary",), vmem_limit_bytes=limit)


def local_adjoint(index, panel, blocks):
    arc_blks, touches, rows, _ = blocks.shape
    scen_rows = panel.shape[1]
    group = GROUP
    return pl.pallas_call(
        functools.partial(local_adjoint_kernel, touches, group),
        out_shape=(
            jax.ShapeDtypeStruct((scen_rows, arc_blks * rows), jnp.float32),
            jax.ShapeDtypeStruct((8, rows), jnp.float32),
        ),
        grid_spec=pltpu.PrefetchScalarGridSpec(
            num_scalar_prefetch=1,
            grid=(arc_blks // group,),
            in_specs=[
                whole(*panel.shape),
                pl.BlockSpec((group, touches, rows, rows), lambda i, *_: (i, 0, 0, 0)),
            ],
            out_specs=(
                pl.BlockSpec((scen_rows, group * rows), lambda i, *_: (0, i)),
                whole(8, rows),
            ),
        ),
        compiler_params=params(LOCAL_VMEM),
        cost_estimate=pl.CostEstimate(
            flops=2 * scen_rows * blocks.size, bytes_accessed=2 * blocks.size, transcendentals=0
        ),
        name="local_adjoint",
    )(index, panel, blocks)


def head_step(places, panels, heads, pulled, flows, costs, risk, sums):
    arc_blks, rows, _ = heads.shape
    scen_rows = flows.shape[0]
    peers = len(panels)
    node_blks = panels[0].shape[0]
    group = min(HEAD_GROUP, arc_blks)
    steps = arc_blks // group
    kept = (node_blks, scen_rows, rows)
    sent = [kept] * (peers // 2)
    sent[-1] = (node_blks + 1, scen_rows, rows)
    arcs = pl.BlockSpec((scen_rows, group * rows), lambda i, *_: (0, i))
    results = pl.pallas_call(
        functools.partial(head_kernel, group, steps, peers),
        out_shape=[
            jax.ShapeDtypeStruct(flows.shape, jnp.float32),
            jax.ShapeDtypeStruct(flows.shape, jnp.bfloat16),
            jax.ShapeDtypeStruct(sums[0].shape, jnp.float32),
        ]
        + [jax.ShapeDtypeStruct(kept, jnp.float32)] * (peers // 2)
        + [jax.ShapeDtypeStruct(shape, jnp.bfloat16) for shape in sent],
        grid_spec=pltpu.PrefetchScalarGridSpec(
            num_scalar_prefetch=1,
            grid=(steps,),
            in_specs=[whole(*panels[0].shape)] * peers
            + [
                pl.BlockSpec((group, rows, rows), lambda i, *_: (i, 0, 0)),
                arcs,
                arcs,
                pl.BlockSpec((1, group * rows), lambda i, *_: (0, i)),
                whole(scen_rows, rows),
                whole(*sums[0].shape),
                whole(*sums[0].shape),
            ],
            out_specs=[arcs, arcs, whole(*sums[0].shape)]
            + [whole(*kept)] * (peers // 2)
            + [whole(*shape) for shape in sent],
            scratch_shapes=[
                pltpu.VMEM((peers * node_blks, scen_rows, rows), jnp.bfloat16),
                pltpu.VMEM((peers * node_blks, scen_rows, rows), jnp.float32),
                pltpu.VMEM((scen_rows, group * rows), jnp.float32),
                pltpu.VMEM((scen_rows, rows), jnp.float32),
            ],
        ),
        compiler_params=params((4 + peers + peers // 4) * MIB),
        cost_estimate=pl.CostEstimate(
            flops=4 * scen_rows * heads.size,
            bytes_accessed=2 * heads.size + 14 * flows.size + 4 * peers * panels[0].size,
            transcendentals=0,
        ),
        name="head_step",
    )(places, *panels, heads, pulled, flows, costs, risk, *sums)
    half = peers // 2
    kept = dict(zip(inner(peers), results[3 : 3 + half]))
    sends = dict(zip(leaves(peers), results[3 + half :]))
    return *results[:3], kept, sends


def small_cost(*arrays):
    size = sum(a.size for a in arrays)
    return pl.CostEstimate(flops=size, bytes_accessed=2 * size, transcendentals=0)


def fold(tops, loss, sums, after):
    node_blks, scen_rows, rows = tops[0][0].shape
    with_loss = loss is not None
    operands = [array for kept, arrived in tops for array in (kept, *arrived)]
    operands += ([loss] if with_loss else []) + list(sums)
    vmem = pl.BlockSpec(memory_space=pltpu.VMEM)
    out_shape = [
        jax.ShapeDtypeStruct((node_blks + (with_loss and number == 0), scen_rows, rows), jnp.bfloat16)
        for number in range(len(tops))
    ]
    out_shape += [jax.ShapeDtypeStruct(array.shape, array.dtype) for array in sums[:1]]
    counts = [len(arrived) for _, arrived in tops]
    results = pl.pallas_call(
        functools.partial(fold_kernel, counts, with_loss, len(sums), len(after)),
        out_shape=out_shape,
        in_specs=[vmem] * len(operands) + [pl.BlockSpec(memory_space=pl.ANY)] * len(after),
        out_specs=[vmem] * len(out_shape),
        compiler_params=pltpu.CompilerParams(vmem_limit_bytes=SMALL_VMEM),
        cost_estimate=small_cost(*operands),
        name="fold",
    )(*operands, *after)
    return results[: len(tops)], results[len(tops) :]


def settle(kept, arrived, loss, base, risk, excess, level, sums, arc_total, scen_total, last):
    node_blks, scen_rows, rows = base.shape
    return pl.pallas_call(
        functools.partial(settle_kernel, len(arrived), arc_total, scen_total, last),
        out_shape=(
            jax.ShapeDtypeStruct((scen_rows, node_blks * rows) if last else base.shape, jnp.float32),
            jax.ShapeDtypeStruct(base.shape, jnp.bfloat16),
            jax.ShapeDtypeStruct((1, scen_rows) if last else risk.shape, jnp.float32),
            jax.ShapeDtypeStruct((1, scen_rows) if last else risk.shape, jnp.float32),
            jax.ShapeDtypeStruct((1, 1) if last else level.shape, jnp.float32),
            jax.ShapeDtypeStruct(level.shape, jnp.float32),
        ),
        compiler_params=pltpu.CompilerParams(vmem_limit_bytes=SMALL_VMEM),
        cost_estimate=small_cost(kept, *arrived, base),
        name="settle",
    )(kept, *arrived, loss, base, risk, excess, level, *sums)


def local_forward(index, bar, blocks, duals, demand):
    arc_blks, touches, rows, _ = blocks.shape
    scen_rows = bar.shape[0]
    group = GROUP
    steps = arc_blks // group
    return pl.pallas_call(
        functools.partial(local_forward_kernel, touches, group, steps),
        out_shape=jax.ShapeDtypeStruct(duals.shape, jnp.float32),
        grid_spec=pltpu.PrefetchScalarGridSpec(
            num_scalar_prefetch=1,
            grid=(steps,),
            in_specs=[
                pl.BlockSpec((scen_rows, group * rows), lambda i, *_: (0, i)),
                pl.BlockSpec((group, touches, rows, rows), lambda i, *_: (i, 0, 0, 0)),
                whole(*duals.shape),
                whole(*demand.shape),
            ],
            out_specs=whole(*duals.shape),
            scratch_shapes=[pltpu.VMEM(duals.shape, jnp.float32)],
        ),
        compiler_params=params(LOCAL_VMEM),
        cost_estimate=pl.CostEstimate(
            flops=2 * scen_rows * blocks.size, bytes_accessed=2 * blocks.size, transcendentals=0
        ),
        name="local_forward",
    )(index, bar, blocks, duals, demand)


def relay(arrived, risk_sum, after):
    def kernel(arrived_ref, sum_ref, *refs):
        arrived_out, sum_out = refs[-2:]
        arrived_out[...] = arrived_ref[...]
        sum_out[...] = sum_ref[...]

    vmem = pl.BlockSpec(memory_space=pltpu.VMEM)
    return pl.pallas_call(
        kernel,
        out_shape=(
            jax.ShapeDtypeStruct(arrived.shape, arrived.dtype),
            jax.ShapeDtypeStruct(risk_sum.shape, risk_sum.dtype),
        ),
        in_specs=[vmem, vmem] + [pl.BlockSpec(memory_space=pl.ANY)] * len(after),
        out_specs=(vmem, vmem),
        compiler_params=pltpu.CompilerParams(vmem_limit_bytes=SMALL_VMEM),
        cost_estimate=small_cost(arrived),
        name="relay",
    )(arrived, risk_sum, *after)


def prepare_kernel(node_blks, risk_ref, excess_ref, level_ref, head_ref, *refs):
    risk_out, excess_out, level_out, sum_out, places_out = refs[-5:]
    head = head_ref[...]
    owner = lax.div(head, node_blks)
    distance = jnp.bitwise_xor(owner, lax.axis_index("net"))
    places_out[...] = head + (distance - owner) * node_blks
    scen_rows = risk_out.shape[0]
    square = (scen_rows, scen_rows)
    same = lax.broadcasted_iota(jnp.int32, square, 0) == lax.broadcasted_iota(jnp.int32, square, 1)
    for row_ref, out in ((risk_ref, risk_out), (excess_ref, excess_out)):
        column = jnp.sum(jnp.where(same, row_ref[...], 0.0), axis=1, keepdims=True)
        out[...] = jnp.broadcast_to(column, out.shape)
    level_out[...] = jnp.broadcast_to(level_ref[...], level_out.shape)
    sum_out[...] = add_rows(risk_out[...], sum_out.shape)


def prepare(risk, excess, level, heads, rows, node_blks, after):
    wide, flat = (risk.shape[0], rows), (8, rows)
    return pl.pallas_call(
        functools.partial(prepare_kernel, node_blks),
        out_shape=[jax.ShapeDtypeStruct(shape, jnp.float32) for shape in (wide, wide, flat, flat)]
        + [jax.ShapeDtypeStruct((1, heads.shape[0]), jnp.int32)],
        in_specs=[pl.BlockSpec(memory_space=pltpu.VMEM)] * 4
        + [pl.BlockSpec(memory_space=pl.ANY)] * len(after),
        compiler_params=pltpu.CompilerParams(vmem_limit_bytes=SMALL_VMEM),
        cost_estimate=small_cost(risk),
        name="prepare",
    )(risk.reshape(1, -1), excess.reshape(1, -1), level.reshape(1, 1), heads.reshape(1, -1), *after)


def swap(value, axis, distance):
    size = lax.axis_size(axis)
    return lax.ppermute(value, axis, [(i, i ^ distance) for i in range(size)])


def gather_panels(own, risk_sum, after):
    peers = lax.axis_size("net")
    panels = [own] + [None] * (peers - 1)
    order = sorted(range(1, peers), key=lambda k: (k.bit_count(), -k))
    for distance in order:
        hop = last_hop(distance)
        panels[distance] = swap(panels[distance ^ hop], "net", hop)
        if distance == 1:
            far = peers // 2
            panels[far], risk_sum = relay(panels[far], risk_sum, after)
    return panels, risk_sum


def per_device(
    arc_flows,
    node_duals,
    demand,
    excess,
    risk_duals,
    threshold,
    arc_costs,
    local_blocks,
    head_blocks,
    local_index,
    head_index,
):
    rows = local_blocks.shape[-1]
    scen_rows = arc_flows.shape[0]
    node_blks = node_duals.shape[1] // rows
    net_size = lax.axis_size("net")
    arc_total = arc_flows.shape[1] * net_size
    scen_total = scen_rows * lax.axis_size("scen")
    costs = arc_costs.reshape(1, -1)
    touched = local_index.T
    scen_size = lax.axis_size("scen")
    duals = node_duals.reshape(scen_rows, node_blks, rows).transpose(1, 0, 2)
    half = duals.astype(jnp.bfloat16)
    flows = arc_flows
    strides = [1 << bit for bit in range(1, scen_size.bit_length() - 1)][::-1]
    for iteration in range(ROUNDS):
        first, last = iteration == 0, iteration == ROUNDS - 1
        pulled, token = local_adjoint(touched, half, local_blocks)
        panels, risk_sum = gather_panels(half, token if first else risk_sum, (token,))
        if first:
            risk, excess_now, level, risk_sum, places = prepare(
                risk_duals,
                excess,
                threshold,
                head_index,
                rows,
                node_blks,
                (panels[net_size // 2], head_blocks, arc_flows),
            )
            places = places.reshape(-1)
        sums = (risk_sum, swap(risk_sum, "scen", 1))
        flows, bar, risk_sum, kept, sends = head_step(
            places, panels, head_blocks, pulled, flows, costs, risk, sums
        )
        base = local_forward(touched, bar, local_blocks, duals, demand)
        tops = sorted(inner(net_size), key=lambda k: (-k.bit_count(), -k))[:-1]
        groups = [(top,) for top in tops]
        loss, loss_top = sends[net_size - 1], net_size - 1
        after = (base,)
        for group in groups:
            terms = []
            for top in group:
                below = sorted(children(top, net_size))
                terms.append(
                    (
                        kept[top],
                        [swap(sends[k], "net", first_hop(k)) for k in below],
                    )
                )
            chain = loss_top ^ first_hop(loss_top) == group[0]
            sums = (risk_sum,) if group[0] == tops[0] else ()
            if loss_top == net_size // 2:
                after = (loss,)
            if group[0] == net_size // 2:
                after = risk_sums[1:]
            folded, passed = fold(terms, loss if chain else None, sums, after)
            sends.update(zip(group, folded))
            after = ()
            if chain:
                loss_top, loss = group[0], folded[0]
            if sums:
                (risk_sum,) = passed
                for stride in strides[:-1]:
                    risk_sum = risk_sum + swap(risk_sum, "scen", stride)
                risk_sums = (risk_sum, swap(risk_sum, "scen", strides[-1]))
        below = sorted(children(0, net_size))
        arrived = [swap(sends[k], "net", first_hop(k)) for k in below]
        duals, half, risk, excess_now, level, risk_sum = settle(
            kept[0],
            arrived,
            loss,
            base,
            risk,
            excess_now,
            level,
            risk_sums,
            arc_total,
            scen_total,
            last,
        )
    return (flows, duals, excess_now.reshape(-1), risk.reshape(-1), level.reshape(-1))


def solution(mesh):
    placed = (
        P("scen", "net"),
        P("scen", "net"),
        P("scen", "net"),
        P("scen"),
        P("scen"),
        P(),
        P("net"),
        P("net", None, None, None),
        P("net", None, None),
        P("net", None),
        P("net"),
    )
    return jax.shard_map(
        per_device,
        mesh=mesh,
        in_specs=placed,
        out_specs=(P("scen", "net"), P("scen", "net"), P("scen"), P("scen"), P()),
        check_vma=False,
    )
```

```python
import functools

import jax
import jax.numpy as jnp
from jax import lax
from jax.experimental import pallas as pl
from jax.experimental.pallas import tpu as pltpu
from jax.sharding import PartitionSpec as P

ROUNDS = 3

primal_step = 0.5
dual_step = 0.5
risk_step = 1.0
tail_weight = 2.0

MIB = 1024 * 1024
GROUP = 32
HEAD_GROUP = 64
SMALL_VMEM = 6 * MIB
LOCAL_VMEM = 14 * MIB


def contract_last(left, right):
    return lax.dot_general(
        left, right, (((1,), (1,)), ((), ())), preferred_element_type=jnp.float32
    )


def local_adjoint_kernel(
    touches, group, index_ref, panel_ref, blocks_ref, out_ref, token_ref
):
    token_ref[...] = jnp.zeros_like(token_ref)
    rows = blocks_ref.shape[-1]
    first = pl.program_id(0) * group
    for member in range(group):
        left = jnp.concatenate(
            [panel_ref[index_ref[k, first + member]] for k in range(touches)], axis=1
        )
        right = jnp.concatenate([blocks_ref[member, k] for k in range(touches)], axis=1)
        out_ref[:, member * rows : (member + 1) * rows] = contract_last(left, right)


def to_parts(column, shape):
    high = column.astype(jnp.bfloat16).astype(jnp.float32)
    rest = column - high
    middle = rest.astype(jnp.bfloat16).astype(jnp.float32)
    low = rest - middle
    lane = lax.broadcasted_iota(jnp.int32, shape, 1)
    packed = jnp.where(
        lane == 0, high, jnp.where(lane == 1, middle, jnp.where(lane == 2, low, 0.0))
    )
    return packed.astype(jnp.bfloat16)


def from_parts(parts):
    return jnp.sum(parts.astype(jnp.float32), axis=1, keepdims=True)


def head_kernel(group, steps, peers, index_ref, *refs):
    panels, refs = refs[:peers], refs[peers:]
    heads_ref, pulled_ref, flows_ref, costs_ref, risk_ref, sum_ref, other_ref = refs[:7]
    flows_out, bar_out, sum_out, refs = *refs[7:10], refs[10:]
    kept, refs = refs[: peers // 2], refs[peers // 2 :]
    sends, (panel, terms, pulled, loss) = refs[:-4], refs[-4:]
    rows = heads_ref.shape[-1]
    node_blks = panels[0].shape[0]
    step = pl.program_id(0)
    first = step * group

    @pl.when(step == 0)
    def _():
        terms[...] = jnp.zeros_like(terms)
        loss[...] = jnp.zeros_like(loss)
        sum_out[...] = sum_ref[...] + other_ref[...]
        for peer in range(peers):
            panel[peer * node_blks : (peer + 1) * node_blks] = panels[peer][...]

    places = [index_ref[first + member] for member in range(group)]
    spans = [slice(member * rows, (member + 1) * rows) for member in range(group)]
    for member in range(group):
        pulled[:, spans[member]] = contract_last(panel[places[member]], heads_ref[member])
    risk = risk_ref[...]
    loss_sum = jnp.zeros_like(risk)
    for columns in spans:
        flows = flows_ref[:, columns]
        cost = costs_ref[:, columns]
        gradient = risk * cost - (pulled[:, columns] + pulled_ref[:, columns])
        flows_new = jnp.maximum(flows - primal_step * gradient, 0.0)
        bar = 2.0 * flows_new - flows
        flows_out[:, columns] = flows_new
        loss_sum += cost * bar
        bar_out[:, columns] = bar.astype(jnp.bfloat16)
    loss[...] += loss_sum
    products = [
        jnp.dot(bar_out[:, spans[m]], heads_ref[m], preferred_element_type=jnp.float32)
        for m in range(group)
    ]
    for member in range(group):
        terms[places[member]] += products[member]

    @pl.when(step == steps - 1)
    def _():
        loss_parts = to_parts(jnp.sum(loss[...], axis=1, keepdims=True), loss.shape)
        for out, distance in zip(kept, inner(peers)):
            out[...] = terms[distance * node_blks : (distance + 1) * node_blks]
        for out, distance in zip(sends, leaves(peers)):
            out[:node_blks] = terms[distance * node_blks : (distance + 1) * node_blks].astype(
                jnp.bfloat16
            )
        sends[-1][node_blks] = loss_parts


def last_hop(distance):
    return 2 if distance == 3 else distance & -distance


def children(distance, peers):
    return [k for k in range(1, peers) if k ^ last_hop(k) == distance]


def inner(peers):
    return [k for k in range(peers) if children(k, peers)]


def leaves(peers):
    return [k for k in range(peers) if not children(k, peers)]


def pair_sum(values):
    while len(values) > 1:
        values = [a + b for a, b in zip(values[::2], values[1::2])] + values[len(values) // 2 * 2 :]
    return values[0]


def fold_kernel(counts, with_loss, sums, after, *refs):
    inputs, refs = refs[: sum(counts) + len(counts)], refs[sum(counts) + len(counts) :]
    if with_loss:
        loss_ref, refs = refs[0], refs[1:]
    sum_in, refs = refs[:sums], refs[sums + after :]
    outs, sum_out = refs[: len(counts)], refs[len(counts) :]
    node_blks = inputs[0].shape[0]
    for number, (count, out_ref) in enumerate(zip(counts, outs)):
        kept_ref, arrived, inputs = inputs[0], inputs[1 : 1 + count], inputs[1 + count :]
        for block in range(node_blks):
            total = pair_sum([ref[block].astype(jnp.float32) for ref in arrived])
            out_ref[block] = (kept_ref[block] + total).astype(jnp.bfloat16)
        if with_loss and number == 0:
            both = from_parts(loss_ref[loss_ref.shape[0] - 1]) + from_parts(arrived[-1][node_blks])
            out_ref[node_blks] = to_parts(both, loss_ref.shape[1:])
    for out in sum_out:
        out[...] = functools.reduce(jnp.add, [ref[...] for ref in sum_in])


def next_level(level, risk_total, scen_total):
    level_new = level - primal_step * (1.0 - risk_total / scen_total)
    return level_new, 2.0 * level_new - level


def add_rows(values, shape):
    return jnp.broadcast_to(jnp.sum(values, axis=0, keepdims=True), shape)


def as_row(values):
    rows = values.shape[0]
    picked = lax.broadcasted_iota(jnp.int32, values.shape, 0) == lax.broadcasted_iota(
        jnp.int32, values.shape, 1
    )
    return jnp.sum(jnp.where(picked, values, 0.0), axis=0, keepdims=True)[:, :rows]


def settle_kernel(count, arc_total, scen_total, last, *refs):
    kept_ref, arrived, refs = refs[0], refs[1 : 1 + count], refs[1 + count :]
    loss_ref, base_ref, risk_ref, excess_ref, level_ref, sum_ref, other_ref = refs[:7]
    duals_out, half_out, risk_out, excess_out, level_out, sum_out = refs[7:]
    node_blks, _, rows = base_ref.shape
    for block in range(node_blks):
        total = kept_ref[block] + pair_sum([ref[block].astype(jnp.float32) for ref in arrived])
        duals = base_ref[block] - dual_step * total
        if last:
            duals_out[:, block * rows : (block + 1) * rows] = duals
        else:
            duals_out[block] = duals
            half_out[block] = duals.astype(jnp.bfloat16)
    losses = from_parts(loss_ref[node_blks]) + from_parts(arrived[-1][node_blks])
    losses = losses / arc_total
    risk = risk_ref[...]
    excess = excess_ref[...]
    excess_new = jnp.maximum(excess - primal_step * (tail_weight - risk), 0.0)
    excess_bar = 2.0 * excess_new - excess
    risk_new = risk + risk_step * (losses - excess_bar)
    risk_total = sum_ref[...] + other_ref[...]
    level_new, level_bar = next_level(level_ref[...], risk_total, scen_total)
    risk_new = jnp.maximum(risk_new - risk_step * level_bar[:1], 0.0)
    if last:
        risk_out[...] = as_row(risk_new)
        excess_out[...] = as_row(excess_new)
        level_out[...] = level_new[:1, :1]
    else:
        risk_out[...] = risk_new
        excess_out[...] = excess_new
        level_out[...] = level_new
        sum_out[...] = add_rows(risk_new, sum_out.shape)


def local_forward_kernel(
    touches,
    group,
    steps,
    index_ref,
    bar_ref,
    blocks_ref,
    duals_ref,
    demand_ref,
    out_ref,
    total,
):
    rows = blocks_ref.shape[-1]
    step = pl.program_id(0)
    first = step * group

    @pl.when(step == 0)
    def _():
        total[...] = jnp.zeros_like(total)

    for member in range(group):
        right = jnp.concatenate([blocks_ref[member, k] for k in range(touches)], axis=1)
        products = jnp.dot(
            bar_ref[:, member * rows : (member + 1) * rows],
            right,
            preferred_element_type=jnp.float32,
        )
        for k in range(touches):
            place = index_ref[k, first + member]
            total[place] += products[:, k * rows : (k + 1) * rows]

    @pl.when(step == steps - 1)
    def _():
        for block in range(total.shape[0]):
            demand = demand_ref[:, block * rows : (block + 1) * rows]
            out_ref[block] = duals_ref[block] + dual_step * (demand - total[block])


def whole(*shape):
    return pl.BlockSpec(shape, lambda i, *_: (0,) * len(shape))


def params(limit):
    return pltpu.CompilerParams(dimension_semantics=("arbitrary",), vmem_limit_bytes=limit)


def local_adjoint(index, panel, blocks):
    arc_blks, touches, rows, _ = blocks.shape
    scen_rows = panel.shape[1]
    group = min(GROUP, arc_blks)
    return pl.pallas_call(
        functools.partial(local_adjoint_kernel, touches, group),
        out_shape=(
            jax.ShapeDtypeStruct((scen_rows, arc_blks * rows), jnp.float32),
            jax.ShapeDtypeStruct((8, rows), jnp.float32),
        ),
        grid_spec=pltpu.PrefetchScalarGridSpec(
            num_scalar_prefetch=1,
            grid=(arc_blks // group,),
            in_specs=[
                whole(*panel.shape),
                pl.BlockSpec((group, touches, rows, rows), lambda i, *_: (i, 0, 0, 0)),
            ],
            out_specs=(
                pl.BlockSpec((scen_rows, group * rows), lambda i, *_: (0, i)),
                whole(8, rows),
            ),
        ),
        compiler_params=params(LOCAL_VMEM),
        cost_estimate=pl.CostEstimate(
            flops=2 * scen_rows * blocks.size, bytes_accessed=2 * blocks.size, transcendentals=0
        ),
        name="local_adjoint",
    )(index, panel, blocks)


def head_step(places, panels, heads, pulled, flows, costs, risk, sums):
    arc_blks, rows, _ = heads.shape
    scen_rows = flows.shape[0]
    peers = len(panels)
    node_blks = panels[0].shape[0]
    group = min(HEAD_GROUP, arc_blks)
    steps = arc_blks // group
    kept = (node_blks, scen_rows, rows)
    sent = [kept] * (peers // 2)
    sent[-1] = (node_blks + 1, scen_rows, rows)
    arcs = pl.BlockSpec((scen_rows, group * rows), lambda i, *_: (0, i))
    results = pl.pallas_call(
        functools.partial(head_kernel, group, steps, peers),
        out_shape=[
            jax.ShapeDtypeStruct(flows.shape, jnp.float32),
            jax.ShapeDtypeStruct(flows.shape, jnp.bfloat16),
            jax.ShapeDtypeStruct(sums[0].shape, jnp.float32),
        ]
        + [jax.ShapeDtypeStruct(kept, jnp.float32)] * (peers // 2)
        + [jax.ShapeDtypeStruct(shape, jnp.bfloat16) for shape in sent],
        grid_spec=pltpu.PrefetchScalarGridSpec(
            num_scalar_prefetch=1,
            grid=(steps,),
            in_specs=[whole(*panels[0].shape)] * peers
            + [
                pl.BlockSpec((group, rows, rows), lambda i, *_: (i, 0, 0)),
                arcs,
                arcs,
                pl.BlockSpec((1, group * rows), lambda i, *_: (0, i)),
                whole(scen_rows, rows),
                whole(*sums[0].shape),
                whole(*sums[0].shape),
            ],
            out_specs=[arcs, arcs, whole(*sums[0].shape)]
            + [whole(*kept)] * (peers // 2)
            + [whole(*shape) for shape in sent],
            scratch_shapes=[
                pltpu.VMEM((peers * node_blks, scen_rows, rows), jnp.bfloat16),
                pltpu.VMEM((peers * node_blks, scen_rows, rows), jnp.float32),
                pltpu.VMEM((scen_rows, group * rows), jnp.float32),
                pltpu.VMEM((scen_rows, rows), jnp.float32),
            ],
        ),
        compiler_params=params((4 + peers + peers // 4) * MIB),
        cost_estimate=pl.CostEstimate(
            flops=4 * scen_rows * heads.size,
            bytes_accessed=2 * heads.size + 14 * flows.size + 4 * peers * panels[0].size,
            transcendentals=0,
        ),
        name="head_step",
    )(places, *panels, heads, pulled, flows, costs, risk, *sums)
    half = peers // 2
    kept = dict(zip(inner(peers), results[3 : 3 + half]))
    sends = dict(zip(leaves(peers), results[3 + half :]))
    return *results[:3], kept, sends


def small_cost(*arrays):
    size = sum(a.size for a in arrays)
    return pl.CostEstimate(flops=size, bytes_accessed=2 * size, transcendentals=0)


def fold(tops, loss, sums, after):
    node_blks, scen_rows, rows = tops[0][0].shape
    with_loss = loss is not None
    operands = [array for kept, arrived in tops for array in (kept, *arrived)]
    operands += ([loss] if with_loss else []) + list(sums)
    vmem = pl.BlockSpec(memory_space=pltpu.VMEM)
    out_shape = [
        jax.ShapeDtypeStruct((node_blks + (with_loss and number == 0), scen_rows, rows), jnp.bfloat16)
        for number in range(len(tops))
    ]
    out_shape += [jax.ShapeDtypeStruct(array.shape, array.dtype) for array in sums[:1]]
    counts = [len(arrived) for _, arrived in tops]
    results = pl.pallas_call(
        functools.partial(fold_kernel, counts, with_loss, len(sums), len(after)),
        out_shape=out_shape,
        in_specs=[vmem] * len(operands) + [pl.BlockSpec(memory_space=pl.ANY)] * len(after),
        out_specs=[vmem] * len(out_shape),
        compiler_params=pltpu.CompilerParams(vmem_limit_bytes=SMALL_VMEM),
        cost_estimate=small_cost(*operands),
        name="fold",
    )(*operands, *after)
    return results[: len(tops)], results[len(tops) :]


def settle(kept, arrived, loss, base, risk, excess, level, sums, arc_total, scen_total, last):
    node_blks, scen_rows, rows = base.shape
    return pl.pallas_call(
        functools.partial(settle_kernel, len(arrived), arc_total, scen_total, last),
        out_shape=(
            jax.ShapeDtypeStruct((scen_rows, node_blks * rows) if last else base.shape, jnp.float32),
            jax.ShapeDtypeStruct(base.shape, jnp.bfloat16),
            jax.ShapeDtypeStruct((1, scen_rows) if last else risk.shape, jnp.float32),
            jax.ShapeDtypeStruct((1, scen_rows) if last else risk.shape, jnp.float32),
            jax.ShapeDtypeStruct((1, 1) if last else level.shape, jnp.float32),
            jax.ShapeDtypeStruct(level.shape, jnp.float32),
        ),
        compiler_params=pltpu.CompilerParams(vmem_limit_bytes=SMALL_VMEM),
        cost_estimate=small_cost(kept, *arrived, base),
        name="settle",
    )(kept, *arrived, loss, base, risk, excess, level, *sums)


def local_forward(index, bar, blocks, duals, demand):
    arc_blks, touches, rows, _ = blocks.shape
    scen_rows = bar.shape[0]
    group = min(GROUP, arc_blks)
    steps = arc_blks // group
    return pl.pallas_call(
        functools.partial(local_forward_kernel, touches, group, steps),
        out_shape=jax.ShapeDtypeStruct(duals.shape, jnp.float32),
        grid_spec=pltpu.PrefetchScalarGridSpec(
            num_scalar_prefetch=1,
            grid=(steps,),
            in_specs=[
                pl.BlockSpec((scen_rows, group * rows), lambda i, *_: (0, i)),
                pl.BlockSpec((group, touches, rows, rows), lambda i, *_: (i, 0, 0, 0)),
                whole(*duals.shape),
                whole(*demand.shape),
            ],
            out_specs=whole(*duals.shape),
            scratch_shapes=[pltpu.VMEM(duals.shape, jnp.float32)],
        ),
        compiler_params=params(LOCAL_VMEM),
        cost_estimate=pl.CostEstimate(
            flops=2 * scen_rows * blocks.size, bytes_accessed=2 * blocks.size, transcendentals=0
        ),
        name="local_forward",
    )(index, bar, blocks, duals, demand)


def relay(arrived, risk_sum, after):
    def kernel(arrived_ref, sum_ref, *refs):
        arrived_out, sum_out = refs[-2:]
        arrived_out[...] = arrived_ref[...]
        sum_out[...] = sum_ref[...]

    vmem = pl.BlockSpec(memory_space=pltpu.VMEM)
    return pl.pallas_call(
        kernel,
        out_shape=(
            jax.ShapeDtypeStruct(arrived.shape, arrived.dtype),
            jax.ShapeDtypeStruct(risk_sum.shape, risk_sum.dtype),
        ),
        in_specs=[vmem, vmem] + [pl.BlockSpec(memory_space=pl.ANY)] * len(after),
        out_specs=(vmem, vmem),
        compiler_params=pltpu.CompilerParams(vmem_limit_bytes=SMALL_VMEM),
        cost_estimate=small_cost(arrived),
        name="relay",
    )(arrived, risk_sum, *after)


def prepare_kernel(node_blks, risk_ref, excess_ref, level_ref, head_ref, *refs):
    risk_out, excess_out, level_out, sum_out, places_out = refs[-5:]
    head = head_ref[...]
    owner = lax.div(head, node_blks)
    distance = jnp.bitwise_xor(owner, lax.axis_index("net"))
    places_out[...] = head + (distance - owner) * node_blks
    scen_rows = risk_out.shape[0]
    square = (scen_rows, scen_rows)
    same = lax.broadcasted_iota(jnp.int32, square, 0) == lax.broadcasted_iota(jnp.int32, square, 1)
    for row_ref, out in ((risk_ref, risk_out), (excess_ref, excess_out)):
        column = jnp.sum(jnp.where(same, row_ref[...], 0.0), axis=1, keepdims=True)
        out[...] = jnp.broadcast_to(column, out.shape)
    level_out[...] = jnp.broadcast_to(level_ref[...], level_out.shape)
    sum_out[...] = add_rows(risk_out[...], sum_out.shape)


def prepare(risk, excess, level, heads, rows, node_blks, after):
    wide, flat = (risk.shape[0], rows), (8, rows)
    return pl.pallas_call(
        functools.partial(prepare_kernel, node_blks),
        out_shape=[jax.ShapeDtypeStruct(shape, jnp.float32) for shape in (wide, wide, flat, flat)]
        + [jax.ShapeDtypeStruct((1, heads.shape[0]), jnp.int32)],
        in_specs=[pl.BlockSpec(memory_space=pltpu.VMEM)] * 4
        + [pl.BlockSpec(memory_space=pl.ANY)] * len(after),
        compiler_params=pltpu.CompilerParams(vmem_limit_bytes=SMALL_VMEM),
        cost_estimate=small_cost(risk),
        name="prepare",
    )(risk.reshape(1, -1), excess.reshape(1, -1), level.reshape(1, 1), heads.reshape(1, -1), *after)


def swap(value, axis, distance):
    size = lax.axis_size(axis)
    return lax.ppermute(value, axis, [(i, i ^ distance) for i in range(size)])


def gather_panels(own, risk_sum, after):
    peers = lax.axis_size("net")
    panels = [own] + [None] * (peers - 1)
    order = sorted(range(1, peers), key=lambda k: (k.bit_count(), -k))
    for distance in order:
        hop = last_hop(distance)
        panels[distance] = swap(panels[distance ^ hop], "net", hop)
        if distance == 1:
            far = peers // 2
            panels[far], risk_sum = relay(panels[far], risk_sum, after)
    return panels, risk_sum


def per_device(
    arc_flows,
    node_duals,
    demand,
    excess,
    risk_duals,
    threshold,
    arc_costs,
    local_blocks,
    head_blocks,
    local_index,
    head_index,
):
    rows = local_blocks.shape[-1]
    scen_rows = arc_flows.shape[0]
    node_blks = node_duals.shape[1] // rows
    net_size = lax.axis_size("net")
    arc_total = arc_flows.shape[1] * net_size
    scen_total = scen_rows * lax.axis_size("scen")
    costs = arc_costs.reshape(1, -1)
    touched = local_index.T
    scen_size = lax.axis_size("scen")
    duals = node_duals.reshape(scen_rows, node_blks, rows).transpose(1, 0, 2)
    half = duals.astype(jnp.bfloat16)
    flows = arc_flows
    strides = [1 << bit for bit in range(1, scen_size.bit_length() - 1)][::-1]
    for iteration in range(ROUNDS):
        first, last = iteration == 0, iteration == ROUNDS - 1
        pulled, token = local_adjoint(touched, half, local_blocks)
        panels, risk_sum = gather_panels(half, token if first else risk_sum, (token,))
        if first:
            risk, excess_now, level, risk_sum, places = prepare(
                risk_duals,
                excess,
                threshold,
                head_index,
                rows,
                node_blks,
                (panels[net_size // 2], head_blocks, arc_flows),
            )
            places = places.reshape(-1)
        sums = (risk_sum, swap(risk_sum, "scen", 1))
        flows, bar, risk_sum, kept, sends = head_step(
            places, panels, head_blocks, pulled, flows, costs, risk, sums
        )
        base = local_forward(touched, bar, local_blocks, duals, demand)
        tops = sorted(inner(net_size), key=lambda k: (-k.bit_count(), -k))[:-1]
        groups = [(top,) for top in tops if top != 1] + [(1,)]
        loss, loss_top = sends[net_size - 1], net_size - 1
        after = (base,)
        for group in groups:
            terms = []
            for top in group:
                below = sorted(children(top, net_size))
                terms.append(
                    (
                        kept[top],
                        [swap(sends[k], "net", last_hop(k)) for k in below],
                    )
                )
            chain = loss_top ^ last_hop(loss_top) == group[0]
            sums = (risk_sum,) if group[0] == tops[0] else ()
            if group == (1,):
                after = (loss,)
            if group[0] == net_size // 2:
                after = risk_sums[1:]
            folded, passed = fold(terms, loss if chain else None, sums, after)
            sends.update(zip(group, folded))
            after = ()
            if chain:
                loss_top, loss = group[0], folded[0]
            if sums:
                (risk_sum,) = passed
                for stride in strides[:-1]:
                    risk_sum = risk_sum + swap(risk_sum, "scen", stride)
                risk_sums = (risk_sum, swap(risk_sum, "scen", strides[-1]))
        below = sorted(children(0, net_size))
        arrived = [swap(sends[k], "net", last_hop(k)) for k in below]
        duals, half, risk, excess_now, level, risk_sum = settle(
            kept[0],
            arrived,
            loss,
            base,
            risk,
            excess_now,
            level,
            risk_sums,
            arc_total,
            scen_total,
            last,
        )
    return (flows, duals, excess_now.reshape(-1), risk.reshape(-1), level.reshape(-1))


def solution(mesh):
    placed = (
        P("scen", "net"),
        P("scen", "net"),
        P("scen", "net"),
        P("scen"),
        P("scen"),
        P(),
        P("net"),
        P("net", None, None, None),
        P("net", None, None),
        P("net", None),
        P("net"),
    )
    return jax.shard_map(
        per_device,
        mesh=mesh,
        in_specs=placed,
        out_specs=(P("scen", "net"), P("scen", "net"), P("scen"), P("scen"), P()),
        check_vma=False,
    )
```
